256 devices in a mesh: row: 16 (over y, x), col: 16 (over z, core).
Axes of the slice: x: 4, y: 4, z: 8, core: 2. Of those that a mesh axis runs over, the one named last changes fastest.
Arguments:
- image: bfloat16 [1024, 1024, 256], P('row', 'col'), may hold values from -6 to 6
- vert_rate: float32 [8, 256], replicated, may hold values from 0.00029296875 to 0.065625
- vert_coef: float32 [8, 256], replicated, may hold values from -28.8 to 28.8
- horiz_rate: float32 [8, 256], replicated, may hold values from 0.00029296875 to 0.065625
- horiz_coef: float32 [8, 256], replicated, may hold values from -28.8 to 28.8
- w_in: bfloat16 [256, 1024], replicated, may hold values from -0.375 to 0.375
- w_out: bfloat16 [1024, 256], replicated, may hold values from -0.1875 to 0.1875
Outputs:
- mixed: bfloat16 [1024, 1024, 256], P('row', 'col')
The draws below stay inside these ranges and needn't reach their ends.
All inputs are finite; a program needn't handle non-finite values.
Results may differ from the reference program's by a relative error of at most 0.006.
Values sent between devices are 32-bit elements; how exact they have to be, the bound alone decides.
No kernel may reach another device: no remote copies, remote signals or barrier semaphores. Data moves between devices by JAX's collectives and lax.ppermute only.
A program may use at most 128 MiB of HBM per device.

```python
import math
import jax
import jax.numpy as jnp
from jax import lax

C = 256
FFN = 1024
MODES = 8
ROWS_DEV = 64
COLS_DEV = 64
NH = 1024
NW = 1024


def modal_law(key, length, total, salt):
    key = jax.random.fold_in(key, salt)
    keys = jax.random.split(key, 7)
    half = MODES // 2
    slow_lo, slow_hi, base_lo, base_hi, amp_lo, slow_scale = (0.3, 2.0, 0.25, 0.6, 0.3, 0.15)
    slow_rate = jnp.exp(jax.random.uniform(keys[0], (half, C), jnp.float32, math.log(slow_lo), math.log(slow_hi))) / total
    base = jnp.exp(jax.random.uniform(keys[1], (C,), jnp.float32, math.log(base_lo), math.log(base_hi)))
    ratio = jax.random.uniform(keys[2], (half - 1, C), jnp.float32, 1.5, 1.9)
    levels = [base]
    for index in range(half - 1):
        levels.append(levels[-1] * ratio[index])
    mid_rate = jnp.stack(levels, axis=0) / length
    weights = jnp.array([1.0, -3.0, 3.0, -1.0], jnp.float32)
    signs = jnp.where(jax.random.bernoulli(keys[3], 0.5, (C,)), 1.0, -1.0)
    amp = jax.random.uniform(keys[4], (C,), jnp.float32, amp_lo, 0.6) * signs
    mid_gain = jnp.sqrt(1.0 - jnp.exp(-2.0 * mid_rate))
    mid_coef = amp[None, :] * weights[:, None] / mid_gain
    slow_coef = jnp.clip(jax.random.normal(keys[5], (half, C), jnp.float32) * slow_scale, -3.0 * slow_scale, 3.0 * slow_scale)
    rates = jnp.concatenate([slow_rate, mid_rate], axis=0)
    coefs = jnp.concatenate([slow_coef, mid_coef], axis=0)
    order = jax.vmap(lambda single: jax.random.permutation(single, MODES))(jax.random.split(keys[6], C))
    rates = jnp.take_along_axis(rates, order.T, axis=0)
    coefs = jnp.take_along_axis(coefs, order.T, axis=0)
    return (rates.astype(jnp.float32), coefs.astype(jnp.float32))


def draw_vert_rate(key, part):
    return modal_law(key, ROWS_DEV, NH, 11)[0]


def draw_vert_coef(key, part):
    return modal_law(key, ROWS_DEV, NH, 11)[1]


def draw_horiz_rate(key, part):
    return modal_law(key, COLS_DEV, NW, 23)[0]


def draw_horiz_coef(key, part):
    return modal_law(key, COLS_DEV, NW, 23)[1]


def block_scale(rng, extent, cuts, least, largest):
    factor_of = 1.0
    for dim, shards_of in cuts:
        draws = jax.random.uniform(jax.random.fold_in(jax.random.fold_in(rng, 6), dim), (shards_of,), jnp.float32, least / len(cuts), largest / len(cuts))
        factor_of = factor_of * jnp.repeat(jnp.exp(draws), extent[dim] // shards_of).reshape((-1,) + (1,) * (len(extent) - 1 - dim))
    return factor_of


def scatter_about(rng, extent, scale, limit, cuts=(), dtype=jnp.bfloat16):
    drawn = jax.random.normal(rng, extent, jnp.float32) * scale
    if len(cuts) > 0:
        drawn = block_scale(rng, extent, cuts, -0.22, 0.18) * drawn
    return jnp.clip(drawn, min=-limit, max=limit).astype(dtype)


def setup_inputs(seed: int = 0) -> dict:
    splits = jax.random.split(jax.random.key(seed), 8)
    image = scatter_about(splits[0], (NH, NW, C), 1.0, 6.0, ((0, 16), (1, 16)))
    vert_rate = draw_vert_rate(jax.random.fold_in(splits[7], 71), 0)
    vert_coef = draw_vert_coef(jax.random.fold_in(splits[7], 71), 0)
    horiz_rate = draw_horiz_rate(jax.random.fold_in(splits[7], 71), 0)
    horiz_coef = draw_horiz_coef(jax.random.fold_in(splits[7], 71), 0)
    w_in = scatter_about(splits[5], (C, FFN), C ** -0.5, 0.375)
    w_out = scatter_about(splits[6], (FFN, C), FFN ** -0.5, 0.1875)
    return {"image": image, "vert_rate": vert_rate, "vert_coef": vert_coef, "horiz_rate": horiz_rate, "horiz_coef": horiz_coef, "w_in": w_in, "w_out": w_out}


def modal_scan(field, rate, coef):
    pole = jnp.exp(-rate)
    gain = jnp.sqrt(1.0 - pole * pole)
    state0 = jnp.zeros((rate.shape[0], field.shape[1], field.shape[2]), jnp.float32)

    def advance(state, line):
        state = pole[:, None, :] * state + gain[:, None, :] * line[None, :, :]
        return (state, lax.optimization_barrier(jnp.sum(coef[:, None, :] * state, axis=0)))
    _, result = lax.scan(advance, state0, field)
    return result

def reference(image, vert_rate, vert_coef, horiz_rate, horiz_coef, w_in, w_out):
    vert = modal_scan(image.astype(jnp.float32), vert_rate, vert_coef)
    act = jax.nn.gelu(vert).astype(jnp.bfloat16)
    horiz = jnp.transpose(modal_scan(jnp.transpose(act.astype(jnp.float32), (1, 0, 2)), horiz_rate, horiz_coef), (1, 0, 2))

    def one_row(line):
        normed = (line * lax.rsqrt(lax.optimization_barrier(jnp.mean(line * line, axis=-1, keepdims=True)) + 1e-06)).astype(jnp.bfloat16)
        hidden = jax.nn.gelu(jnp.dot(normed, w_in, preferred_element_type=jnp.float32)).astype(jnp.bfloat16)
        return (line + jnp.dot(hidden, w_out, preferred_element_type=jnp.float32)).astype(jnp.bfloat16)
    return lax.map(one_row, horiz)
```

```python
import math

import jax
import jax.numpy as jnp
from jax import lax
from jax.experimental import pallas as pl
from jax.experimental.pallas import tpu as pltpu
from jax.sharding import PartitionSpec as P

F32 = jnp.float32
BF16 = jnp.bfloat16
LANES = 128
MODES = 8
SQRT_2_PI = math.sqrt(2.0 / math.pi)


def gelu(x):
    inner = x * (SQRT_2_PI + (SQRT_2_PI * 0.044715) * (x * x))
    half = 0.5 * x
    return half + half * jnp.tanh(inner)


def poles(rate_ref, half, rows):
    lanes = slice(half * LANES, (half + 1) * LANES)
    return [
        jnp.broadcast_to(jnp.exp(-rate_ref[m : m + 1, lanes]), (rows, LANES)) for m in range(MODES)
    ]


def weights(rate_ref, coef_ref, half, rows):
    lanes = slice(half * LANES, (half + 1) * LANES)
    return [
        jnp.broadcast_to(
            coef_ref[m : m + 1, lanes] * jnp.sqrt(1.0 - jnp.exp(-2.0 * rate_ref[m : m + 1, lanes])),
            (rows, LANES),
        )
        for m in range(MODES)
    ]


def tree(terms):
    while len(terms) > 1:
        terms = [a + b for a, b in zip(terms[::2], terms[1::2])]
    return terms[0]


def edge_kernel(image_ref, rate_ref, edge_ref):
    for half in range(2):
        lanes = slice(half * LANES, (half + 1) * LANES)
        pole = poles(rate_ref, half, 16)

        def steps(i, states, lanes=lanes, pole=pole):
            for k in range(8):
                u = image_ref[i * 8 + k, :, lanes].astype(F32)
                states = [p * h + u for p, h in zip(pole, states)]
            return states

        states = lax.fori_loop(0, 8, steps, [jnp.zeros((16, LANES), F32)] * MODES)
        for m in range(MODES):
            edge_ref[half, :, m] = states[m].reshape(2, 8, LANES)


def prefix_kernel(span, edge_ref, rate_ref, out_ref):
    decay = [
        jnp.broadcast_to(jnp.exp(-span * rate_ref[m : m + 1, :]), (8, LANES)) for m in range(MODES)
    ]
    states = [jnp.zeros((8, LANES), F32)] * MODES
    for r in range(edge_ref.shape[0]):
        for m in range(MODES):
            out_ref[r, m] = states[m]
            states[m] = decay[m] * states[m] + edge_ref[r, m]


def act_kernel(image_ref, in_ref, vr_ref, vc_ref, hr_ref, act_ref, edge_ref, state, field):
    @pl.when(pl.program_id(0) == 0)
    def _():
        state[...] = in_ref[...]

    for half in range(2):
        lanes = slice(half * LANES, (half + 1) * LANES)
        pole = poles(vr_ref, half, 16)
        weight = weights(vr_ref, vc_ref, half, 16)

        def block(b, _, half=half, lanes=lanes, pole=pole, weight=weight):
            pair = pl.ds(b * 2, 2)
            cols = pl.ds(pl.multiple_of(b * 16, 16), 16)
            hs = [state[half, pair, m].reshape(16, LANES) for m in range(MODES)]
            for s in range(16):
                u = image_ref[s, cols, lanes].astype(F32)
                hs = [p * h + u for p, h in zip(pole, hs)]
                y = tree([q * h for q, h in zip(weight, hs)])
                a = gelu(y).astype(BF16).astype(F32)
                field[half, pl.ds(pl.multiple_of(s * 64 + b * 16, 16), 16), :] = a
            for m in range(MODES):
                state[half, pair, m] = hs[m].reshape(2, 8, LANES)
            return 0

        lax.fori_loop(0, 4, block, 0)

    for half in range(2):
        lanes = slice(half * LANES, (half + 1) * LANES)
        pole = poles(hr_ref, half, 16)

        def steps(i, states, half=half, lanes=lanes, pole=pole):
            for k in range(8):
                w = i * 8 + k
                u = field[half, pl.ds(w, 16, stride=64), :]
                act_ref[w, :, lanes] = u.astype(BF16)
                states = [p * h + u for p, h in zip(pole, states)]
            return states

        states = lax.fori_loop(0, 8, steps, [jnp.zeros((16, LANES), F32)] * MODES)
        for m in range(MODES):
            edge_ref[half, :, m] = states[m].reshape(2, 8, LANES)


def mix_kernel(core_ref, act_ref, keep_ref, got_ref, hr_ref, hc_ref, w_in_ref, w_out_ref, out_ref, horiz, mixed):
    core = core_ref[0]
    for half in range(2):
        lanes = slice(half * LANES, (half + 1) * LANES)
        pole = poles(hr_ref, half, 16)
        weight = weights(hr_ref, hc_ref, half, 16)
        mine = core == half
        start = [
            jnp.where(mine, keep_ref[:, m], got_ref[:, m]).reshape(16, LANES) for m in range(MODES)
        ]

        def steps(i, states, lanes=lanes, pole=pole, weight=weight):
            for k in range(8):
                w = i * 8 + k
                u = act_ref[w, :, lanes].astype(F32)
                states = [p * h + u for p, h in zip(pole, states)]
                y = tree([q * h for q, h in zip(weight, states)])
                horiz[pl.ds(pl.multiple_of(w * 16, 16), 16), lanes] = y
            return states

        lax.fori_loop(0, 8, steps, start)

    def mlp(i, _):
        y = horiz[pl.ds(pl.multiple_of(i * 256, 256), 256), :]
        scale = lax.rsqrt(jnp.mean(y * y, axis=-1, keepdims=True) + 1e-06)
        normed = (y * scale).astype(BF16)
        hidden = gelu(jnp.dot(normed, w_in_ref[...], preferred_element_type=F32)).astype(BF16)
        out = y + jnp.dot(hidden, w_out_ref[...], preferred_element_type=F32)
        for k in range(16):
            for half in range(2):
                lanes = slice(half * LANES, (half + 1) * LANES)
                mixed[half, pl.ds(i * 16 + k, 16, stride=64), :] = out[k * 16 : (k + 1) * 16, lanes]
        return 0

    lax.fori_loop(0, 4, mlp, 0)
    for half in range(2):
        lanes = slice(half * LANES, (half + 1) * LANES)
        out_ref[:, :, lanes] = mixed[half].astype(BF16).reshape(16, 64, LANES)


def whole(shape):
    return pl.BlockSpec(shape, lambda i: (0,) * len(shape))


def params(mib):
    return pltpu.CompilerParams(vmem_limit_bytes=mib * 1024 * 1024)


def row_edges(image, rate):
    return pl.pallas_call(
        edge_kernel,
        grid=(4,),
        in_specs=[pl.BlockSpec((64, 16, 256), lambda i: (0, i, 0)), whole((8, 256))],
        out_specs=pl.BlockSpec((2, 2, 8, 8, LANES), lambda i: (0, i, 0, 0, 0)),
        out_shape=jax.ShapeDtypeStruct((2, 8, 8, 8, LANES), F32),
        compiler_params=params(16),
        name="row_edges",
    )(image, rate)


def prefix(edges, rate, span):
    def kernel(edge_ref, rate_ref, out_ref):
        prefix_kernel(span, edge_ref, rate_ref, out_ref)

    return pl.pallas_call(
        kernel,
        out_shape=jax.ShapeDtypeStruct(edges.shape, F32),
        compiler_params=params(8),
        name="prefix",
    )(edges, rate)


def act_and_edges(image, incoming, vert_rate, vert_coef, horiz_rate):
    return pl.pallas_call(
        act_kernel,
        grid=(4,),
        in_specs=[
            pl.BlockSpec((16, 64, 256), lambda i: (i, 0, 0)),
            whole((2, 8, 8, 8, LANES)),
            whole((8, 256)),
            whole((8, 256)),
            whole((8, 256)),
        ],
        out_specs=[
            pl.BlockSpec((64, 16, 256), lambda i: (0, i, 0)),
            pl.BlockSpec((2, 2, 8, 8, LANES), lambda i: (0, i, 0, 0, 0)),
        ],
        out_shape=[
            jax.ShapeDtypeStruct((64, 64, 256), BF16),
            jax.ShapeDtypeStruct((2, 8, 8, 8, LANES), F32),
        ],
        scratch_shapes=[
            pltpu.VMEM((2, 8, 8, 8, LANES), F32),
            pltpu.VMEM((2, 1024, LANES), F32),
        ],
        compiler_params=params(16),
        name="act_and_edges",
    )(image, incoming, vert_rate, vert_coef, horiz_rate)


def mix(core, act, keep, got, horiz_rate, horiz_coef, w_in, w_out):
    return pl.pallas_call(
        mix_kernel,
        grid=(4,),
        in_specs=[
            pl.BlockSpec(memory_space=pltpu.SMEM),
            pl.BlockSpec((64, 16, 256), lambda i: (0, i, 0)),
            pl.BlockSpec((2, 8, 8, LANES), lambda i: (i, 0, 0, 0)),
            pl.BlockSpec((2, 8, 8, LANES), lambda i: (i, 0, 0, 0)),
            whole((8, 256)),
            whole((8, 256)),
            whole((256, 1024)),
            whole((1024, 256)),
        ],
        out_specs=pl.BlockSpec((16, 64, 256), lambda i: (i, 0, 0)),
        out_shape=jax.ShapeDtypeStruct((64, 64, 256), BF16),
        scratch_shapes=[pltpu.VMEM((1024, 256), F32), pltpu.VMEM((2, 1024, LANES), F32)],
        compiler_params=params(32),
        name="mix",
    )(core, act, keep, got, horiz_rate, horiz_coef, w_in, w_out)


def swap_cores(block):
    n = lax.axis_size("col")
    return lax.ppermute(block, "col", [(i, i ^ 1) for i in range(n)])


def on_device(image, vert_rate, vert_coef, horiz_rate, horiz_coef, w_in, w_out):
    rows, cols = lax.axis_size("row"), lax.axis_size("col")
    piece = lax.axis_index("row")
    core = lax.axis_index("col") % 2

    edges = row_edges(image, vert_rate).reshape(rows, 8, 8, LANES)
    edges = lax.all_to_all(edges, "row", 0, 0, tiled=True)
    rate_here = lax.dynamic_slice_in_dim(vert_rate, (piece // 8) * LANES, LANES, 1)
    incoming = prefix(edges, rate_here, 64.0)
    incoming = lax.all_to_all(incoming, "row", 0, 0, tiled=True).reshape(2, 8, 8, 8, LANES)

    act, edge = act_and_edges(image, incoming, vert_rate, vert_coef, horiz_rate)

    chips = [[2 * z + c for z in range(cols // 2)] for c in range(2)]
    mine = lax.dynamic_index_in_dim(edge, core, 0, keepdims=False)
    other = swap_cores(lax.dynamic_index_in_dim(edge, 1 - core, 0, keepdims=False))
    rate_here = lax.dynamic_slice_in_dim(horiz_rate, core * LANES, LANES, 1)
    decay = jnp.exp(-64.0 * rate_here)[None, :, None, :]
    first = jnp.where(core == 0, mine, other)
    second = jnp.where(core == 0, other, mine)
    joined = lax.all_to_all(decay * first + second, "col", 0, 0, tiled=True, axis_index_groups=chips)
    chain = prefix(joined, rate_here, 128.0)
    chain = lax.all_to_all(chain, "col", 0, 0, tiled=True, axis_index_groups=chips)
    after = decay * chain + first
    keep = jnp.where(core == 0, chain, after)
    got = swap_cores(jnp.where(core == 0, after, chain))

    return mix(core.reshape(1), act, keep, got, horiz_rate, horiz_coef, w_in, w_out)


def solution(mesh):
    placed = (P("row", "col", None), P(), P(), P(), P(), P(), P())
    return jax.shard_map(
        on_device, mesh=mesh, in_specs=placed, out_specs=P("row", "col", None), check_vma=False
    )
```

```python
import math

import jax
import jax.numpy as jnp
from jax import lax
from jax.experimental import pallas as pl
from jax.experimental.pallas import tpu as pltpu
from jax.sharding import PartitionSpec as P

F32 = jnp.float32
BF16 = jnp.bfloat16
LANES = 128
MODES = 8
SQRT_2_PI = math.sqrt(2.0 / math.pi)
PITCH = 72


def gelu(x):
    inner = x * (SQRT_2_PI + (SQRT_2_PI * 0.044715) * (x * x))
    half = 0.5 * x
    return half + half * jnp.tanh(inner)


def gelu_packed(x):
    x = x.astype(BF16)
    inner = x * (BF16(SQRT_2_PI) + BF16(SQRT_2_PI * 0.044715) * (x * x))
    half = BF16(0.5) * x
    return half + half * jnp.tanh(inner)


def poles(rate_ref, half, rows):
    lanes = slice(half * LANES, (half + 1) * LANES)
    return [
        jnp.broadcast_to(jnp.exp(-rate_ref[m : m + 1, lanes]), (rows, LANES)) for m in range(MODES)
    ]


def weights(rate_ref, coef_ref, half, rows):
    lanes = slice(half * LANES, (half + 1) * LANES)
    return [
        jnp.broadcast_to(
            coef_ref[m : m + 1, lanes] * jnp.sqrt(1.0 - jnp.exp(-2.0 * rate_ref[m : m + 1, lanes])),
            (rows, LANES),
        )
        for m in range(MODES)
    ]


def tree(terms):
    while len(terms) > 1:
        terms = [a + b for a, b in zip(terms[::2], terms[1::2])]
    return terms[0]


def edge_kernel(image_ref, rate_ref, edge_ref):
    for half in range(2):
        lanes = slice(half * LANES, (half + 1) * LANES)
        pole = poles(rate_ref, half, 16)

        def steps(i, states, lanes=lanes, pole=pole):
            for k in range(8):
                u = image_ref[i * 8 + k, :, lanes].astype(F32)
                states = [p * h + u for p, h in zip(pole, states)]
            return states

        states = lax.fori_loop(0, 8, steps, [jnp.zeros((16, LANES), F32)] * MODES)
        for m in range(MODES):
            edge_ref[half, :, m] = states[m].reshape(2, 8, LANES)


def prefix_kernel(span, edge_ref, rate_ref, out_ref):
    decay = [
        jnp.broadcast_to(jnp.exp(-span * rate_ref[m : m + 1, :]), (8, LANES)) for m in range(MODES)
    ]
    states = [jnp.zeros((8, LANES), F32)] * MODES
    for r in range(edge_ref.shape[0]):
        for m in range(MODES):
            out_ref[r, m] = states[m]
            states[m] = decay[m] * states[m] + edge_ref[r, m]


def local_kernel(image_ref, rate_ref, coef_ref, out_ref):
    for half in range(2):
        lanes = slice(half * LANES, (half + 1) * LANES)
        pole = poles(rate_ref, half, 16)
        weight = weights(rate_ref, coef_ref, half, 16)

        def steps(i, states, lanes=lanes, pole=pole, weight=weight):
            for k in range(8):
                s = i * 8 + k
                u = image_ref[s, :, lanes].astype(F32)
                states = [p * h + u for p, h in zip(pole, states)]
                out_ref[s, :, lanes] = tree([q * h for q, h in zip(weight, states)])
            return states

        lax.fori_loop(0, 8, steps, [jnp.zeros((16, LANES), F32)] * MODES)


def act_kernel(local_ref, in_ref, vr_ref, vc_ref, hr_ref, act_ref, edge_ref, tails, field):
    for half in range(2):
        lanes = slice(half * LANES, (half + 1) * LANES)
        pole = poles(vr_ref, half, 16)

        @pl.when(pl.program_id(0) == 0)
        def _(half=half, pole=pole):
            weight = weights(vr_ref, vc_ref, half, 16)
            for m in range(MODES):
                factor = (pole[m] * weight[m])[None, :8]
                tails[half, :, m] = in_ref[half, :, m] * factor

        def block(b, _, half=half, lanes=lanes, pole=pole):
            pair = pl.ds(b * 2, 2)
            cols = pl.ds(pl.multiple_of(b * 16, 16), 16)
            tail = [tails[half, pair, m].reshape(16, LANES) for m in range(MODES)]
            for s in range(16):
                y = local_ref[s, cols, lanes] + tree(tail)
                tail = [p * g for p, g in zip(pole, tail)]
                a = gelu(y).astype(BF16).astype(F32)
                field[half, pl.ds(pl.multiple_of(s * PITCH + b * 16, 8), 16), :] = a
            for m in range(MODES):
                tails[half, pair, m] = tail[m].reshape(2, 8, LANES)
            return 0

        lax.fori_loop(0, 4, block, 0)

    for half in range(2):
        lanes = slice(half * LANES, (half + 1) * LANES)
        pole = poles(hr_ref, half, 16)

        def steps(i, states, half=half, lanes=lanes, pole=pole):
            for k in range(8):
                w = i * 8 + k
                u = field[half, pl.ds(w, 16, stride=PITCH), :]
                act_ref[w, :, lanes] = u.astype(BF16)
                states = [p * h + u for p, h in zip(pole, states)]
            return states

        states = lax.fori_loop(0, 8, steps, [jnp.zeros((16, LANES), F32)] * MODES)
        for m in range(MODES):
            edge_ref[half, :, m] = states[m].reshape(2, 8, LANES)


def mix_kernel(core_ref, local_ref, keep_ref, got_ref, hr_ref, hc_ref, w_in_ref, w_out_ref, out_ref, horiz, mixed):
    core = core_ref[0]
    for half in range(2):
        lanes = slice(half * LANES, (half + 1) * LANES)
        pole = poles(hr_ref, half, 16)
        weight = weights(hr_ref, hc_ref, half, 16)
        mine = core == half
        tail = [
            jnp.where(mine, keep_ref[:, m], got_ref[:, m]).reshape(16, LANES) * (pole[m] * weight[m])
            for m in range(MODES)
        ]

        def steps(i, tail, lanes=lanes, pole=pole):
            for k in range(8):
                w = i * 8 + k
                y = local_ref[w, :, lanes] + tree(tail)
                tail = [p * g for p, g in zip(pole, tail)]
                horiz[pl.ds(pl.multiple_of(w * 16, 16), 16), lanes] = y
            return tail

        lax.fori_loop(0, 8, steps, tail)

    y = horiz[...]
    scale = lax.rsqrt(jnp.mean(y * y, axis=-1, keepdims=True) + 1e-06)
    normed = (y * scale).astype(BF16)
    hidden = gelu_packed(jnp.dot(normed, w_in_ref[...], preferred_element_type=F32))
    out = y + jnp.dot(hidden, w_out_ref[...], preferred_element_type=F32)
    for w in range(64):
        for half in range(2):
            lanes = slice(half * LANES, (half + 1) * LANES)
            mixed[half, pl.ds(w, 16, stride=PITCH), :] = out[w * 16 : (w + 1) * 16, lanes]
    for half in range(2):
        lanes = slice(half * LANES, (half + 1) * LANES)
        for h in range(16):
            out_ref[h, :, lanes] = mixed[half, h * PITCH : h * PITCH + 64].astype(BF16)


LOCAL_COST = pl.CostEstimate(flops=5_000_000_000, bytes_accessed=8_000_000, transcendentals=0)


def whole(shape):
    return pl.BlockSpec(shape, lambda i: (0,) * len(shape))


def params(mib):
    return pltpu.CompilerParams(vmem_limit_bytes=mib * 1024 * 1024)


def row_edges(image, rate):
    return pl.pallas_call(
        edge_kernel,
        grid=(4,),
        in_specs=[pl.BlockSpec((64, 16, 256), lambda i: (0, i, 0)), whole((8, 256))],
        out_specs=pl.BlockSpec((2, 2, 8, 8, LANES), lambda i: (0, i, 0, 0, 0)),
        out_shape=jax.ShapeDtypeStruct((2, 8, 8, 8, LANES), F32),
        compiler_params=params(56),
        name="row_edges",
    )(image, rate)


def prefix(edges, rate, span, after):
    def kernel(edge_ref, rate_ref, after_ref, out_ref):
        prefix_kernel(span, edge_ref, rate_ref, out_ref)

    vmem = pl.BlockSpec(memory_space=pltpu.VMEM)
    return pl.pallas_call(
        kernel,
        in_specs=[vmem, vmem, pl.BlockSpec(memory_space=pltpu.HBM)],
        out_specs=vmem,
        out_shape=jax.ShapeDtypeStruct(edges.shape, F32),
        compiler_params=params(8),
        name="prefix",
    )(edges, rate, after)


def local_scan(block, rate, coef, mib, name):
    return pl.pallas_call(
        local_kernel,
        grid=(4,),
        in_specs=[pl.BlockSpec((64, 16, 256), lambda i: (0, i, 0)), whole((8, 256)), whole((8, 256))],
        out_specs=pl.BlockSpec((64, 16, 256), lambda i: (0, i, 0)),
        out_shape=pltpu.HBM((64, 64, 256), F32),
        compiler_params=params(mib),
        cost_estimate=LOCAL_COST,
        name=name,
    )(block, rate, coef)


def act_and_edges(local, incoming, vert_rate, vert_coef, horiz_rate):
    return pl.pallas_call(
        act_kernel,
        grid=(4,),
        in_specs=[
            pl.BlockSpec((16, 64, 256), lambda i: (i, 0, 0)),
            whole((2, 8, 8, 8, LANES)),
            whole((8, 256)),
            whole((8, 256)),
            whole((8, 256)),
        ],
        out_specs=[
            pl.BlockSpec((64, 16, 256), lambda i: (0, i, 0)),
            pl.BlockSpec((2, 2, 8, 8, LANES), lambda i: (0, i, 0, 0, 0)),
        ],
        out_shape=[
            pltpu.HBM((64, 64, 256), BF16),
            jax.ShapeDtypeStruct((2, 8, 8, 8, LANES), F32),
        ],
        scratch_shapes=[
            pltpu.VMEM((2, 8, 8, 8, LANES), F32),
            pltpu.VMEM((2, 16 * PITCH, LANES), F32),
        ],
        compiler_params=params(24),
        name="act_and_edges",
    )(local, incoming, vert_rate, vert_coef, horiz_rate)


def mix(core, local, keep, got, horiz_rate, horiz_coef, w_in, w_out):
    return pl.pallas_call(
        mix_kernel,
        grid=(4,),
        in_specs=[
            pl.BlockSpec(memory_space=pltpu.SMEM),
            pl.BlockSpec((64, 16, 256), lambda i: (0, i, 0)),
            pl.BlockSpec((2, 8, 8, LANES), lambda i: (i, 0, 0, 0)),
            pl.BlockSpec((2, 8, 8, LANES), lambda i: (i, 0, 0, 0)),
            whole((8, 256)),
            whole((8, 256)),
            whole((256, 1024)),
            whole((1024, 256)),
        ],
        out_specs=pl.BlockSpec((16, 64, 256), lambda i: (i, 0, 0)),
        out_shape=jax.ShapeDtypeStruct((64, 64, 256), BF16),
        scratch_shapes=[pltpu.VMEM((1024, 256), F32), pltpu.VMEM((2, 16 * PITCH, LANES), F32)],
        compiler_params=params(40),
        name="mix",
    )(core, local, keep, got, horiz_rate, horiz_coef, w_in, w_out)


def swap_cores(block):
    n = lax.axis_size("col")
    return lax.ppermute(block, "col", [(i, i ^ 1) for i in range(n)])


def on_device(image, vert_rate, vert_coef, horiz_rate, horiz_coef, w_in, w_out):
    rows, cols = lax.axis_size("row"), lax.axis_size("col")
    piece = lax.axis_index("row")
    core = lax.axis_index("col") % 2

    edges = row_edges(image, vert_rate).reshape(rows, 8, 8, LANES)
    edges = lax.all_to_all(edges, "row", 0, 0, tiled=True)
    rate_here = lax.dynamic_slice_in_dim(vert_rate, (piece // 8) * LANES, LANES, 1)
    local = local_scan(image, vert_rate, vert_coef, 56, "vert_local")
    incoming = prefix(edges, rate_here, 64.0, local)
    incoming = lax.all_to_all(incoming, "row", 0, 0, tiled=True).reshape(2, 8, 8, 8, LANES)

    act, edge = act_and_edges(local, incoming, vert_rate, vert_coef, horiz_rate)

    horiz = local_scan(act, horiz_rate, horiz_coef, 56, "horiz_local")

    chips = [[2 * z + c for z in range(cols // 2)] for c in range(2)]
    mine = lax.dynamic_index_in_dim(edge, core, 0, keepdims=False)
    other = swap_cores(lax.dynamic_index_in_dim(edge, 1 - core, 0, keepdims=False))
    rate_here = lax.dynamic_slice_in_dim(horiz_rate, core * LANES, LANES, 1)
    decay = jnp.exp(-64.0 * rate_here)[None, :, None, :]
    first = jnp.where(core == 0, mine, other)
    second = jnp.where(core == 0, other, mine)
    joined = lax.all_to_all(decay * first + second, "col", 0, 0, tiled=True, axis_index_groups=chips)
    chain = prefix(joined, rate_here, 128.0, horiz)
    chain = lax.all_to_all(chain, "col", 0, 0, tiled=True, axis_index_groups=chips)
    after = decay * chain + first
    keep = jnp.where(core == 0, chain, after)
    got = swap_cores(jnp.where(core == 0, after, chain))

    return mix(core.reshape(1), horiz, keep, got, horiz_rate, horiz_coef, w_in, w_out)


def solution(mesh):
    placed = (P("row", "col", None), P(), P(), P(), P(), P(), P())
    return jax.shard_map(
        on_device, mesh=mesh, in_specs=placed, out_specs=P("row", "col", None), check_vma=False
    )
```

```python
import math

import jax
import jax.numpy as jnp
from jax import lax
from jax.experimental import pallas as pl
from jax.experimental.pallas import tpu as pltpu
from jax.sharding import PartitionSpec as P

F32 = jnp.float32
BF16 = jnp.bfloat16
LANES = 128
MODES = 8
SQRT_2_PI = math.sqrt(2.0 / math.pi)
PITCH = 72


def gelu(x):
    inner = x * (SQRT_2_PI + (SQRT_2_PI * 0.044715) * (x * x))
    half = 0.5 * x
    return half + half * jnp.tanh(inner)


def gelu_packed(x):
    x = x.astype(BF16)
    inner = x * (BF16(SQRT_2_PI) + BF16(SQRT_2_PI * 0.044715) * (x * x))
    half = BF16(0.5) * x
    return half + half * jnp.tanh(inner)


def poles(rate_ref, half, rows):
    lanes = slice(half * LANES, (half + 1) * LANES)
    return [
        jnp.broadcast_to(jnp.exp(-rate_ref[m : m + 1, lanes]), (rows, LANES)) for m in range(MODES)
    ]


def weights(rate_ref, coef_ref, half, rows):
    lanes = slice(half * LANES, (half + 1) * LANES)
    return [
        jnp.broadcast_to(
            coef_ref[m : m + 1, lanes] * jnp.sqrt(1.0 - jnp.exp(-2.0 * rate_ref[m : m + 1, lanes])),
            (rows, LANES),
        )
        for m in range(MODES)
    ]


def tree(terms):
    while len(terms) > 1:
        terms = [a + b for a, b in zip(terms[::2], terms[1::2])]
    return terms[0]


def edge_kernel(image_ref, rate_ref, edge_ref):
    for half in range(2):
        lanes = slice(half * LANES, (half + 1) * LANES)
        pole = poles(rate_ref, half, 16)

        def steps(i, states, lanes=lanes, pole=pole):
            for k in range(8):
                u = image_ref[i * 8 + k, :, lanes].astype(F32)
                states = [p * h + u for p, h in zip(pole, states)]
            return states

        states = lax.fori_loop(0, 8, steps, [jnp.zeros((16, LANES), F32)] * MODES)
        for m in range(MODES):
            edge_ref[half, :, m] = states[m].reshape(2, 8, LANES)


def prefix_kernel(span, edge_ref, rate_ref, out_ref):
    decay = [
        jnp.broadcast_to(jnp.exp(-span * rate_ref[m : m + 1, :]), (8, LANES)) for m in range(MODES)
    ]
    states = [jnp.zeros((8, LANES), F32)] * MODES
    for r in range(edge_ref.shape[0]):
        for m in range(MODES):
            out_ref[r, m] = states[m]
            states[m] = decay[m] * states[m] + edge_ref[r, m]


def local_kernel(image_ref, rate_ref, coef_ref, out_ref):
    for half in range(2):
        lanes = slice(half * LANES, (half + 1) * LANES)
        pole = poles(rate_ref, half, 16)
        weight = weights(rate_ref, coef_ref, half, 16)

        def steps(i, states, lanes=lanes, pole=pole, weight=weight):
            for k in range(8):
                s = i * 8 + k
                u = image_ref[s, :, lanes].astype(F32)
                states = [p * h + u for p, h in zip(pole, states)]
                out_ref[s, :, lanes] = tree([q * h for q, h in zip(weight, states)])
            return states

        lax.fori_loop(0, 8, steps, [jnp.zeros((16, LANES), F32)] * MODES)


def act_kernel(local_ref, in_ref, vr_ref, vc_ref, hr_ref, act_ref, edge_ref, tails, field):
    for half in range(2):
        lanes = slice(half * LANES, (half + 1) * LANES)
        pole = poles(vr_ref, half, 16)

        @pl.when(pl.program_id(0) == 0)
        def _(half=half, pole=pole):
            weight = weights(vr_ref, vc_ref, half, 16)
            for m in range(MODES):
                factor = (pole[m] * weight[m])[None, :8]
                tails[half, :, m] = in_ref[half, :, m] * factor

        def block(b, _, half=half, lanes=lanes, pole=pole):
            pair = pl.ds(b * 2, 2)
            cols = pl.ds(pl.multiple_of(b * 16, 16), 16)
            tail = [tails[half, pair, m].reshape(16, LANES) for m in range(MODES)]
            for s in range(16):
                y = local_ref[s, cols, lanes] + tree(tail)
                tail = [p * g for p, g in zip(pole, tail)]
                a = gelu(y).astype(BF16).astype(F32)
                field[half, pl.ds(pl.multiple_of(s * PITCH + b * 16, 8), 16), :] = a
            for m in range(MODES):
                tails[half, pair, m] = tail[m].reshape(2, 8, LANES)
            return 0

        lax.fori_loop(0, 4, block, 0)

    for half in range(2):
        lanes = slice(half * LANES, (half + 1) * LANES)
        pole = poles(hr_ref, half, 16)

        def steps(i, states, half=half, lanes=lanes, pole=pole):
            for k in range(8):
                w = i * 8 + k
                u = field[half, pl.ds(w, 16, stride=PITCH), :]
                act_ref[w, :, lanes] = u.astype(BF16)
                states = [p * h + u for p, h in zip(pole, states)]
            return states

        states = lax.fori_loop(0, 8, steps, [jnp.zeros((16, LANES), F32)] * MODES)
        for m in range(MODES):
            edge_ref[half, :, m] = states[m].reshape(2, 8, LANES)


def mix_kernel(core_ref, local_ref, keep_ref, got_ref, hr_ref, hc_ref, w_in_ref, w_out_ref, out_ref, horiz, mixed):
    core = core_ref[0]
    for half in range(2):
        lanes = slice(half * LANES, (half + 1) * LANES)
        pole = poles(hr_ref, half, 16)
        weight = weights(hr_ref, hc_ref, half, 16)
        mine = core == half
        tail = [
            jnp.where(mine, keep_ref[:, m], got_ref[:, m]).reshape(16, LANES) * (pole[m] * weight[m])
            for m in range(MODES)
        ]

        def steps(i, tail, lanes=lanes, pole=pole):
            for k in range(8):
                w = i * 8 + k
                y = local_ref[w, :, lanes] + tree(tail)
                tail = [p * g for p, g in zip(pole, tail)]
                horiz[pl.ds(pl.multiple_of(w * 16, 16), 16), lanes] = y
            return tail

        lax.fori_loop(0, 8, steps, tail)

    y = horiz[...]
    scale = lax.rsqrt(jnp.mean(y * y, axis=-1, keepdims=True) + 1e-06)
    normed = (y * scale).astype(BF16)
    hidden = gelu_packed(jnp.dot(normed, w_in_ref[...], preferred_element_type=F32))
    out = y + jnp.dot(hidden, w_out_ref[...], preferred_element_type=F32)
    for w in range(64):
        for half in range(2):
            lanes = slice(half * LANES, (half + 1) * LANES)
            mixed[half, pl.ds(w, 16, stride=PITCH), :] = out[w * 16 : (w + 1) * 16, lanes]
    for half in range(2):
        lanes = slice(half * LANES, (half + 1) * LANES)
        for h in range(16):
            out_ref[h, :, lanes] = mixed[half, h * PITCH : h * PITCH + 64].astype(BF16)


LOCAL_COST = pl.CostEstimate(flops=5_000_000_000, bytes_accessed=8_000_000, transcendentals=0)


def in_hbm(block):
    return pltpu.with_memory_space_constraint(block, pltpu.HBM)


def whole(shape):
    return pl.BlockSpec(shape, lambda i: (0,) * len(shape))


def params(mib):
    return pltpu.CompilerParams(vmem_limit_bytes=mib * 1024 * 1024)


def row_edges(image, rate):
    return pl.pallas_call(
        edge_kernel,
        grid=(4,),
        in_specs=[pl.BlockSpec((64, 16, 256), lambda i: (0, i, 0)), whole((8, 256))],
        out_specs=pl.BlockSpec((2, 2, 8, 8, LANES), lambda i: (0, i, 0, 0, 0)),
        out_shape=jax.ShapeDtypeStruct((2, 8, 8, 8, LANES), F32),
        compiler_params=params(56),
        name="row_edges",
    )(image, rate)


def prefix(edges, rate, span):
    def kernel(edge_ref, rate_ref, out_ref):
        prefix_kernel(span, edge_ref, rate_ref, out_ref)

    return pl.pallas_call(
        kernel,
        out_shape=jax.ShapeDtypeStruct(edges.shape, F32),
        compiler_params=params(8),
        name="prefix",
    )(edges, rate)


def local_scan(block, rate, coef, mib, name):
    return pl.pallas_call(
        local_kernel,
        grid=(4,),
        in_specs=[pl.BlockSpec((64, 16, 256), lambda i: (0, i, 0)), whole((8, 256)), whole((8, 256))],
        out_specs=pl.BlockSpec((64, 16, 256), lambda i: (0, i, 0)),
        out_shape=pltpu.HBM((64, 64, 256), F32),
        compiler_params=params(mib),
        cost_estimate=LOCAL_COST,
        name=name,
    )(block, rate, coef)


def act_and_edges(local, incoming, vert_rate, vert_coef, horiz_rate):
    return pl.pallas_call(
        act_kernel,
        grid=(4,),
        in_specs=[
            pl.BlockSpec((16, 64, 256), lambda i: (i, 0, 0)),
            whole((2, 8, 8, 8, LANES)),
            whole((8, 256)),
            whole((8, 256)),
            whole((8, 256)),
        ],
        out_specs=[
            pl.BlockSpec((64, 16, 256), lambda i: (0, i, 0)),
            pl.BlockSpec((2, 2, 8, 8, LANES), lambda i: (0, i, 0, 0, 0)),
        ],
        out_shape=[
            pltpu.HBM((64, 64, 256), BF16),
            jax.ShapeDtypeStruct((2, 8, 8, 8, LANES), F32),
        ],
        scratch_shapes=[
            pltpu.VMEM((2, 8, 8, 8, LANES), F32),
            pltpu.VMEM((2, 16 * PITCH, LANES), F32),
        ],
        compiler_params=params(24),
        name="act_and_edges",
    )(in_hbm(local), incoming, vert_rate, vert_coef, horiz_rate)


def mix(core, local, keep, got, horiz_rate, horiz_coef, w_in, w_out):
    return pl.pallas_call(
        mix_kernel,
        grid=(4,),
        in_specs=[
            pl.BlockSpec(memory_space=pltpu.SMEM),
            pl.BlockSpec((64, 16, 256), lambda i: (0, i, 0)),
            pl.BlockSpec((2, 8, 8, LANES), lambda i: (i, 0, 0, 0)),
            pl.BlockSpec((2, 8, 8, LANES), lambda i: (i, 0, 0, 0)),
            whole((8, 256)),
            whole((8, 256)),
            whole((256, 1024)),
            whole((1024, 256)),
        ],
        out_specs=pl.BlockSpec((16, 64, 256), lambda i: (i, 0, 0)),
        out_shape=jax.ShapeDtypeStruct((64, 64, 256), BF16),
        scratch_shapes=[pltpu.VMEM((1024, 256), F32), pltpu.VMEM((2, 16 * PITCH, LANES), F32)],
        compiler_params=params(40),
        name="mix",
    )(core, in_hbm(local), keep, got, horiz_rate, horiz_coef, w_in, w_out)


def swap_cores(block):
    n = lax.axis_size("col")
    return lax.ppermute(block, "col", [(i, i ^ 1) for i in range(n)])


def on_device(image, vert_rate, vert_coef, horiz_rate, horiz_coef, w_in, w_out):
    rows, cols = lax.axis_size("row"), lax.axis_size("col")
    piece = lax.axis_index("row")
    core = lax.axis_index("col") % 2

    edges = row_edges(image, vert_rate).reshape(rows, 8, 8, LANES)
    edges = lax.all_to_all(edges, "row", 0, 0, tiled=True)
    rate_here = lax.dynamic_slice_in_dim(vert_rate, (piece // 8) * LANES, LANES, 1)
    local = local_scan(image, vert_rate, vert_coef, 56, "vert_local")
    edges, local = lax.optimization_barrier((edges, local))
    incoming = prefix(edges, rate_here, 64.0)
    incoming = lax.all_to_all(incoming, "row", 0, 0, tiled=True).reshape(2, 8, 8, 8, LANES)

    act, edge = act_and_edges(local, incoming, vert_rate, vert_coef, horiz_rate)

    horiz = local_scan(act, horiz_rate, horiz_coef, 56, "horiz_local")

    chips = [[2 * z + c for z in range(cols // 2)] for c in range(2)]
    mine = lax.dynamic_index_in_dim(edge, core, 0, keepdims=False)
    other = swap_cores(lax.dynamic_index_in_dim(edge, 1 - core, 0, keepdims=False))
    rate_here = lax.dynamic_slice_in_dim(horiz_rate, core * LANES, LANES, 1)
    decay = jnp.exp(-64.0 * rate_here)[None, :, None, :]
    first = jnp.where(core == 0, mine, other)
    second = jnp.where(core == 0, other, mine)
    joined = lax.all_to_all(decay * first + second, "col", 0, 0, tiled=True, axis_index_groups=chips)
    joined, horiz = lax.optimization_barrier((joined, horiz))
    chain = prefix(joined, rate_here, 128.0)
    chain = lax.all_to_all(chain, "col", 0, 0, tiled=True, axis_index_groups=chips)
    after = decay * chain + first
    keep = jnp.where(core == 0, chain, after)
    got = swap_cores(jnp.where(core == 0, after, chain))

    return mix(core.reshape(1), horiz, keep, got, horiz_rate, horiz_coef, w_in, w_out)


def solution(mesh):
    placed = (P("row", "col", None), P(), P(), P(), P(), P(), P())
    return jax.shard_map(
        on_device, mesh=mesh, in_specs=placed, out_specs=P("row", "col", None), check_vma=False
    )
```

```python
import math

import jax
import jax.numpy as jnp
from jax import lax
from jax.experimental import pallas as pl
from jax.experimental.pallas import tpu as pltpu
from jax.sharding import PartitionSpec as P

F32 = jnp.float32
BF16 = jnp.bfloat16
LANES = 128
MODES = 8
SQRT_2_PI = math.sqrt(2.0 / math.pi)
PITCH = 72


def gelu(x):
    inner = x * (SQRT_2_PI + (SQRT_2_PI * 0.044715) * (x * x))
    half = 0.5 * x
    return half + half * jnp.tanh(inner)


def gelu_packed(x):
    x = x.astype(BF16)
    inner = x * (BF16(SQRT_2_PI) + BF16(SQRT_2_PI * 0.044715) * (x * x))
    half = BF16(0.5) * x
    return half + half * jnp.tanh(inner)


def poles(rate_ref, half, rows):
    lanes = slice(half * LANES, (half + 1) * LANES)
    return [
        jnp.broadcast_to(jnp.exp(-rate_ref[m : m + 1, lanes]), (rows, LANES)) for m in range(MODES)
    ]


def weights(rate_ref, coef_ref, half, rows):
    lanes = slice(half * LANES, (half + 1) * LANES)
    return [
        jnp.broadcast_to(
            coef_ref[m : m + 1, lanes] * jnp.sqrt(1.0 - jnp.exp(-2.0 * rate_ref[m : m + 1, lanes])),
            (rows, LANES),
        )
        for m in range(MODES)
    ]


def tree(terms):
    while len(terms) > 1:
        terms = [a + b for a, b in zip(terms[::2], terms[1::2])]
    return terms[0]


def edge_kernel(image_ref, rate_hbm_ref, edge_ref, image, rate_ref, arrived):
    def fetch(i):
        cols = pl.ds(pl.multiple_of(i * 16, 16), 16)
        return pltpu.make_async_copy(image_ref.at[:, cols, :], image.at[:, cols, :], arrived.at[i])

    rates = pltpu.make_async_copy(rate_hbm_ref, rate_ref, arrived.at[4])
    rates.start()
    for i in range(4):
        fetch(i).start()
    rates.wait()

    def chunk(i, _):
        fetch(i).wait()
        cols = pl.ds(pl.multiple_of(i * 16, 16), 16)
        for half in range(2):
            lanes = slice(half * LANES, (half + 1) * LANES)
            pole = poles(rate_ref, half, 16)

            def steps(j, states, lanes=lanes, pole=pole):
                for k in range(16):
                    u = image[j * 16 + k, cols, lanes].astype(F32)
                    states = [p * h + u for p, h in zip(pole, states)]
                return states

            states = lax.fori_loop(0, 4, steps, [jnp.zeros((16, LANES), F32)] * MODES)
            for m in range(MODES):
                edge_ref[half, pl.ds(i * 2, 2), m] = states[m].reshape(2, 8, LANES)
        return 0

    lax.fori_loop(0, 4, chunk, 0)


def prefix_kernel(span, edge_ref, rate_ref, out_ref):
    decay = [
        jnp.broadcast_to(jnp.exp(-span * rate_ref[m : m + 1, :]), (8, LANES)) for m in range(MODES)
    ]
    states = [jnp.zeros((8, LANES), F32)] * MODES
    for r in range(edge_ref.shape[0]):
        for m in range(MODES):
            out_ref[r, m] = states[m]
            states[m] = decay[m] * states[m] + edge_ref[r, m]


def local_kernel(image_ref, rate_ref, coef_ref, out_ref):
    for half in range(2):
        lanes = slice(half * LANES, (half + 1) * LANES)
        pole = poles(rate_ref, half, 16)
        weight = weights(rate_ref, coef_ref, half, 16)

        def steps(i, states, lanes=lanes, pole=pole, weight=weight):
            for k in range(8):
                s = i * 8 + k
                u = image_ref[s, :, lanes].astype(F32)
                states = [p * h + u for p, h in zip(pole, states)]
                out_ref[s, :, lanes] = tree([q * h for q, h in zip(weight, states)])
            return states

        lax.fori_loop(0, 8, steps, [jnp.zeros((16, LANES), F32)] * MODES)


def decays(rate_ref, span):
    return [jnp.broadcast_to(jnp.exp(-span * rate_ref[m : m + 1, :]), (8, LANES)) for m in range(MODES)]


def join_cores_kernel(info_ref, mine_ref, other_ref, rate_ref, first_ref, keep_ref, send_ref):
    even_core, here = info_ref[0] == 0, info_ref[1] * 4
    decay = decays(rate_ref, 64.0)
    for b in range(8):
        for m in range(MODES):
            mine, other = mine_ref[b, m], other_ref[b, m]
            first_ref[b, m] = jnp.where(even_core, mine, other)
    for b in range(4):
        for out_ref, at in ((keep_ref, here + b), (send_ref, 4 - here + b)):
            for m in range(MODES):
                mine, other, first = mine_ref[at, m], other_ref[at, m], first_ref[at, m]
                out_ref[b, m] = decay[m] * first + jnp.where(even_core, other, mine)


def join_chips_kernel(info_ref, keep_ref, came_ref, rate_ref, even_ref, q0_ref, q1_ref, q2_ref, q3_ref):
    even_chip, pair = info_ref[1] == 0, info_ref[2]
    decay = decays(rate_ref, 128.0)
    for d, q_ref in enumerate((q0_ref, q1_ref, q2_ref, q3_ref)):
        b = pair ^ d
        for m in range(MODES):
            keep, came = keep_ref[b, m], came_ref[b, m]
            even = jnp.where(even_chip, keep, came)
            even_ref[b, m] = even
            q_ref[m] = decay[m] * even + jnp.where(even_chip, came, keep)


def prefix_pairs_kernel(info_ref, e0_ref, e1_ref, e2_ref, e3_ref, rate_ref, h0_ref, h1_ref, h2_ref, h3_ref):
    pair = info_ref[2]
    decay = decays(rate_ref, 256.0)
    edges = (e0_ref, e1_ref, e2_ref, e3_ref)
    for m in range(MODES):
        e = [edge[m] for edge in edges]
        state = jnp.zeros((8, LANES), F32)
        states = []
        for p in range(4):
            states.append(state)
            edge = e[3]
            for d in range(3):
                edge = jnp.where((pair ^ d) == p, e[d], edge)
            state = decay[m] * state + edge
        for d, out_ref in enumerate((h0_ref, h1_ref, h2_ref, h3_ref)):
            out = states[3]
            for p in range(3):
                out = jnp.where((pair ^ d) == p, states[p], out)
            out_ref[m] = out


def part_chips_kernel(info_ref, h0_ref, h1_ref, h2_ref, h3_ref, even_ref, rate_ref, keep_ref, send_ref):
    even_chip, pair = info_ref[1] == 0, info_ref[2]
    decay = decays(rate_ref, 128.0)
    for d, h_ref in enumerate((h0_ref, h1_ref, h2_ref, h3_ref)):
        b = pair ^ d
        for m in range(MODES):
            first = h_ref[m]
            second = decay[m] * first + even_ref[b, m]
            keep_ref[b, m] = jnp.where(even_chip, first, second)
            send_ref[b, m] = jnp.where(even_chip, second, first)


def part_cores_kernel(info_ref, own_ref, came_ref, first_ref, rate_ref, keep_ref, send_ref):
    even_core, here = info_ref[0] == 0, info_ref[1] * 4
    decay = decays(rate_ref, 64.0)
    for b in range(4):
        for in_ref, at in ((own_ref, here + b), (came_ref, 4 - here + b)):
            for m in range(MODES):
                chain = in_ref[b, m]
                after = decay[m] * chain + first_ref[at, m]
                keep_ref[at, m] = jnp.where(even_core, chain, after)
                send_ref[at, m] = jnp.where(even_core, after, chain)


def act_kernel(
    info_ref, local_ref, in_ref, vr_ref, vc_ref, hr_ref, act_ref, mine_ref, other_ref,
    local, act, tails, field, arrived, left,
):
    def rows(i):
        return pl.ds(pl.multiple_of(i * 16, 16), 16)

    def fetch(i):
        return pltpu.make_async_copy(local_ref.at[rows(i)], local.at[rows(i)], arrived.at[i])

    def put(i):
        return pltpu.make_async_copy(act.at[:, rows(i), :], act_ref.at[:, rows(i), :], left.at[i])

    fetch(0).start()
    for half in range(2):
        pole = poles(vr_ref, half, 8)
        weight = weights(vr_ref, vc_ref, half, 8)
        for m in range(MODES):
            tails[half, :, m] = in_ref[half, :, m] * (pole[m] * weight[m])[None]

    def chunk(i, _):
        fetch(i).wait()

        @pl.when(i < 3)
        def _():
            fetch(i + 1).start()

        for half in range(2):
            lanes = slice(half * LANES, (half + 1) * LANES)
            pole = poles(vr_ref, half, 16)

            def block(b, _, half=half, lanes=lanes, pole=pole):
                pair = pl.ds(b * 2, 2)
                cols = pl.ds(pl.multiple_of(b * 16, 16), 16)
                tail = [tails[half, pair, m].reshape(16, LANES) for m in range(MODES)]
                for s in range(16):
                    y = local[i * 16 + s, cols, lanes] + tree(tail)
                    tail = [p * g for p, g in zip(pole, tail)]
                    a = gelu(y).astype(BF16).astype(F32)
                    field[half, pl.ds(pl.multiple_of(s * PITCH + b * 16, 8), 16), :] = a
                for m in range(MODES):
                    tails[half, pair, m] = tail[m].reshape(2, 8, LANES)
                return 0

            lax.fori_loop(0, 4, block, 0)

        for half in range(2):
            lanes = slice(half * LANES, (half + 1) * LANES)
            pole = poles(hr_ref, half, 16)

            def steps(j, states, half=half, lanes=lanes, pole=pole):
                for k in range(8):
                    w = j * 8 + k
                    u = field[half, pl.ds(w, 16, stride=PITCH), :]
                    act[w, rows(i), lanes] = u.astype(BF16)
                    states = [p * h + u for p, h in zip(pole, states)]
                return states

            states = lax.fori_loop(0, 8, steps, [jnp.zeros((16, LANES), F32)] * MODES)
            mine = info_ref[0] == half

            @pl.when(mine)
            def _(states=states):
                for m in range(MODES):
                    mine_ref[pl.ds(i * 2, 2), m] = states[m].reshape(2, 8, LANES)

            @pl.when(jnp.logical_not(mine))
            def _(states=states):
                for m in range(MODES):
                    other_ref[pl.ds(i * 2, 2), m] = states[m].reshape(2, 8, LANES)
        put(i).start()
        return 0

    lax.fori_loop(0, 4, chunk, 0)
    for i in range(4):
        put(i).wait()


def mix_kernel(
    info_ref, top_ref, bottom_ref, keep_ref, got_ref, hr_ref, hc_ref, w_in_ref, w_out_ref, out_ref,
    local, result, horiz, mixed, arrived, left,
):
    core = info_ref[0]

    def rows(i):
        return pl.ds(pl.multiple_of(i * 16, 16), 16)

    def fetch(i, part_ref):
        source = part_ref.at[:, rows(i % 2), :]
        return pltpu.make_async_copy(source, local.at[:, rows(i), :], arrived.at[i])

    def put(i):
        return pltpu.make_async_copy(result.at[rows(i)], out_ref.at[rows(i)], left.at[i])

    for i in range(4):
        fetch(i, (top_ref, bottom_ref)[i // 2]).start()

    def chunk(i, _):
        fetch(i, top_ref).wait()
        for half in range(2):
            lanes = slice(half * LANES, (half + 1) * LANES)
            pole = poles(hr_ref, half, 16)
            weight = weights(hr_ref, hc_ref, half, 16)
            mine = core == half
            pair = pl.ds(i * 2, 2)
            tail = [
                jnp.where(mine, keep_ref[pair, m], got_ref[pair, m]).reshape(16, LANES)
                * (pole[m] * weight[m])
                for m in range(MODES)
            ]

            def steps(j, tail, lanes=lanes, pole=pole):
                for k in range(8):
                    w = j * 8 + k
                    y = local[w, rows(i), lanes] + tree(tail)
                    tail = [p * g for p, g in zip(pole, tail)]
                    horiz[pl.ds(pl.multiple_of(w * 16, 16), 16), lanes] = y
                return tail

            lax.fori_loop(0, 8, steps, tail)

        y = horiz[...]
        scale = lax.rsqrt(jnp.mean(y * y, axis=-1, keepdims=True) + 1e-06)
        normed = (y * scale).astype(BF16)
        hidden = gelu_packed(jnp.dot(normed, w_in_ref[...], preferred_element_type=F32))
        out = y + jnp.dot(hidden, w_out_ref[...], preferred_element_type=F32)
        for w in range(64):
            for half in range(2):
                lanes = slice(half * LANES, (half + 1) * LANES)
                mixed[half, pl.ds(w, 16, stride=PITCH), :] = out[w * 16 : (w + 1) * 16, lanes]
        for half in range(2):
            lanes = slice(half * LANES, (half + 1) * LANES)
            for h in range(16):
                result[i * 16 + h, :, lanes] = mixed[half, h * PITCH : h * PITCH + 64].astype(BF16)
        put(i).start()
        return 0

    lax.fori_loop(0, 4, chunk, 0)
    for i in range(4):
        put(i).wait()


LOCAL_COST = {
    1: pl.CostEstimate(flops=5_000_000_000, bytes_accessed=8_000_000, transcendentals=0),
    2: pl.CostEstimate(flops=2_500_000_000, bytes_accessed=4_000_000, transcendentals=0),
}


def in_hbm(block):
    return pltpu.with_memory_space_constraint(block, pltpu.HBM)


def whole(shape):
    return pl.BlockSpec(shape, lambda i: (0,) * len(shape))


def params(mib):
    return pltpu.CompilerParams(vmem_limit_bytes=mib * 1024 * 1024)


VMEM = pl.BlockSpec(memory_space=pltpu.VMEM)
HBM = pl.BlockSpec(memory_space=pltpu.HBM)
SMEM = pl.BlockSpec(memory_space=pltpu.SMEM)


def row_edges(image, rate):
    return pl.pallas_call(
        edge_kernel,
        in_specs=[HBM, HBM],
        out_specs=VMEM,
        out_shape=jax.ShapeDtypeStruct((2, 8, 8, 8, LANES), F32),
        scratch_shapes=[
            pltpu.VMEM((64, 64, 256), BF16),
            pltpu.VMEM((8, 256), F32),
            pltpu.SemaphoreType.DMA((5,)),
        ],
        compiler_params=params(24),
        name="row_edges",
    )(in_hbm(image), in_hbm(rate))


def prefix(edges, rate, span):
    def kernel(edge_ref, rate_ref, out_ref):
        prefix_kernel(span, edge_ref, rate_ref, out_ref)

    return pl.pallas_call(
        kernel,
        out_shape=jax.ShapeDtypeStruct(edges.shape, F32),
        compiler_params=params(8),
        name="prefix",
    )(edges, rate)


def local_scan(block, rate, coef, part, parts, name):
    steps = 4 // parts
    return pl.pallas_call(
        local_kernel,
        grid=(steps,),
        in_specs=[
            pl.BlockSpec((64, 16, 256), lambda i: (0, i + part * steps, 0)),
            whole((8, 256)),
            whole((8, 256)),
        ],
        out_specs=pl.BlockSpec((64, 16, 256), lambda i: (0, i, 0)),
        out_shape=pltpu.HBM((64, 64 // parts, 256), F32),
        compiler_params=params(56),
        cost_estimate=LOCAL_COST[parts],
        name=name,
    )(block, rate, coef)


def small(kernel, name, outs, *operands):
    return pl.pallas_call(
        kernel,
        in_specs=[SMEM] + [VMEM] * (len(operands) - 1),
        out_specs=[VMEM] * len(outs),
        out_shape=[jax.ShapeDtypeStruct(shape, F32) for shape in outs],
        compiler_params=params(8),
        name=name,
    )(*operands)


def act_and_edges(info, local, incoming, vert_rate, vert_coef, horiz_rate):
    return pl.pallas_call(
        act_kernel,
        in_specs=[SMEM, HBM, VMEM, VMEM, VMEM, VMEM],
        out_specs=[HBM, VMEM, VMEM],
        out_shape=[pltpu.HBM((64, 64, 256), BF16)] + [jax.ShapeDtypeStruct((8, 8, 8, LANES), F32)] * 2,
        scratch_shapes=[
            pltpu.VMEM((64, 64, 256), F32),
            pltpu.VMEM((64, 64, 256), BF16),
            pltpu.VMEM((2, 8, 8, 8, LANES), F32),
            pltpu.VMEM((2, 16 * PITCH, LANES), F32),
            pltpu.SemaphoreType.DMA((4,)),
            pltpu.SemaphoreType.DMA((4,)),
        ],
        compiler_params=params(24),
        name="act_and_edges",
    )(info, in_hbm(local), incoming, vert_rate, vert_coef, horiz_rate)


def mix(info, top, bottom, keep, got, horiz_rate, horiz_coef, w_in, w_out):
    return pl.pallas_call(
        mix_kernel,
        in_specs=[SMEM, HBM, HBM, VMEM, VMEM, VMEM, VMEM, VMEM, VMEM],
        out_specs=HBM,
        out_shape=jax.ShapeDtypeStruct((64, 64, 256), BF16),
        scratch_shapes=[
            pltpu.VMEM((64, 64, 256), F32),
            pltpu.VMEM((64, 64, 256), BF16),
            pltpu.VMEM((1024, 256), F32),
            pltpu.VMEM((2, 16 * PITCH, LANES), F32),
            pltpu.SemaphoreType.DMA((4,)),
            pltpu.SemaphoreType.DMA((4,)),
        ],
        compiler_params=params(40),
        name="mix",
    )(info, in_hbm(top), in_hbm(bottom), keep, got, horiz_rate, horiz_coef, w_in, w_out)


def swap(block, bits):
    n = lax.axis_size("col")
    return lax.ppermute(block, "col", [(i, i ^ bits) for i in range(n)])


def on_device(image, vert_rate, vert_coef, horiz_rate, horiz_coef, w_in, w_out):
    rows = lax.axis_size("row")
    piece = lax.axis_index("row")
    col = lax.axis_index("col")
    core = col % 2
    info = jnp.stack([core, col // 2 % 2, col // 4]).astype(jnp.int32)

    edges = row_edges(image, vert_rate).reshape(rows, 8, 8, LANES)
    edges = lax.all_to_all(edges, "row", 0, 0, tiled=True)
    rate_here = lax.dynamic_slice_in_dim(vert_rate, (piece // 8) * LANES, LANES, 1)
    local = local_scan(image, vert_rate, vert_coef, 0, 1, "vert_local")
    edges, local = lax.optimization_barrier((edges, local))
    incoming = prefix(edges, rate_here, 64.0)
    incoming = lax.all_to_all(incoming, "row", 0, 0, tiled=True).reshape(2, 8, 8, 8, LANES)

    act, mine, other = act_and_edges(info, local, incoming, vert_rate, vert_coef, horiz_rate)

    half, quarter, one = (8, 8, 8, LANES), (4, 8, 8, LANES), (8, 8, LANES)
    rate_here = lax.dynamic_slice_in_dim(horiz_rate, core * LANES, LANES, 1)
    came = swap(other, 1)
    first, keep, send = small(
        join_cores_kernel, "join_cores", [half, quarter, quarter], info, mine, came, rate_here
    )
    top = local_scan(act, horiz_rate, horiz_coef, 0, 2, "horiz_top")
    came = swap(send, 2)
    came, top = lax.optimization_barrier((came, top))
    even, *q = small(
        join_chips_kernel, "join_chips", [quarter] + [one] * 4, info, keep, came, rate_here
    )
    e = [q[0]] + [swap(q[d], 4 * d) for d in range(1, 4)]
    h = small(prefix_pairs_kernel, "prefix_pairs", [one] * 4, info, *e, rate_here)
    h = [h[0]] + [swap(h[d], 4 * d) for d in range(1, 4)]
    own, send = small(
        part_chips_kernel, "part_chips", [quarter] * 2, info, *h, even, rate_here
    )
    bottom = local_scan(act, horiz_rate, horiz_coef, 1, 2, "horiz_bottom")
    came = swap(send, 2)
    came, bottom = lax.optimization_barrier((came, bottom))
    keep, send = small(
        part_cores_kernel, "part_cores", [half] * 2, info, own, came, first, rate_here
    )
    got = swap(send, 1)

    return mix(info, top, bottom, keep, got, horiz_rate, horiz_coef, w_in, w_out)


def solution(mesh):
    placed = (P("row", "col", None), P(), P(), P(), P(), P(), P())
    return jax.shard_map(
        on_device, mesh=mesh, in_specs=placed, out_specs=P("row", "col", None), check_vma=False
    )
```

```python
import functools
import math

import jax
import jax.numpy as jnp
from jax import lax
from jax.experimental import pallas as pl
from jax.experimental.pallas import tpu as pltpu
from jax.sharding import PartitionSpec as P

F32 = jnp.float32
BF16 = jnp.bfloat16
LANES = 128
MODES = 8
SQRT_2_PI = math.sqrt(2.0 / math.pi)
PITCH = 72


def gelu(x):
    inner = x * (SQRT_2_PI + (SQRT_2_PI * 0.044715) * (x * x))
    half = 0.5 * x
    return half + half * jnp.tanh(inner)


def gelu_packed(x):
    x = x.astype(BF16)
    inner = x * (BF16(SQRT_2_PI) + BF16(SQRT_2_PI * 0.044715) * (x * x))
    half = BF16(0.5) * x
    return half + half * jnp.tanh(inner)


def poles(rate_ref, half, rows):
    lanes = slice(half * LANES, (half + 1) * LANES)
    return [
        jnp.broadcast_to(jnp.exp(-rate_ref[m : m + 1, lanes]), (rows, LANES)) for m in range(MODES)
    ]


def weights(rate_ref, coef_ref, half, rows):
    lanes = slice(half * LANES, (half + 1) * LANES)
    return [
        jnp.broadcast_to(
            coef_ref[m : m + 1, lanes] * jnp.sqrt(1.0 - jnp.exp(-2.0 * rate_ref[m : m + 1, lanes])),
            (rows, LANES),
        )
        for m in range(MODES)
    ]


def tree(terms):
    while len(terms) > 1:
        terms = [a + b for a, b in zip(terms[::2], terms[1::2])]
    return terms[0]


def edge_kernel(image_ref, rate_hbm_ref, edge_ref, image, rate_ref, arrived):
    def fetch(i):
        cols = pl.ds(pl.multiple_of(i * 16, 16), 16)
        return pltpu.make_async_copy(image_ref.at[:, cols, :], image.at[:, cols, :], arrived.at[i])

    rates = pltpu.make_async_copy(rate_hbm_ref, rate_ref, arrived.at[4])
    rates.start()
    for i in range(4):
        fetch(i).start()
    rates.wait()

    def chunk(i, _):
        fetch(i).wait()
        cols = pl.ds(pl.multiple_of(i * 16, 16), 16)
        for half in range(2):
            lanes = slice(half * LANES, (half + 1) * LANES)
            pole = poles(rate_ref, half, 16)

            def steps(j, states, lanes=lanes, pole=pole):
                for k in range(16):
                    u = image[j * 16 + k, cols, lanes].astype(F32)
                    states = [p * h + u for p, h in zip(pole, states)]
                return states

            states = lax.fori_loop(0, 4, steps, [jnp.zeros((16, LANES), F32)] * MODES)
            for m in range(MODES):
                edge_ref[half, pl.ds(i * 2, 2), m] = states[m].reshape(2, 8, LANES)
        return 0

    lax.fori_loop(0, 4, chunk, 0)


def prefix_kernel(span, edge_ref, rate_ref, out_ref):
    decay = [
        jnp.broadcast_to(jnp.exp(-span * rate_ref[m : m + 1, :]), (8, LANES)) for m in range(MODES)
    ]
    states = [jnp.zeros((8, LANES), F32)] * MODES
    for r in range(edge_ref.shape[0]):
        for m in range(MODES):
            out_ref[r, m] = states[m]
            states[m] = decay[m] * states[m] + edge_ref[r, m]


def local_kernel(image_ref, rate_ref, coef_ref, out_ref):
    for half in range(2):
        lanes = slice(half * LANES, (half + 1) * LANES)
        pole = poles(rate_ref, half, 16)
        weight = weights(rate_ref, coef_ref, half, 16)

        def steps(i, states, lanes=lanes, pole=pole, weight=weight):
            for k in range(8):
                s = i * 8 + k
                u = image_ref[s, :, lanes].astype(F32)
                states = [p * h + u for p, h in zip(pole, states)]
                out_ref[s, :, lanes] = tree([q * h for q, h in zip(weight, states)])
            return states

        lax.fori_loop(0, 8, steps, [jnp.zeros((16, LANES), F32)] * MODES)


def decays(rate_ref, span):
    return [jnp.broadcast_to(jnp.exp(-span * rate_ref[m : m + 1, :]), (8, LANES)) for m in range(MODES)]


def join_kernel(level, span, info_ref, keep_ref, came_ref, rate_ref, first_ref, *out_refs):
    left_here = info_ref[level] == 0
    here = info_ref[4 + level] if len(out_refs) == 2 else 0
    decay = decays(rate_ref, span)
    part = keep_ref.shape[0] // len(out_refs)
    for b in range(part):
        for k, out_ref in enumerate(out_refs):
            at = b if len(out_refs) == 1 else (here * part if k == 0 else part - here * part) + b
            for m in range(MODES):
                keep, came = keep_ref[at, m], came_ref[at, m]
                first = jnp.where(left_here, keep, came)
                first_ref[at, m] = first
                out_ref[b, m] = decay[m] * first + jnp.where(left_here, came, keep)


def part_kernel(level, span, info_ref, *refs):
    *in_refs, first_ref, rate_ref, keep_ref, send_ref = refs
    left_here = info_ref[level] == 0
    here = info_ref[4 + level] if len(in_refs) == 2 else 0
    decay = decays(rate_ref, span)
    part = first_ref.shape[0] // len(in_refs)
    for b in range(part):
        for k, in_ref in enumerate(in_refs):
            at = b if len(in_refs) == 1 else (here * part if k == 0 else part - here * part) + b
            for m in range(MODES):
                chain = in_ref[b, m]
                after = decay[m] * chain + first_ref[at, m]
                keep_ref[at, m] = jnp.where(left_here, chain, after)
                send_ref[at, m] = jnp.where(left_here, after, chain)


def act_kernel(info_ref, local_ref, in_ref, vr_ref, vc_ref, hr_ref, act_ref, mine_ref, other_ref, tails, field):
    for half in range(2):
        lanes = slice(half * LANES, (half + 1) * LANES)
        pole = poles(vr_ref, half, 16)

        @pl.when(pl.program_id(0) == 0)
        def _(half=half, pole=pole):
            weight = weights(vr_ref, vc_ref, half, 16)
            for m in range(MODES):
                factor = (pole[m] * weight[m])[None, :8]
                tails[half, :, m] = in_ref[half, :, m] * factor

        def block(b, _, half=half, lanes=lanes, pole=pole):
            pair = pl.ds(b * 2, 2)
            cols = pl.ds(pl.multiple_of(b * 16, 16), 16)
            tail = [tails[half, pair, m].reshape(16, LANES) for m in range(MODES)]
            for s in range(16):
                y = local_ref[s, cols, lanes] + tree(tail)
                tail = [p * g for p, g in zip(pole, tail)]
                a = gelu(y).astype(BF16).astype(F32)
                field[half, pl.ds(pl.multiple_of(s * PITCH + b * 16, 8), 16), :] = a
            for m in range(MODES):
                tails[half, pair, m] = tail[m].reshape(2, 8, LANES)
            return 0

        lax.fori_loop(0, 4, block, 0)

    for half in range(2):
        lanes = slice(half * LANES, (half + 1) * LANES)
        pole = poles(hr_ref, half, 16)

        def steps(i, states, half=half, lanes=lanes, pole=pole):
            for k in range(8):
                w = i * 8 + k
                u = field[half, pl.ds(w, 16, stride=PITCH), :]
                act_ref[w, :, lanes] = u.astype(BF16)
                states = [p * h + u for p, h in zip(pole, states)]
            return states

        states = lax.fori_loop(0, 8, steps, [jnp.zeros((16, LANES), F32)] * MODES)
        mine = info_ref[0] == half

        @pl.when(mine)
        def _(states=states):
            for m in range(MODES):
                mine_ref[:, m] = states[m].reshape(2, 8, LANES)

        @pl.when(jnp.logical_not(mine))
        def _(states=states):
            for m in range(MODES):
                other_ref[:, m] = states[m].reshape(2, 8, LANES)


def mix_kernel(info_ref, local_ref, keep_ref, got_ref, hr_ref, hc_ref, w_in_ref, w_out_ref, out_ref, horiz, mixed):
    core = info_ref[0]
    for half in range(2):
        lanes = slice(half * LANES, (half + 1) * LANES)
        pole = poles(hr_ref, half, 16)
        weight = weights(hr_ref, hc_ref, half, 16)
        mine = core == half
        tail = [
            jnp.where(mine, keep_ref[:, m], got_ref[:, m]).reshape(16, LANES) * (pole[m] * weight[m])
            for m in range(MODES)
        ]

        def steps(i, tail, lanes=lanes, pole=pole):
            for k in range(8):
                w = i * 8 + k
                y = local_ref[w, :, lanes] + tree(tail)
                tail = [p * g for p, g in zip(pole, tail)]
                horiz[pl.ds(pl.multiple_of(w * 16, 16), 16), lanes] = y
            return tail

        lax.fori_loop(0, 8, steps, tail)

    y = horiz[...]
    scale = lax.rsqrt(jnp.mean(y * y, axis=-1, keepdims=True) + 1e-06)
    normed = (y * scale).astype(BF16)
    hidden = gelu_packed(jnp.dot(normed, w_in_ref[...], preferred_element_type=F32))
    out = y + jnp.dot(hidden, w_out_ref[...], preferred_element_type=F32)
    for w in range(64):
        for half in range(2):
            lanes = slice(half * LANES, (half + 1) * LANES)
            mixed[half, pl.ds(w, 16, stride=PITCH), :] = out[w * 16 : (w + 1) * 16, lanes]
    for half in range(2):
        lanes = slice(half * LANES, (half + 1) * LANES)
        for h in range(16):
            out_ref[h, :, lanes] = mixed[half, h * PITCH : h * PITCH + 64].astype(BF16)


def in_hbm(block):
    return pltpu.with_memory_space_constraint(block, pltpu.HBM)


def whole(shape):
    return pl.BlockSpec(shape, lambda i: (0,) * len(shape))


def params(mib):
    return pltpu.CompilerParams(vmem_limit_bytes=mib * 1024 * 1024)


VMEM = pl.BlockSpec(memory_space=pltpu.VMEM)
HBM = pl.BlockSpec(memory_space=pltpu.HBM)
SMEM = pl.BlockSpec(memory_space=pltpu.SMEM)


def row_edges(image, rate):
    return pl.pallas_call(
        edge_kernel,
        in_specs=[HBM, HBM],
        out_specs=VMEM,
        out_shape=jax.ShapeDtypeStruct((2, 8, 8, 8, LANES), F32),
        scratch_shapes=[
            pltpu.VMEM((64, 64, 256), BF16),
            pltpu.VMEM((8, 256), F32),
            pltpu.SemaphoreType.DMA((5,)),
        ],
        compiler_params=params(24),
        name="row_edges",
    )(in_hbm(image), in_hbm(rate))


def prefix(edges, rate, span):
    def kernel(edge_ref, rate_ref, out_ref):
        prefix_kernel(span, edge_ref, rate_ref, out_ref)

    return pl.pallas_call(
        kernel,
        out_shape=jax.ShapeDtypeStruct(edges.shape, F32),
        compiler_params=params(8),
        name="prefix",
    )(edges, rate)


def local_scan(block, rate, coef, name, part=0, parts=1, into=None):
    steps = 4 // parts

    def kernel(*refs):
        local_kernel(*refs[:3], refs[-1])

    place = pl.BlockSpec((64, 16, 256), lambda i: (0, i + part * steps, 0))
    more = [] if into is None else [in_hbm(into)]
    return pl.pallas_call(
        kernel,
        grid=(steps,),
        in_specs=[place, whole((8, 256)), whole((8, 256))] + [HBM] * len(more),
        out_specs=place,
        out_shape=pltpu.HBM((64, 64, 256), F32),
        input_output_aliases={3: 0} if more else {},
        compiler_params=params(56),
        cost_estimate=pl.CostEstimate(
            flops=5_000_000_000 // parts, bytes_accessed=8_000_000 // parts, transcendentals=0
        ),
        name=name,
    )(block, rate, coef, *more)


def small(kernel, name, outs, *operands):
    return pl.pallas_call(
        kernel,
        in_specs=[SMEM] + [VMEM] * (len(operands) - 1),
        out_specs=[VMEM] * len(outs),
        out_shape=[jax.ShapeDtypeStruct(shape, F32) for shape in outs],
        compiler_params=params(8),
        name=name,
    )(*operands)


def act_and_edges(info, local, incoming, vert_rate, vert_coef, horiz_rate):
    edge = pl.BlockSpec((2, 8, 8, LANES), lambda i: (i, 0, 0, 0))
    return pl.pallas_call(
        act_kernel,
        grid=(4,),
        in_specs=[
            SMEM,
            pl.BlockSpec((16, 64, 256), lambda i: (i, 0, 0)),
            whole((2, 8, 8, 8, LANES)),
            whole((8, 256)),
            whole((8, 256)),
            whole((8, 256)),
        ],
        out_specs=[pl.BlockSpec((64, 16, 256), lambda i: (0, i, 0)), edge, edge],
        out_shape=[pltpu.HBM((64, 64, 256), BF16)] + [jax.ShapeDtypeStruct((8, 8, 8, LANES), F32)] * 2,
        scratch_shapes=[
            pltpu.VMEM((2, 8, 8, 8, LANES), F32),
            pltpu.VMEM((2, 16 * PITCH, LANES), F32),
        ],
        compiler_params=params(24),
        name="act_and_edges",
    )(info, in_hbm(local), incoming, vert_rate, vert_coef, horiz_rate)


def mix(info, local, keep, got, horiz_rate, horiz_coef, w_in, w_out):
    state = pl.BlockSpec((2, 8, 8, LANES), lambda i: (i, 0, 0, 0))
    return pl.pallas_call(
        mix_kernel,
        grid=(4,),
        in_specs=[
            SMEM,
            pl.BlockSpec((64, 16, 256), lambda i: (0, i, 0)),
            state,
            state,
            whole((8, 256)),
            whole((8, 256)),
            whole((256, 1024)),
            whole((1024, 256)),
        ],
        out_specs=pl.BlockSpec((16, 64, 256), lambda i: (i, 0, 0)),
        out_shape=jax.ShapeDtypeStruct((64, 64, 256), BF16),
        scratch_shapes=[pltpu.VMEM((1024, 256), F32), pltpu.VMEM((2, 16 * PITCH, LANES), F32)],
        compiler_params=params(40),
        name="mix",
    )(info, in_hbm(local), keep, got, horiz_rate, horiz_coef, w_in, w_out)


def swap(block, bits):
    n = lax.axis_size("col")
    return lax.ppermute(block, "col", [(i, i ^ bits) for i in range(n)])


def together(arrived, local):
    return lax.optimization_barrier((arrived, local))


def on_device(image, vert_rate, vert_coef, horiz_rate, horiz_coef, w_in, w_out):
    rows = lax.axis_size("row")
    piece = lax.axis_index("row")
    col = lax.axis_index("col")
    core, chip = col % 2, col // 2
    bits = [chip % 2, chip // 2 % 2, chip // 4]
    info = jnp.stack([core, bits[0], bits[1], bits[2], bits[0] ^ bits[2], bits[1] ^ bits[2]]).astype(jnp.int32)

    edges = row_edges(image, vert_rate).reshape(rows, 8, 8, LANES)
    edges = lax.all_to_all(edges, "row", 0, 0, tiled=True)
    rate_here = lax.dynamic_slice_in_dim(vert_rate, (piece // 8) * LANES, LANES, 1)
    local = local_scan(image, vert_rate, vert_coef, "vert_local")
    edges, local = together(edges, local)
    incoming = prefix(edges, rate_here, 64.0)
    incoming = lax.all_to_all(incoming, "row", 0, 0, tiled=True).reshape(2, 8, 8, 8, LANES)

    act, mine, other = act_and_edges(info, local, incoming, vert_rate, vert_coef, horiz_rate)

    rate = lax.dynamic_slice_in_dim(horiz_rate, core * LANES, LANES, 1)
    eight, four, two = (8, 8, 8, LANES), (4, 8, 8, LANES), (2, 8, 8, LANES)

    def horiz(part, into):
        return local_scan(act, horiz_rate, horiz_coef, f"horiz_local_{part}", part, 4, into)

    def join(level, outs, keep, came):
        kernel = functools.partial(join_kernel, level, 64.0 * 2**level)
        return small(kernel, f"join_{level}", outs, info, keep, came, rate)

    def part(level, shape, chains, first):
        kernel = functools.partial(part_kernel, level, 64.0 * 2**level)
        return small(kernel, f"part_{level}", [shape] * 2, info, *chains, first, rate)

    first_tile, keep, send = join(0, [eight, four, four], mine, swap(other, 1))
    came, local = together(swap(send, 2), horiz(0, None))
    first_chip, keep, send = join(1, [four, two, two], keep, came)
    came, local = together(swap(send, 4), horiz(1, local))
    first_pair, group = join(2, [two, two], keep, came)
    n = lax.axis_size("col")
    chain = lax.ppermute(group, "col", [(i, i ^ (n - 2)) for i in range(n // 2)])
    chain, local = together(chain, horiz(2, local))
    keep, send = part(2, two, [chain], first_pair)
    came, local = together(swap(send, 4), horiz(3, local))
    keep, send = part(1, four, [keep, came], first_chip)
    keep, send = part(0, eight, [keep, swap(send, 2)], first_tile)
    got = swap(send, 1)

    return mix(info, local, keep, got, horiz_rate, horiz_coef, w_in, w_out)


def solution(mesh):
    placed = (P("row", "col", None), P(), P(), P(), P(), P(), P())
    return jax.shard_map(
        on_device, mesh=mesh, in_specs=placed, out_specs=P("row", "col", None), check_vma=False
    )
```

```python
import functools
import math

import jax
import jax.numpy as jnp
from jax import lax
from jax.experimental import pallas as pl
from jax.experimental.pallas import tpu as pltpu
from jax.sharding import PartitionSpec as P

F32 = jnp.float32
BF16 = jnp.bfloat16
LANES = 128
MODES = 8
SQRT_2_PI = math.sqrt(2.0 / math.pi)
PITCH = 72
ACT_ROWS = 32


def gelu(x):
    inner = x * (SQRT_2_PI + (SQRT_2_PI * 0.044715) * (x * x))
    half = 0.5 * x
    return half + half * jnp.tanh(inner)


def gelu_packed(x):
    x = x.astype(BF16)
    inner = x * (BF16(SQRT_2_PI) + BF16(SQRT_2_PI * 0.044715) * (x * x))
    half = BF16(0.5) * x
    return half + half * jnp.tanh(inner)


def poles(rate_ref, half, rows):
    lanes = slice(half * LANES, (half + 1) * LANES)
    return [
        jnp.broadcast_to(jnp.exp(-rate_ref[m : m + 1, lanes]), (rows, LANES)) for m in range(MODES)
    ]


def weights(rate_ref, coef_ref, half, rows):
    lanes = slice(half * LANES, (half + 1) * LANES)
    return [
        jnp.broadcast_to(
            coef_ref[m : m + 1, lanes] * jnp.sqrt(1.0 - jnp.exp(-2.0 * rate_ref[m : m + 1, lanes])),
            (rows, LANES),
        )
        for m in range(MODES)
    ]


def tree(terms):
    while len(terms) > 1:
        terms = [a + b for a, b in zip(terms[::2], terms[1::2])]
    return terms[0]


def edge_kernel(image_ref, rate_hbm_ref, edge_ref, image, rate_ref, arrived):
    def fetch(i):
        cols = pl.ds(pl.multiple_of(i * 16, 16), 16)
        return pltpu.make_async_copy(image_ref.at[:, cols, :], image.at[:, cols, :], arrived.at[i])

    rates = pltpu.make_async_copy(rate_hbm_ref, rate_ref, arrived.at[4])
    rates.start()
    for i in range(4):
        fetch(i).start()
    rates.wait()

    def chunk(i, _):
        fetch(i).wait()
        cols = pl.ds(pl.multiple_of(i * 16, 16), 16)
        for half in range(2):
            lanes = slice(half * LANES, (half + 1) * LANES)
            pole = poles(rate_ref, half, 16)

            def steps(j, states, lanes=lanes, pole=pole):
                for k in range(16):
                    u = image[j * 16 + k, cols, lanes].astype(F32)
                    states = [p * h + u for p, h in zip(pole, states)]
                return states

            states = lax.fori_loop(0, 4, steps, [jnp.zeros((16, LANES), F32)] * MODES)
            for m in range(MODES):
                edge_ref[half, pl.ds(i * 2, 2), m] = states[m].reshape(2, 8, LANES)
        return 0

    lax.fori_loop(0, 4, chunk, 0)


def prefix_kernel(span, edge_ref, rate_ref, out_ref):
    decay = [
        jnp.broadcast_to(jnp.exp(-span * rate_ref[m : m + 1, :]), (8, LANES)) for m in range(MODES)
    ]
    states = [jnp.zeros((8, LANES), F32)] * MODES
    for r in range(edge_ref.shape[0]):
        for m in range(MODES):
            out_ref[r, m] = states[m]
            states[m] = decay[m] * states[m] + edge_ref[r, m]


def local_kernel(image_ref, rate_ref, coef_ref, out_ref):
    for half in range(2):
        lanes = slice(half * LANES, (half + 1) * LANES)
        pole = poles(rate_ref, half, 16)
        weight = weights(rate_ref, coef_ref, half, 16)

        def steps(i, states, lanes=lanes, pole=pole, weight=weight):
            for k in range(8):
                s = i * 8 + k
                u = image_ref[s, :, lanes].astype(F32)
                states = [p * h + u for p, h in zip(pole, states)]
                out_ref[s, :, lanes] = tree([q * h for q, h in zip(weight, states)])
            return states

        lax.fori_loop(0, 8, steps, [jnp.zeros((16, LANES), F32)] * MODES)


def decays(rate_ref, span):
    return [jnp.broadcast_to(jnp.exp(-span * rate_ref[m : m + 1, :]), (8, LANES)) for m in range(MODES)]


def join_kernel(span, core_ref, mine_ref, came_ref, rate_ref, first_ref, joined_ref):
    left_here = core_ref[0] == 0
    decay = decays(rate_ref, span)
    for b in range(8):
        for m in range(MODES):
            mine, came = mine_ref[b, m], came_ref[b, m]
            first = jnp.where(left_here, mine, came)
            first_ref[b, m] = first
            joined_ref[b, m] = decay[m] * first + jnp.where(left_here, came, mine)


def part_kernel(span, core_ref, chain_ref, first_ref, rate_ref, keep_ref, send_ref):
    left_here = core_ref[0] == 0
    decay = decays(rate_ref, span)
    for b in range(8):
        for m in range(MODES):
            chain = chain_ref[b, m]
            after = decay[m] * chain + first_ref[b, m]
            keep_ref[b, m] = jnp.where(left_here, chain, after)
            send_ref[b, m] = jnp.where(left_here, after, chain)


def act_kernel(side_ref, local_ref, in_ref, vr_ref, vc_ref, hr_ref, *refs):
    act_ref, edge_ref, tails, field = refs[-4:]
    rows = local_ref.shape[0]
    pole = poles(vr_ref, 0, 16)

    @pl.when(pl.program_id(0) == 0)
    def _():
        weight = weights(vr_ref, vc_ref, 0, 16)
        for m in range(MODES):
            tails[:, m] = in_ref[0, :, m] * (pole[m] * weight[m])[None, :8]

    def block(b, _):
        pair = pl.ds(b * 2, 2)
        cols = pl.ds(pl.multiple_of(b * 16, 16), 16)
        tail = [tails[pair, m].reshape(16, LANES) for m in range(MODES)]
        for s in range(rows):
            y = local_ref[s, cols, :] + tree(tail)
            tail = [p * g for p, g in zip(pole, tail)]
            a = gelu(y).astype(BF16).astype(F32)
            field[pl.ds(pl.multiple_of(s * PITCH + b * 16, 8), 16), :] = a
        for m in range(MODES):
            tails[pair, m] = tail[m].reshape(2, 8, LANES)
        return 0

    lax.fori_loop(0, 4, block, 0)
    pole_along = poles(hr_ref, 0, 16)
    for r in range(0, rows, 16):

        def steps(i, states, r=r):
            for k in range(8):
                w = i * 8 + k
                u = field[pl.ds(w + r * PITCH, 16, stride=PITCH), :]
                act_ref[w, r : r + 16, :] = u.astype(BF16)
                states = [p * h + u for p, h in zip(pole_along, states)]
            return states

        states = lax.fori_loop(0, 8, steps, [jnp.zeros((16, LANES), F32)] * MODES)
        for m in range(MODES):
            edge_ref[r // 8 : r // 8 + 2, m] = states[m].reshape(2, 8, LANES)


def mix_kernel(info_ref, local_ref, keep_ref, got_ref, hr_ref, hc_ref, w_in_ref, w_out_ref, out_ref, horiz, mixed):
    core = info_ref[0]
    for half in range(2):
        lanes = slice(half * LANES, (half + 1) * LANES)
        pole = poles(hr_ref, half, 16)
        weight = weights(hr_ref, hc_ref, half, 16)
        mine = core == half
        tail = [
            jnp.where(mine, keep_ref[:, m], got_ref[:, m]).reshape(16, LANES) * (pole[m] * weight[m])
            for m in range(MODES)
        ]

        def steps(i, tail, lanes=lanes, pole=pole):
            for k in range(8):
                w = i * 8 + k
                y = local_ref[w, :, lanes] + tree(tail)
                tail = [p * g for p, g in zip(pole, tail)]
                horiz[pl.ds(pl.multiple_of(w * 16, 16), 16), lanes] = y
            return tail

        lax.fori_loop(0, 8, steps, tail)

    y = horiz[...]
    scale = lax.rsqrt(jnp.mean(y * y, axis=-1, keepdims=True) + 1e-06)
    normed = (y * scale).astype(BF16)
    hidden = gelu_packed(jnp.dot(normed, w_in_ref[...], preferred_element_type=F32))
    out = y + jnp.dot(hidden, w_out_ref[...], preferred_element_type=F32)
    for w in range(64):
        for half in range(2):
            lanes = slice(half * LANES, (half + 1) * LANES)
            mixed[half, pl.ds(w, 16, stride=PITCH), :] = out[w * 16 : (w + 1) * 16, lanes]
    for half in range(2):
        lanes = slice(half * LANES, (half + 1) * LANES)
        for h in range(16):
            out_ref[h, :, lanes] = mixed[half, h * PITCH : h * PITCH + 64].astype(BF16)


def in_hbm(block):
    return pltpu.with_memory_space_constraint(block, pltpu.HBM)


def whole(shape):
    return pl.BlockSpec(shape, lambda i: (0,) * len(shape))


def params(mib):
    return pltpu.CompilerParams(vmem_limit_bytes=mib * 1024 * 1024)


VMEM = pl.BlockSpec(memory_space=pltpu.VMEM)
HBM = pl.BlockSpec(memory_space=pltpu.HBM)
SMEM = pl.BlockSpec(memory_space=pltpu.SMEM)


def row_edges(image, rate):
    return pl.pallas_call(
        edge_kernel,
        in_specs=[HBM, HBM],
        out_specs=VMEM,
        out_shape=jax.ShapeDtypeStruct((2, 8, 8, 8, LANES), F32),
        scratch_shapes=[
            pltpu.VMEM((64, 64, 256), BF16),
            pltpu.VMEM((8, 256), F32),
            pltpu.SemaphoreType.DMA((5,)),
        ],
        compiler_params=params(24),
        name="row_edges",
    )(in_hbm(image), in_hbm(rate))


def prefix(edges, rate, span):
    def kernel(edge_ref, rate_ref, out_ref):
        prefix_kernel(span, edge_ref, rate_ref, out_ref)

    return pl.pallas_call(
        kernel,
        out_shape=jax.ShapeDtypeStruct(edges.shape, F32),
        compiler_params=params(8),
        name="prefix",
    )(edges, rate)


def local_scan(block, rate, coef, name):
    place = pl.BlockSpec((64, 16, 256), lambda i: (0, i, 0))
    return pl.pallas_call(
        local_kernel,
        grid=(4,),
        in_specs=[place, whole((8, 256)), whole((8, 256))],
        out_specs=place,
        out_shape=pltpu.HBM((64, 64, 256), F32),
        compiler_params=params(56),
        cost_estimate=pl.CostEstimate(flops=5_000_000_000, bytes_accessed=8_000_000, transcendentals=0),
        name=name,
    )(block, rate, coef)


def small(kernel, name, outs, *operands):
    return pl.pallas_call(
        kernel,
        in_specs=[SMEM] + [VMEM] * (len(operands) - 1),
        out_specs=[VMEM] * len(outs),
        out_shape=[jax.ShapeDtypeStruct(shape, F32) for shape in outs],
        compiler_params=params(8),
        name=name,
    )(*operands)


def act_and_edges(side, local, incoming, vert_rate, vert_coef, horiz_rate, into=None):
    rate = pl.BlockSpec((8, LANES), lambda i, side: (0, side[0]))
    more = [] if into is None else [in_hbm(into)]
    return pl.pallas_call(
        act_kernel,
        grid_spec=pltpu.PrefetchScalarGridSpec(
            num_scalar_prefetch=1,
            grid=(64 // ACT_ROWS,),
            in_specs=[
                pl.BlockSpec((ACT_ROWS, 64, LANES), lambda i, side: (i, 0, side[0])),
                pl.BlockSpec((1, 8, 8, 8, LANES), lambda i, side: (side[0], 0, 0, 0, 0)),
                rate,
                rate,
                rate,
            ]
            + [HBM] * len(more),
            out_specs=[
                pl.BlockSpec((64, ACT_ROWS, LANES), lambda i, side: (0, i, side[0])),
                pl.BlockSpec((ACT_ROWS // 8, 8, 8, LANES), lambda i, side: (i, 0, 0, 0)),
            ],
            scratch_shapes=[
                pltpu.VMEM((8, 8, 8, LANES), F32),
                pltpu.VMEM((ACT_ROWS * PITCH, LANES), F32),
            ],
        ),
        out_shape=[pltpu.HBM((64, 64, 256), BF16), jax.ShapeDtypeStruct((8, 8, 8, LANES), F32)],
        input_output_aliases={6: 0} if more else {},
        compiler_params=params(24),
        cost_estimate=pl.CostEstimate(flops=3_000_000_000, bytes_accessed=4_000_000, transcendentals=0),
        name="act_and_edges",
    )(side, in_hbm(local), incoming, vert_rate, vert_coef, horiz_rate, *more)


def mix(info, local, keep, got, horiz_rate, horiz_coef, w_in, w_out):
    state = pl.BlockSpec((2, 8, 8, LANES), lambda i: (i, 0, 0, 0))
    return pl.pallas_call(
        mix_kernel,
        grid=(4,),
        in_specs=[
            SMEM,
            pl.BlockSpec((64, 16, 256), lambda i: (0, i, 0)),
            state,
            state,
            whole((8, 256)),
            whole((8, 256)),
            whole((256, 1024)),
            whole((1024, 256)),
        ],
        out_specs=pl.BlockSpec((16, 64, 256), lambda i: (i, 0, 0)),
        out_shape=jax.ShapeDtypeStruct((64, 64, 256), BF16),
        scratch_shapes=[pltpu.VMEM((1024, 256), F32), pltpu.VMEM((2, 16 * PITCH, LANES), F32)],
        compiler_params=params(40),
        name="mix",
    )(info, in_hbm(local), keep, got, horiz_rate, horiz_coef, w_in, w_out)


def swap(block, bits):
    n = lax.axis_size("col")
    return lax.ppermute(block, "col", [(i, i ^ bits) for i in range(n)])


def together(arrived, local):
    return lax.optimization_barrier((arrived, local))


def on_device(image, vert_rate, vert_coef, horiz_rate, horiz_coef, w_in, w_out):
    rows, cols = lax.axis_size("row"), lax.axis_size("col")
    piece = lax.axis_index("row")
    core = lax.axis_index("col") % 2
    mine, other = core.reshape(1), (1 - core).reshape(1)

    edges = row_edges(image, vert_rate).reshape(rows, 8, 8, LANES)
    edges = lax.all_to_all(edges, "row", 0, 0, tiled=True)
    rate = lax.dynamic_slice_in_dim(vert_rate, (piece // 8) * LANES, LANES, 1)
    local = local_scan(image, vert_rate, vert_coef, "vert_local")
    edges, local = together(edges, local)
    incoming = prefix(edges, rate, 64.0)
    incoming = lax.all_to_all(incoming, "row", 0, 0, tiled=True).reshape(2, 8, 8, 8, LANES)

    vert = (incoming, vert_rate, vert_coef, horiz_rate)
    act, edge = act_and_edges(other, local, *vert)
    came = swap(edge, 1)
    act, edge = act_and_edges(mine, local, *vert, act)

    chips = [[2 * z + c for z in range(cols // 2)] for c in range(2)]
    rate = lax.dynamic_slice_in_dim(horiz_rate, core * LANES, LANES, 1)
    tile = [(8, 8, 8, LANES)] * 2
    join = functools.partial(join_kernel, 64.0)
    first, joined = small(join, "join_cores", tile, mine, edge, came, rate)
    joined = lax.all_to_all(joined, "col", 0, 0, tiled=True, axis_index_groups=chips)
    local = local_scan(act, horiz_rate, horiz_coef, "horiz_local")
    joined, local = together(joined, local)
    chain = prefix(joined, rate, 128.0)
    chain = lax.all_to_all(chain, "col", 0, 0, tiled=True, axis_index_groups=chips)
    part = functools.partial(part_kernel, 64.0)
    keep, send = small(part, "part_cores", tile, mine, chain, first, rate)
    got = swap(send, 1)

    return mix(mine, local, keep, got, horiz_rate, horiz_coef, w_in, w_out)


def solution(mesh):
    placed = (P("row", "col", None), P(), P(), P(), P(), P(), P())
    return jax.shard_map(
        on_device, mesh=mesh, in_specs=placed, out_specs=P("row", "col", None), check_vma=False
    )
```

```python
import functools
import math

import jax
import jax.numpy as jnp
from jax import lax
from jax.experimental import pallas as pl
from jax.experimental.pallas import tpu as pltpu
from jax.sharding import PartitionSpec as P

F32 = jnp.float32
BF16 = jnp.bfloat16
LANES = 128
MODES = 8
SQRT_2_PI = math.sqrt(2.0 / math.pi)
PITCH = 73
ACT_ROWS = 16
MIX_ROWS = 16


def gelu_of_half(x):
    inner = x * (2.0 * SQRT_2_PI + (8.0 * SQRT_2_PI * 0.044715) * (x * x))
    return x + x * jnp.tanh(inner)


def gelu_packed(x):
    x = x.astype(BF16)
    inner = x * (BF16(SQRT_2_PI) + BF16(SQRT_2_PI * 0.044715) * (x * x))
    half = BF16(0.5) * x
    return half + half * jnp.tanh(inner)


def poles(rate_ref, half, rows):
    lanes = slice(half * LANES, (half + 1) * LANES)
    return [
        jnp.broadcast_to(jnp.exp(-rate_ref[m : m + 1, lanes]), (rows, LANES)) for m in range(MODES)
    ]


def weights(rate_ref, coef_ref, half, rows):
    lanes = slice(half * LANES, (half + 1) * LANES)
    return [
        jnp.broadcast_to(
            coef_ref[m : m + 1, lanes] * jnp.sqrt(1.0 - jnp.exp(-2.0 * rate_ref[m : m + 1, lanes])),
            (rows, LANES),
        )
        for m in range(MODES)
    ]


def tree(terms):
    while len(terms) > 1:
        terms = [a + b for a, b in zip(terms[::2], terms[1::2])]
    return terms[0]


def edge_kernel(image_ref, rate_hbm_ref, edge_ref, image, rate_ref, arrived):
    def fetch(i):
        cols = pl.ds(pl.multiple_of(i * 16, 16), 16)
        return pltpu.make_async_copy(image_ref.at[:, cols, :], image.at[:, cols, :], arrived.at[i])

    rates = pltpu.make_async_copy(rate_hbm_ref, rate_ref, arrived.at[4])
    rates.start()
    for i in range(4):
        fetch(i).start()
    rates.wait()

    def chunk(i, _):
        fetch(i).wait()
        cols = pl.ds(pl.multiple_of(i * 16, 16), 16)
        for half in range(2):
            lanes = slice(half * LANES, (half + 1) * LANES)
            pole = poles(rate_ref, half, 16)

            def steps(j, states, lanes=lanes, pole=pole):
                for k in range(16):
                    u = image[j * 16 + k, cols, lanes].astype(F32)
                    states = [p * h + u for p, h in zip(pole, states)]
                return states

            states = lax.fori_loop(0, 4, steps, [jnp.zeros((16, LANES), F32)] * MODES)
            for m in range(MODES):
                edge_ref[half, pl.ds(i * 2, 2), m] = states[m].reshape(2, 8, LANES)
        return 0

    lax.fori_loop(0, 4, chunk, 0)


def prefix_kernel(span, edge_ref, rate_ref, out_ref):
    decay = [
        jnp.broadcast_to(jnp.exp(-span * rate_ref[m : m + 1, :]), (8, LANES)) for m in range(MODES)
    ]
    states = [jnp.zeros((8, LANES), F32)] * MODES
    for r in range(edge_ref.shape[0]):
        for m in range(MODES):
            out_ref[r, m] = states[m]
            states[m] = decay[m] * states[m] + edge_ref[r, m]


def local_kernel(scale, image_ref, rate_ref, coef_ref, out_ref):
    for half in range(2):
        lanes = slice(half * LANES, (half + 1) * LANES)
        pole = poles(rate_ref, half, 16)
        weight = [scale * q for q in weights(rate_ref, coef_ref, half, 16)]

        def steps(i, states, lanes=lanes, pole=pole, weight=weight):
            for k in range(8):
                s = i * 8 + k
                u = image_ref[s, :, lanes].astype(F32)
                states = [p * h + u for p, h in zip(pole, states)]
                out_ref[s, :, lanes] = tree([q * h for q, h in zip(weight, states)])
            return states

        lax.fori_loop(0, 8, steps, [jnp.zeros((16, LANES), F32)] * MODES)


def decays(rate_ref, span):
    return [jnp.broadcast_to(jnp.exp(-span * rate_ref[m : m + 1, :]), (8, LANES)) for m in range(MODES)]


def join_kernel(span, core_ref, mine_ref, came_ref, rate_ref, first_ref, joined_ref):
    left_here = core_ref[0] == 0
    decay = decays(rate_ref, span)
    for b in range(8):
        for m in range(MODES):
            mine, came = mine_ref[b, m], came_ref[b, m]
            first = jnp.where(left_here, mine, came)
            first_ref[b, m] = first
            joined_ref[b, m] = decay[m] * first + jnp.where(left_here, came, mine)


def part_kernel(span, core_ref, chain_ref, first_ref, rate_ref, keep_ref, send_ref):
    left_here = core_ref[0] == 0
    decay = decays(rate_ref, span)
    for b in range(8):
        for m in range(MODES):
            chain = chain_ref[b, m]
            after = decay[m] * chain + first_ref[b, m]
            keep_ref[b, m] = jnp.where(left_here, chain, after)
            send_ref[b, m] = jnp.where(left_here, after, chain)


def act_kernel(core_ref, local_ref, in_ref, vr_ref, vc_ref, hr_ref, act_ref, mine_ref, other_ref, tails, field):
    for half in range(2):
        lanes = slice(half * LANES, (half + 1) * LANES)
        pole = poles(vr_ref, half, 16)

        @pl.when(pl.program_id(0) == 0)
        def _(half=half, pole=pole):
            weight = weights(vr_ref, vc_ref, half, 16)
            for m in range(MODES):
                factor = (0.5 * pole[m] * weight[m])[None, :8]
                tails[half, :, m] = in_ref[half, :, m] * factor

        def block(b, _, half=half, lanes=lanes, pole=pole):
            pair = pl.ds(b * 2, 2)
            cols = pl.ds(pl.multiple_of(b * 16, 16), 16)
            tail = [tails[half, pair, m].reshape(16, LANES) for m in range(MODES)]
            for s in range(local_ref.shape[0]):
                y = local_ref[s, cols, lanes] + tree(tail)
                tail = [p * g for p, g in zip(pole, tail)]
                a = gelu_of_half(y).astype(BF16).astype(F32)
                field[half, pl.ds(s * PITCH + b * 16, 16), :] = a
            for m in range(MODES):
                tails[half, pair, m] = tail[m].reshape(2, 8, LANES)
            return 0

        lax.fori_loop(0, 4, block, 0)

    for half in range(2):
        lanes = slice(half * LANES, (half + 1) * LANES)
        pole = poles(hr_ref, half, 16)
        mine = core_ref[0] == half
        for r in range(0, local_ref.shape[0], 16):

            def steps(i, states, half=half, lanes=lanes, pole=pole, r=r):
                for k in range(16):
                    w = i * 16 + k
                    u = field[half, pl.ds(w + r * PITCH, 16, stride=PITCH), :]
                    act_ref[w, r : r + 16, lanes] = u.astype(BF16)
                    states = [p * h + u for p, h in zip(pole, states)]
                return states

            states = lax.fori_loop(0, 4, steps, [jnp.zeros((16, LANES), F32)] * MODES)

            @pl.when(mine)
            def _(states=states, r=r):
                for m in range(MODES):
                    mine_ref[r // 8 : r // 8 + 2, m] = states[m].reshape(2, 8, LANES)

            @pl.when(jnp.logical_not(mine))
            def _(states=states, r=r):
                for m in range(MODES):
                    other_ref[r // 8 : r // 8 + 2, m] = states[m].reshape(2, 8, LANES)


def mix_kernel(core_ref, local_ref, keep_ref, got_ref, hr_ref, hc_ref, w_in_ref, w_out_ref, out_ref, horiz, mixed):
    core = core_ref[0]
    rows = local_ref.shape[1]
    for r in range(0, rows, 16):
        pair = pl.ds(pl.program_id(0) * (rows // 8) + r // 8, 2)
        for half in range(2):
            lanes = slice(half * LANES, (half + 1) * LANES)
            pole = poles(hr_ref, half, 16)
            weight = weights(hr_ref, hc_ref, half, 16)
            mine = core == half
            tail = [
                jnp.where(mine, keep_ref[pair, m], got_ref[pair, m]).reshape(16, LANES)
                * (pole[m] * weight[m])
                for m in range(MODES)
            ]

            def steps(i, tail, lanes=lanes, pole=pole, r=r):
                for k in range(8):
                    w = i * 8 + k
                    y = local_ref[w, r : r + 16, lanes] + tree(tail)
                    tail = [p * g for p, g in zip(pole, tail)]
                    horiz[pl.ds(pl.multiple_of(w * 16, 16), 16), lanes] = y
                return tail

            lax.fori_loop(0, 8, steps, tail)

        y = horiz[...]
        scale = lax.rsqrt(jnp.mean(y * y, axis=-1, keepdims=True) + 1e-06)
        normed = (y * scale).astype(BF16)
        hidden = gelu_packed(jnp.dot(normed, w_in_ref[...], preferred_element_type=F32))
        out = y + jnp.dot(hidden, w_out_ref[...], preferred_element_type=F32)
        for w in range(64):
            for half in range(2):
                lanes = slice(half * LANES, (half + 1) * LANES)
                mixed[half, pl.ds(w, 16, stride=PITCH), :] = out[w * 16 : (w + 1) * 16, lanes]
        for half in range(2):
            lanes = slice(half * LANES, (half + 1) * LANES)
            for h in range(16):
                out_ref[r + h, :, lanes] = mixed[half, h * PITCH : h * PITCH + 64].astype(BF16)


def in_hbm(block):
    return pltpu.with_memory_space_constraint(block, pltpu.HBM)


def whole(shape):
    return pl.BlockSpec(shape, lambda i: (0,) * len(shape))


def params(mib):
    return pltpu.CompilerParams(vmem_limit_bytes=mib * 1024 * 1024)


VMEM = pl.BlockSpec(memory_space=pltpu.VMEM)
HBM = pl.BlockSpec(memory_space=pltpu.HBM)
SMEM = pl.BlockSpec(memory_space=pltpu.SMEM)


def row_edges(image, rate):
    return pl.pallas_call(
        edge_kernel,
        in_specs=[HBM, HBM],
        out_specs=VMEM,
        out_shape=jax.ShapeDtypeStruct((2, 8, 8, 8, LANES), F32),
        scratch_shapes=[
            pltpu.VMEM((64, 64, 256), BF16),
            pltpu.VMEM((8, 256), F32),
            pltpu.SemaphoreType.DMA((5,)),
        ],
        compiler_params=params(24),
        name="row_edges",
    )(in_hbm(image), in_hbm(rate))


def prefix(edges, rate, span):
    def kernel(edge_ref, rate_ref, out_ref):
        prefix_kernel(span, edge_ref, rate_ref, out_ref)

    return pl.pallas_call(
        kernel,
        out_shape=jax.ShapeDtypeStruct(edges.shape, F32),
        compiler_params=params(8),
        name="prefix",
    )(edges, rate)


def local_scan(block, rate, coef, name, scale):
    place = pl.BlockSpec((64, 16, 256), lambda i: (0, i, 0))
    return pl.pallas_call(
        functools.partial(local_kernel, scale),
        grid=(4,),
        in_specs=[place, whole((8, 256)), whole((8, 256))],
        out_specs=place,
        out_shape=pltpu.HBM((64, 64, 256), F32),
        compiler_params=params(56),
        cost_estimate=pl.CostEstimate(flops=5_000_000_000, bytes_accessed=8_000_000, transcendentals=0),
        name=name,
    )(block, rate, coef)


def small(kernel, name, outs, *operands):
    return pl.pallas_call(
        kernel,
        in_specs=[SMEM] + [VMEM] * (len(operands) - 1),
        out_specs=[VMEM] * len(outs),
        out_shape=[jax.ShapeDtypeStruct(shape, F32) for shape in outs],
        compiler_params=params(8),
        name=name,
    )(*operands)


def act_and_edges(core, local, incoming, vert_rate, vert_coef, horiz_rate):
    edge = pl.BlockSpec((ACT_ROWS // 8, 8, 8, LANES), lambda i: (i, 0, 0, 0))
    return pl.pallas_call(
        act_kernel,
        grid=(64 // ACT_ROWS,),
        in_specs=[SMEM, pl.BlockSpec((ACT_ROWS, 64, 256), lambda i: (i, 0, 0)), VMEM, VMEM, VMEM, VMEM],
        out_specs=[pl.BlockSpec((64, ACT_ROWS, 256), lambda i: (0, i, 0)), edge, edge],
        out_shape=[pltpu.HBM((64, 64, 256), BF16)] + [jax.ShapeDtypeStruct((8, 8, 8, LANES), F32)] * 2,
        scratch_shapes=[
            pltpu.VMEM((2, 8, 8, 8, LANES), F32),
            pltpu.VMEM((2, ACT_ROWS * PITCH, LANES), F32),
        ],
        compiler_params=params(24),
        name="act_and_edges",
    )(core, in_hbm(local), incoming, vert_rate, vert_coef, horiz_rate)


def mix(core, local, keep, got, horiz_rate, horiz_coef, w_in, w_out):
    return pl.pallas_call(
        mix_kernel,
        grid=(64 // MIX_ROWS,),
        in_specs=[SMEM, pl.BlockSpec((64, MIX_ROWS, 256), lambda i: (0, i, 0))] + [VMEM] * 6,
        out_specs=pl.BlockSpec((MIX_ROWS, 64, 256), lambda i: (i, 0, 0)),
        out_shape=jax.ShapeDtypeStruct((64, 64, 256), BF16),
        scratch_shapes=[pltpu.VMEM((1024, 256), F32), pltpu.VMEM((2, 16 * PITCH, LANES), F32)],
        compiler_params=params(40),
        name="mix",
    )(core, in_hbm(local), keep, got, horiz_rate, horiz_coef, w_in, w_out)


def swap(block, bits):
    n = lax.axis_size("col")
    return lax.ppermute(block, "col", [(i, i ^ bits) for i in range(n)])


def together(arrived, local):
    return lax.optimization_barrier((arrived, local))


def on_device(image, vert_rate, vert_coef, horiz_rate, horiz_coef, w_in, w_out):
    rows, cols = lax.axis_size("row"), lax.axis_size("col")
    piece = lax.axis_index("row")
    core = (lax.axis_index("col") % 2).reshape(1)

    edges = row_edges(image, vert_rate).reshape(rows, 8, 8, LANES)
    edges = lax.all_to_all(edges, "row", 0, 0, tiled=True)
    rate = lax.dynamic_slice_in_dim(vert_rate, (piece // 8) * LANES, LANES, 1)
    local = local_scan(image, vert_rate, vert_coef, "vert_local", 0.5)
    edges, local = together(edges, local)
    incoming = prefix(edges, rate, 64.0)
    incoming = lax.all_to_all(incoming, "row", 0, 0, tiled=True).reshape(2, 8, 8, 8, LANES)

    act, edge, other = act_and_edges(core, local, incoming, vert_rate, vert_coef, horiz_rate)

    chips = [[2 * z + c for z in range(cols // 2)] for c in range(2)]
    rate = lax.dynamic_slice_in_dim(horiz_rate, core[0] * LANES, LANES, 1)
    tile = [(8, 8, 8, LANES)] * 2
    join = functools.partial(join_kernel, 64.0)
    first, joined = small(join, "join_cores", tile, core, edge, swap(other, 1), rate)
    joined = lax.all_to_all(joined, "col", 0, 0, tiled=True, axis_index_groups=chips)
    local = local_scan(act, horiz_rate, horiz_coef, "horiz_local", 1.0)
    joined, local = together(joined, local)
    chain = prefix(joined, rate, 128.0)
    chain = lax.all_to_all(chain, "col", 0, 0, tiled=True, axis_index_groups=chips)
    part = functools.partial(part_kernel, 64.0)
    keep, send = small(part, "part_cores", tile, core, chain, first, rate)
    got = swap(send, 1)

    return mix(core, local, keep, got, horiz_rate, horiz_coef, w_in, w_out)


def solution(mesh):
    placed = (P("row", "col", None), P(), P(), P(), P(), P(), P())
    return jax.shard_map(
        on_device, mesh=mesh, in_specs=placed, out_specs=P("row", "col", None), check_vma=False
    )
```

```python
import functools
import math

import jax
import jax.numpy as jnp
from jax import lax
from jax.experimental import pallas as pl
from jax.experimental.pallas import tpu as pltpu
from jax.sharding import PartitionSpec as P

F32 = jnp.float32
BF16 = jnp.bfloat16
LANES = 128
MODES = 8
SQRT_2_PI = math.sqrt(2.0 / math.pi)
PITCH = 73
ACT_ROWS = 16
MIX_ROWS = 16


def gelu_of_half(x):
    inner = x * (2.0 * SQRT_2_PI + (8.0 * SQRT_2_PI * 0.044715) * (x * x))
    return x + x * jnp.tanh(inner)


def gelu_packed(x):
    x = x.astype(BF16)
    inner = x * (BF16(SQRT_2_PI) + BF16(SQRT_2_PI * 0.044715) * (x * x))
    half = BF16(0.5) * x
    return half + half * jnp.tanh(inner)


def poles(rate_ref, half, rows):
    lanes = slice(half * LANES, (half + 1) * LANES)
    return [
        jnp.broadcast_to(jnp.exp(-rate_ref[m : m + 1, lanes]), (rows, LANES)) for m in range(MODES)
    ]


def weights(rate_ref, coef_ref, half, rows):
    lanes = slice(half * LANES, (half + 1) * LANES)
    return [
        jnp.broadcast_to(
            coef_ref[m : m + 1, lanes] * jnp.sqrt(1.0 - jnp.exp(-2.0 * rate_ref[m : m + 1, lanes])),
            (rows, LANES),
        )
        for m in range(MODES)
    ]


def tree(terms):
    while len(terms) > 1:
        terms = [a + b for a, b in zip(terms[::2], terms[1::2])]
    return terms[0]


def edge_kernel(image_ref, rate_hbm_ref, edge_ref, image, rate_ref, arrived):
    def fetch(i):
        cols = pl.ds(pl.multiple_of(i * 16, 16), 16)
        return pltpu.make_async_copy(image_ref.at[:, cols, :], image.at[:, cols, :], arrived.at[i])

    rates = pltpu.make_async_copy(rate_hbm_ref, rate_ref, arrived.at[4])
    rates.start()
    for i in range(4):
        fetch(i).start()
    rates.wait()

    def chunk(i, _):
        fetch(i).wait()
        cols = pl.ds(pl.multiple_of(i * 16, 16), 16)
        for half in range(2):
            lanes = slice(half * LANES, (half + 1) * LANES)
            pole = poles(rate_ref, half, 16)

            def steps(j, states, lanes=lanes, pole=pole):
                for k in range(16):
                    u = image[j * 16 + k, cols, lanes].astype(F32)
                    states = [p * h + u for p, h in zip(pole, states)]
                return states

            states = lax.fori_loop(0, 4, steps, [jnp.zeros((16, LANES), F32)] * MODES)
            for m in range(MODES):
                edge_ref[half, pl.ds(i * 2, 2), m] = states[m].reshape(2, 8, LANES)
        return 0

    lax.fori_loop(0, 4, chunk, 0)


def prefix_kernel(span, edge_ref, rate_ref, out_ref):
    decay = [
        jnp.broadcast_to(jnp.exp(-span * rate_ref[m : m + 1, :]), (8, LANES)) for m in range(MODES)
    ]
    states = [jnp.zeros((8, LANES), F32)] * MODES
    for r in range(edge_ref.shape[0]):
        for m in range(MODES):
            out_ref[r, m] = states[m]
            states[m] = decay[m] * states[m] + edge_ref[r, m]


def local_kernel(scale, block_ref, rate_ref, coef_ref, out_ref, block, result, arrived, left):
    def part(i):
        return pl.ds(pl.multiple_of(i * 16, 16), 16)

    def fetch(i):
        return pltpu.make_async_copy(block_ref.at[:, part(i), :], block.at[:, part(i), :], arrived.at[i])

    def put(i):
        return pltpu.make_async_copy(result.at[:, part(i), :], out_ref.at[:, part(i), :], left.at[i])

    for i in range(4):
        fetch(i).start()

    def chunk(i, _):
        fetch(i).wait()
        for half in range(2):
            lanes = slice(half * LANES, (half + 1) * LANES)
            pole = poles(rate_ref, half, 16)
            weight = [scale * q for q in weights(rate_ref, coef_ref, half, 16)]

            def steps(j, states, lanes=lanes, pole=pole, weight=weight):
                for k in range(16):
                    s = j * 16 + k
                    u = block[s, part(i), lanes].astype(F32)
                    states = [p * h + u for p, h in zip(pole, states)]
                    result[s, part(i), lanes] = tree([q * h for q, h in zip(weight, states)])
                return states

            lax.fori_loop(0, 4, steps, [jnp.zeros((16, LANES), F32)] * MODES)
        put(i).start()
        return 0

    lax.fori_loop(0, 4, chunk, 0)
    for i in range(4):
        put(i).wait()


def decays(rate_ref, span):
    return [jnp.broadcast_to(jnp.exp(-span * rate_ref[m : m + 1, :]), (8, LANES)) for m in range(MODES)]


def join_kernel(span, core_ref, mine_ref, came_ref, rate_ref, first_ref, joined_ref):
    left_here = core_ref[0] == 0
    decay = decays(rate_ref, span)
    for b in range(8):
        for m in range(MODES):
            mine, came = mine_ref[b, m], came_ref[b, m]
            first = jnp.where(left_here, mine, came)
            first_ref[b, m] = first
            joined_ref[b, m] = decay[m] * first + jnp.where(left_here, came, mine)


def part_kernel(span, core_ref, chain_ref, first_ref, rate_ref, keep_ref, send_ref):
    left_here = core_ref[0] == 0
    decay = decays(rate_ref, span)
    for b in range(8):
        for m in range(MODES):
            chain = chain_ref[b, m]
            after = decay[m] * chain + first_ref[b, m]
            keep_ref[b, m] = jnp.where(left_here, chain, after)
            send_ref[b, m] = jnp.where(left_here, after, chain)


def act_kernel(core_ref, local_ref, in_ref, vr_ref, vc_ref, hr_ref, act_ref, mine_ref, other_ref, tails, field):
    for half in range(2):
        lanes = slice(half * LANES, (half + 1) * LANES)
        pole = poles(vr_ref, half, 16)

        @pl.when(pl.program_id(0) == 0)
        def _(half=half, pole=pole):
            weight = weights(vr_ref, vc_ref, half, 16)
            for m in range(MODES):
                factor = (0.5 * pole[m] * weight[m])[None, :8]
                tails[half, :, m] = in_ref[half, :, m] * factor

        def block(b, _, half=half, lanes=lanes, pole=pole):
            pair = pl.ds(b * 2, 2)
            cols = pl.ds(pl.multiple_of(b * 16, 16), 16)
            tail = [tails[half, pair, m].reshape(16, LANES) for m in range(MODES)]
            for s in range(local_ref.shape[0]):
                y = local_ref[s, cols, lanes] + tree(tail)
                tail = [p * g for p, g in zip(pole, tail)]
                a = gelu_of_half(y).astype(BF16).astype(F32)
                field[half, pl.ds(s * PITCH + b * 16, 16), :] = a
            for m in range(MODES):
                tails[half, pair, m] = tail[m].reshape(2, 8, LANES)
            return 0

        lax.fori_loop(0, 4, block, 0)

    for half in range(2):
        lanes = slice(half * LANES, (half + 1) * LANES)
        pole = poles(hr_ref, half, 16)
        mine = core_ref[0] == half
        for r in range(0, local_ref.shape[0], 16):

            def steps(i, states, half=half, lanes=lanes, pole=pole, r=r):
                for k in range(16):
                    w = i * 16 + k
                    u = field[half, pl.ds(w + r * PITCH, 16, stride=PITCH), :]
                    act_ref[w, r : r + 16, lanes] = u.astype(BF16)
                    states = [p * h + u for p, h in zip(pole, states)]
                return states

            states = lax.fori_loop(0, 4, steps, [jnp.zeros((16, LANES), F32)] * MODES)

            @pl.when(mine)
            def _(states=states, r=r):
                for m in range(MODES):
                    mine_ref[r // 8 : r // 8 + 2, m] = states[m].reshape(2, 8, LANES)

            @pl.when(jnp.logical_not(mine))
            def _(states=states, r=r):
                for m in range(MODES):
                    other_ref[r // 8 : r // 8 + 2, m] = states[m].reshape(2, 8, LANES)


def mix_kernel(core_ref, local_ref, keep_ref, got_ref, hr_ref, hc_ref, w_in_ref, w_out_ref, out_ref, horiz, mixed):
    core = core_ref[0]
    rows = local_ref.shape[1]
    for r in range(0, rows, 16):
        pair = pl.ds(pl.program_id(0) * (rows // 8) + r // 8, 2)
        for half in range(2):
            lanes = slice(half * LANES, (half + 1) * LANES)
            pole = poles(hr_ref, half, 16)
            weight = weights(hr_ref, hc_ref, half, 16)
            mine = core == half
            tail = [
                jnp.where(mine, keep_ref[pair, m], got_ref[pair, m]).reshape(16, LANES)
                * (pole[m] * weight[m])
                for m in range(MODES)
            ]

            def steps(i, tail, lanes=lanes, pole=pole, r=r):
                for k in range(8):
                    w = i * 8 + k
                    y = local_ref[w, r : r + 16, lanes] + tree(tail)
                    tail = [p * g for p, g in zip(pole, tail)]
                    horiz[pl.ds(pl.multiple_of(w * 16, 16), 16), lanes] = y
                return tail

            lax.fori_loop(0, 8, steps, tail)

        y = horiz[...]
        scale = lax.rsqrt(jnp.mean(y * y, axis=-1, keepdims=True) + 1e-06)
        normed = (y * scale).astype(BF16)
        hidden = gelu_packed(jnp.dot(normed, w_in_ref[...], preferred_element_type=F32))
        out = y + jnp.dot(hidden, w_out_ref[...], preferred_element_type=F32)
        for w in range(64):
            for half in range(2):
                lanes = slice(half * LANES, (half + 1) * LANES)
                mixed[half, pl.ds(w, 16, stride=PITCH), :] = out[w * 16 : (w + 1) * 16, lanes]
        for half in range(2):
            lanes = slice(half * LANES, (half + 1) * LANES)
            for h in range(16):
                out_ref[r + h, :, lanes] = mixed[half, h * PITCH : h * PITCH + 64].astype(BF16)


def in_hbm(block):
    return pltpu.with_memory_space_constraint(block, pltpu.HBM)


def whole(shape):
    return pl.BlockSpec(shape, lambda i: (0,) * len(shape))


def params(mib):
    return pltpu.CompilerParams(vmem_limit_bytes=mib * 1024 * 1024)


VMEM = pl.BlockSpec(memory_space=pltpu.VMEM)
HBM = pl.BlockSpec(memory_space=pltpu.HBM)
SMEM = pl.BlockSpec(memory_space=pltpu.SMEM)


def row_edges(image, rate):
    return pl.pallas_call(
        edge_kernel,
        in_specs=[HBM, HBM],
        out_specs=VMEM,
        out_shape=jax.ShapeDtypeStruct((2, 8, 8, 8, LANES), F32),
        scratch_shapes=[
            pltpu.VMEM((64, 64, 256), BF16),
            pltpu.VMEM((8, 256), F32),
            pltpu.SemaphoreType.DMA((5,)),
        ],
        compiler_params=params(24),
        name="row_edges",
    )(in_hbm(image), in_hbm(rate))


def prefix(edges, rate, span):
    def kernel(edge_ref, rate_ref, out_ref):
        prefix_kernel(span, edge_ref, rate_ref, out_ref)

    return pl.pallas_call(
        kernel,
        out_shape=jax.ShapeDtypeStruct(edges.shape, F32),
        compiler_params=params(8),
        name="prefix",
    )(edges, rate)


def local_scan(block, rate, coef, name, scale):
    return pl.pallas_call(
        functools.partial(local_kernel, scale),
        in_specs=[HBM, VMEM, VMEM],
        out_specs=HBM,
        out_shape=pltpu.HBM((64, 64, 256), F32),
        scratch_shapes=[
            pltpu.VMEM((64, 64, 256), BF16),
            pltpu.VMEM((64, 64, 256), F32),
            pltpu.SemaphoreType.DMA((4,)),
            pltpu.SemaphoreType.DMA((4,)),
        ],
        compiler_params=params(24),
        cost_estimate=pl.CostEstimate(flops=5_000_000_000, bytes_accessed=8_000_000, transcendentals=0),
        name=name,
    )(in_hbm(block), rate, coef)


def small(kernel, name, outs, *operands):
    return pl.pallas_call(
        kernel,
        in_specs=[SMEM] + [VMEM] * (len(operands) - 1),
        out_specs=[VMEM] * len(outs),
        out_shape=[jax.ShapeDtypeStruct(shape, F32) for shape in outs],
        compiler_params=params(8),
        name=name,
    )(*operands)


def act_and_edges(core, local, incoming, vert_rate, vert_coef, horiz_rate):
    edge = pl.BlockSpec((ACT_ROWS // 8, 8, 8, LANES), lambda i: (i, 0, 0, 0))
    return pl.pallas_call(
        act_kernel,
        grid=(64 // ACT_ROWS,),
        in_specs=[SMEM, pl.BlockSpec((ACT_ROWS, 64, 256), lambda i: (i, 0, 0)), VMEM, VMEM, VMEM, VMEM],
        out_specs=[pl.BlockSpec((64, ACT_ROWS, 256), lambda i: (0, i, 0)), edge, edge],
        out_shape=[pltpu.HBM((64, 64, 256), BF16)] + [jax.ShapeDtypeStruct((8, 8, 8, LANES), F32)] * 2,
        scratch_shapes=[
            pltpu.VMEM((2, 8, 8, 8, LANES), F32),
            pltpu.VMEM((2, ACT_ROWS * PITCH, LANES), F32),
        ],
        compiler_params=params(24),
        name="act_and_edges",
    )(core, in_hbm(local), incoming, vert_rate, vert_coef, horiz_rate)


def mix(core, local, keep, got, horiz_rate, horiz_coef, w_in, w_out):
    return pl.pallas_call(
        mix_kernel,
        grid=(64 // MIX_ROWS,),
        in_specs=[SMEM, pl.BlockSpec((64, MIX_ROWS, 256), lambda i: (0, i, 0))] + [VMEM] * 6,
        out_specs=pl.BlockSpec((MIX_ROWS, 64, 256), lambda i: (i, 0, 0)),
        out_shape=jax.ShapeDtypeStruct((64, 64, 256), BF16),
        scratch_shapes=[pltpu.VMEM((1024, 256), F32), pltpu.VMEM((2, 16 * PITCH, LANES), F32)],
        compiler_params=params(40),
        name="mix",
    )(core, in_hbm(local), keep, got, horiz_rate, horiz_coef, w_in, w_out)


def swap(block, bits):
    n = lax.axis_size("col")
    return lax.ppermute(block, "col", [(i, i ^ bits) for i in range(n)])


def together(arrived, local):
    return lax.optimization_barrier((arrived, local))


def on_device(image, vert_rate, vert_coef, horiz_rate, horiz_coef, w_in, w_out):
    rows, cols = lax.axis_size("row"), lax.axis_size("col")
    piece = lax.axis_index("row")
    core = (lax.axis_index("col") % 2).reshape(1)
    rate_along = lax.dynamic_slice_in_dim(horiz_rate, core[0] * LANES, LANES, 1)

    edges = row_edges(image, vert_rate).reshape(rows, 8, 8, LANES)
    edges = lax.all_to_all(edges, "row", 0, 0, tiled=True)
    rate = lax.dynamic_slice_in_dim(vert_rate, (piece // 8) * LANES, LANES, 1)
    local = local_scan(image, vert_rate, vert_coef, "vert_local", 0.5)
    edges, local, core, rate_along = lax.optimization_barrier((edges, local, core, rate_along))
    incoming = prefix(edges, rate, 64.0)
    incoming = lax.all_to_all(incoming, "row", 0, 0, tiled=True).reshape(2, 8, 8, 8, LANES)

    act, edge, other = act_and_edges(core, local, incoming, vert_rate, vert_coef, horiz_rate)

    chips = [[2 * z + c for z in range(cols // 2)] for c in range(2)]
    tile = [(8, 8, 8, LANES)] * 2
    join = functools.partial(join_kernel, 64.0)
    first, joined = small(join, "join_cores", tile, core, edge, swap(other, 1), rate_along)
    joined = lax.all_to_all(joined, "col", 0, 0, tiled=True, axis_index_groups=chips)
    local = local_scan(act, horiz_rate, horiz_coef, "horiz_local", 1.0)
    joined, local = together(joined, local)
    chain = prefix(joined, rate_along, 128.0)
    chain = lax.all_to_all(chain, "col", 0, 0, tiled=True, axis_index_groups=chips)
    part = functools.partial(part_kernel, 64.0)
    keep, send = small(part, "part_cores", tile, core, chain, first, rate_along)
    got = swap(send, 1)

    return mix(core, local, keep, got, horiz_rate, horiz_coef, w_in, w_out)


def solution(mesh):
    placed = (P("row", "col", None), P(), P(), P(), P(), P(), P())
    return jax.shard_map(
        on_device, mesh=mesh, in_specs=placed, out_specs=P("row", "col", None), check_vma=False
    )
```

```python
import functools
import math

import jax
import jax.numpy as jnp
from jax import lax
from jax.experimental import pallas as pl
from jax.experimental.pallas import tpu as pltpu
from jax.sharding import PartitionSpec as P

F32 = jnp.float32
BF16 = jnp.bfloat16
LANES = 128
MODES = 8
SQRT_2_PI = math.sqrt(2.0 / math.pi)
PITCH = 73
ACT_ROWS = 16
MIX_ROWS = 16


def gelu_of_half(x):
    inner = x * (2.0 * SQRT_2_PI + (8.0 * SQRT_2_PI * 0.044715) * (x * x))
    return x + x * jnp.tanh(inner)


def gelu_packed(x):
    x = x.astype(BF16)
    inner = x * (BF16(SQRT_2_PI) + BF16(SQRT_2_PI * 0.044715) * (x * x))
    half = BF16(0.5) * x
    return half + half * jnp.tanh(inner)


def poles(rate_ref, half, rows):
    lanes = slice(half * LANES, (half + 1) * LANES)
    return [
        jnp.broadcast_to(jnp.exp(-rate_ref[m : m + 1, lanes]), (rows, LANES)) for m in range(MODES)
    ]


def weights(rate_ref, coef_ref, half, rows):
    lanes = slice(half * LANES, (half + 1) * LANES)
    return [
        jnp.broadcast_to(
            coef_ref[m : m + 1, lanes] * jnp.sqrt(1.0 - jnp.exp(-2.0 * rate_ref[m : m + 1, lanes])),
            (rows, LANES),
        )
        for m in range(MODES)
    ]


def tree(terms):
    while len(terms) > 1:
        terms = [a + b for a, b in zip(terms[::2], terms[1::2])]
    return terms[0]


def edge_kernel(image_ref, rate_hbm_ref, edge_ref, image, rate_ref, arrived):
    def fetch(i):
        cols = pl.ds(pl.multiple_of(i * 16, 16), 16)
        return pltpu.make_async_copy(image_ref.at[:, cols, :], image.at[:, cols, :], arrived.at[i])

    rates = pltpu.make_async_copy(rate_hbm_ref, rate_ref, arrived.at[4])
    rates.start()
    for i in range(4):
        fetch(i).start()
    rates.wait()

    def chunk(i, _):
        fetch(i).wait()
        cols = pl.ds(pl.multiple_of(i * 16, 16), 16)
        for half in range(2):
            lanes = slice(half * LANES, (half + 1) * LANES)
            pole = poles(rate_ref, half, 16)

            def steps(j, states, lanes=lanes, pole=pole):
                for k in range(16):
                    u = image[j * 16 + k, cols, lanes].astype(F32)
                    states = [p * h + u for p, h in zip(pole, states)]
                return states

            states = lax.fori_loop(0, 4, steps, [jnp.zeros((16, LANES), F32)] * MODES)
            for m in range(MODES):
                edge_ref[half, pl.ds(i * 2, 2), m] = states[m].reshape(2, 8, LANES)
        return 0

    lax.fori_loop(0, 4, chunk, 0)


def prefix_kernel(span, edge_ref, rate_ref, out_ref):
    decay = [
        jnp.broadcast_to(jnp.exp(-span * rate_ref[m : m + 1, :]), (8, LANES)) for m in range(MODES)
    ]
    states = [jnp.zeros((8, LANES), F32)] * MODES
    for r in range(edge_ref.shape[0]):
        for m in range(MODES):
            out_ref[r, m] = states[m]
            states[m] = decay[m] * states[m] + edge_ref[r, m]


def local_kernel(scale, block_ref, rate_hbm_ref, coef_hbm_ref, out_ref, block, result, rate_ref, coef_ref, arrived, left):
    def part(i):
        return pl.ds(pl.multiple_of(i * 16, 16), 16)

    def fetch(i):
        return pltpu.make_async_copy(block_ref.at[:, part(i), :], block.at[:, part(i), :], arrived.at[i])

    def put(i):
        return pltpu.make_async_copy(result.at[:, part(i), :], out_ref.at[:, part(i), :], left.at[i])

    tables = [
        pltpu.make_async_copy(rate_hbm_ref, rate_ref, arrived.at[4]),
        pltpu.make_async_copy(coef_hbm_ref, coef_ref, arrived.at[5]),
    ]
    for table in tables:
        table.start()
    for i in range(4):
        fetch(i).start()
    for table in tables:
        table.wait()

    def chunk(i, _):
        fetch(i).wait()
        for half in range(2):
            lanes = slice(half * LANES, (half + 1) * LANES)
            pole = poles(rate_ref, half, 16)
            weight = [scale * q for q in weights(rate_ref, coef_ref, half, 16)]

            def steps(j, states, lanes=lanes, pole=pole, weight=weight):
                for k in range(16):
                    s = j * 16 + k
                    u = block[s, part(i), lanes].astype(F32)
                    states = [p * h + u for p, h in zip(pole, states)]
                    result[s, part(i), lanes] = tree([q * h for q, h in zip(weight, states)])
                return states

            lax.fori_loop(0, 4, steps, [jnp.zeros((16, LANES), F32)] * MODES)
        put(i).start()
        return 0

    lax.fori_loop(0, 4, chunk, 0)
    for i in range(4):
        put(i).wait()


def decays(rate_ref, span):
    return [jnp.broadcast_to(jnp.exp(-span * rate_ref[m : m + 1, :]), (8, LANES)) for m in range(MODES)]


def join_kernel(span, left_ref, here_ref, keep_ref, came_ref, rate_ref, first_ref, *out_refs):
    left_here, here = left_ref[0] == 0, here_ref[0]
    decay = decays(rate_ref, span)
    part = keep_ref.shape[0] // len(out_refs)
    for b in range(part):
        for k, out_ref in enumerate(out_refs):
            at = b if len(out_refs) == 1 else (here * part if k == 0 else part - here * part) + b
            for m in range(MODES):
                keep, came = keep_ref[at, m], came_ref[at, m]
                first = jnp.where(left_here, keep, came)
                first_ref[at, m] = first
                out_ref[b, m] = decay[m] * first + jnp.where(left_here, came, keep)


def part_kernel(span, left_ref, here_ref, *refs):
    *in_refs, first_ref, rate_ref, keep_ref, send_ref = refs
    left_here, here = left_ref[0] == 0, here_ref[0]
    decay = decays(rate_ref, span)
    part = first_ref.shape[0] // len(in_refs)
    for b in range(part):
        for k, in_ref in enumerate(in_refs):
            at = b if len(in_refs) == 1 else (here * part if k == 0 else part - here * part) + b
            for m in range(MODES):
                chain = in_ref[b, m]
                after = decay[m] * chain + first_ref[at, m]
                keep_ref[at, m] = jnp.where(left_here, chain, after)
                send_ref[at, m] = jnp.where(left_here, after, chain)


def piece_kernel(part, block_ref, rate_ref, coef_ref, *refs):
    out_ref, block, result, arrived, left = refs[-5:]
    rows = pl.ds(part * 16, 16)

    def fetch(half):
        lanes = pl.ds(half * LANES, LANES)
        return pltpu.make_async_copy(block_ref.at[:, rows, lanes], block.at[:, :, lanes], arrived.at[half])

    def put(half):
        lanes = pl.ds(half * LANES, LANES)
        return pltpu.make_async_copy(result.at[:, :, lanes], out_ref.at[:, rows, lanes], left.at[half])

    for half in range(2):
        fetch(half).start()
    for half in range(2):
        lanes = slice(half * LANES, (half + 1) * LANES)
        pole = poles(rate_ref, half, 16)
        weight = weights(rate_ref, coef_ref, half, 16)
        fetch(half).wait()

        def steps(j, states, lanes=lanes, pole=pole, weight=weight):
            for k in range(16):
                s = j * 16 + k
                u = block[s, :, lanes].astype(F32)
                states = [p * h + u for p, h in zip(pole, states)]
                result[s, :, lanes] = tree([q * h for q, h in zip(weight, states)])
            return states

        lax.fori_loop(0, 4, steps, [jnp.zeros((16, LANES), F32)] * MODES)
        put(half).start()
    for half in range(2):
        put(half).wait()


def act_kernel(core_ref, local_ref, in_ref, vr_ref, vc_ref, hr_ref, act_ref, mine_ref, other_ref, tails, field):
    for half in range(2):
        lanes = slice(half * LANES, (half + 1) * LANES)
        pole = poles(vr_ref, half, 16)

        @pl.when(pl.program_id(0) == 0)
        def _(half=half, pole=pole):
            weight = weights(vr_ref, vc_ref, half, 16)
            for m in range(MODES):
                factor = (0.5 * pole[m] * weight[m])[None, :8]
                tails[half, :, m] = in_ref[half, :, m] * factor

        def block(b, _, half=half, lanes=lanes, pole=pole):
            pair = pl.ds(b * 2, 2)
            cols = pl.ds(pl.multiple_of(b * 16, 16), 16)
            tail = [tails[half, pair, m].reshape(16, LANES) for m in range(MODES)]
            for s in range(local_ref.shape[0]):
                y = local_ref[s, cols, lanes] + tree(tail)
                tail = [p * g for p, g in zip(pole, tail)]
                a = gelu_of_half(y).astype(BF16).astype(F32)
                field[half, pl.ds(s * PITCH + b * 16, 16), :] = a
            for m in range(MODES):
                tails[half, pair, m] = tail[m].reshape(2, 8, LANES)
            return 0

        lax.fori_loop(0, 4, block, 0)

    for half in range(2):
        lanes = slice(half * LANES, (half + 1) * LANES)
        pole = poles(hr_ref, half, 16)
        mine = core_ref[0] == half
        for r in range(0, local_ref.shape[0], 16):

            def steps(i, states, half=half, lanes=lanes, pole=pole, r=r):
                for k in range(16):
                    w = i * 16 + k
                    u = field[half, pl.ds(w + r * PITCH, 16, stride=PITCH), :]
                    act_ref[w, r : r + 16, lanes] = u.astype(BF16)
                    states = [p * h + u for p, h in zip(pole, states)]
                return states

            states = lax.fori_loop(0, 4, steps, [jnp.zeros((16, LANES), F32)] * MODES)

            @pl.when(mine)
            def _(states=states, r=r):
                for m in range(MODES):
                    mine_ref[r // 8 : r // 8 + 2, m] = states[m].reshape(2, 8, LANES)

            @pl.when(jnp.logical_not(mine))
            def _(states=states, r=r):
                for m in range(MODES):
                    other_ref[r // 8 : r // 8 + 2, m] = states[m].reshape(2, 8, LANES)


def mix_kernel(core_ref, local_ref, keep_ref, got_ref, hr_ref, hc_ref, w_in_ref, w_out_ref, out_ref, horiz, mixed):
    core = core_ref[0]
    rows = local_ref.shape[1]
    for r in range(0, rows, 16):
        pair = pl.ds(pl.program_id(0) * (rows // 8) + r // 8, 2)
        for half in range(2):
            lanes = slice(half * LANES, (half + 1) * LANES)
            pole = poles(hr_ref, half, 16)
            weight = weights(hr_ref, hc_ref, half, 16)
            mine = core == half
            tail = [
                jnp.where(mine, keep_ref[pair, m], got_ref[pair, m]).reshape(16, LANES)
                * (pole[m] * weight[m])
                for m in range(MODES)
            ]

            def steps(i, tail, lanes=lanes, pole=pole, r=r):
                for k in range(8):
                    w = i * 8 + k
                    y = local_ref[w, r : r + 16, lanes] + tree(tail)
                    tail = [p * g for p, g in zip(pole, tail)]
                    horiz[pl.ds(pl.multiple_of(w * 16, 16), 16), lanes] = y
                return tail

            lax.fori_loop(0, 8, steps, tail)

        y = horiz[...]
        scale = lax.rsqrt(jnp.mean(y * y, axis=-1, keepdims=True) + 1e-06)
        normed = (y * scale).astype(BF16)
        hidden = gelu_packed(jnp.dot(normed, w_in_ref[...], preferred_element_type=F32))
        out = y + jnp.dot(hidden, w_out_ref[...], preferred_element_type=F32)
        for w in range(64):
            for half in range(2):
                lanes = slice(half * LANES, (half + 1) * LANES)
                mixed[half, pl.ds(w, 16, stride=PITCH), :] = out[w * 16 : (w + 1) * 16, lanes]
        for half in range(2):
            lanes = slice(half * LANES, (half + 1) * LANES)
            for h in range(16):
                out_ref[r + h, :, lanes] = mixed[half, h * PITCH : h * PITCH + 64].astype(BF16)


def in_hbm(block):
    return pltpu.with_memory_space_constraint(block, pltpu.HBM)


def whole(shape):
    return pl.BlockSpec(shape, lambda i: (0,) * len(shape))


def params(mib):
    return pltpu.CompilerParams(vmem_limit_bytes=mib * 1024 * 1024)


VMEM = pl.BlockSpec(memory_space=pltpu.VMEM)
HBM = pl.BlockSpec(memory_space=pltpu.HBM)
SMEM = pl.BlockSpec(memory_space=pltpu.SMEM)


def row_edges(image, rate):
    return pl.pallas_call(
        edge_kernel,
        in_specs=[HBM, HBM],
        out_specs=VMEM,
        out_shape=jax.ShapeDtypeStruct((2, 8, 8, 8, LANES), F32),
        scratch_shapes=[
            pltpu.VMEM((64, 64, 256), BF16),
            pltpu.VMEM((8, 256), F32),
            pltpu.SemaphoreType.DMA((5,)),
        ],
        compiler_params=params(24),
        name="row_edges",
    )(in_hbm(image), in_hbm(rate))


def prefix(edges, rate, span):
    def kernel(edge_ref, rate_ref, out_ref):
        prefix_kernel(span, edge_ref, rate_ref, out_ref)

    return pl.pallas_call(
        kernel,
        out_shape=jax.ShapeDtypeStruct(edges.shape, F32),
        compiler_params=params(8),
        name="prefix",
    )(edges, rate)


def local_scan(block, rate, coef, name, scale):
    return pl.pallas_call(
        functools.partial(local_kernel, scale),
        in_specs=[HBM, HBM, HBM],
        out_specs=HBM,
        out_shape=pltpu.HBM((64, 64, 256), F32),
        scratch_shapes=[
            pltpu.VMEM((64, 64, 256), BF16),
            pltpu.VMEM((64, 64, 256), F32),
            pltpu.VMEM((8, 256), F32),
            pltpu.VMEM((8, 256), F32),
            pltpu.SemaphoreType.DMA((6,)),
            pltpu.SemaphoreType.DMA((4,)),
        ],
        compiler_params=params(24),
        cost_estimate=pl.CostEstimate(flops=5_000_000_000, bytes_accessed=8_000_000, transcendentals=0),
        name=name,
    )(in_hbm(block), in_hbm(rate), in_hbm(coef))


def local_piece(block, rate, coef, part, into):
    more = [] if into is None else [in_hbm(into)]
    return pl.pallas_call(
        functools.partial(piece_kernel, part),
        in_specs=[HBM, VMEM, VMEM] + [HBM] * len(more),
        out_specs=HBM,
        out_shape=pltpu.HBM((64, 64, 256), F32),
        input_output_aliases={3: 0} if more else {},
        scratch_shapes=[
            pltpu.VMEM((64, 16, 256), BF16),
            pltpu.VMEM((64, 16, 256), F32),
            pltpu.SemaphoreType.DMA((2,)),
            pltpu.SemaphoreType.DMA((2,)),
        ],
        compiler_params=params(8),
        cost_estimate=pl.CostEstimate(flops=1_250_000_000, bytes_accessed=2_000_000, transcendentals=0),
        name=f"horiz_local_{part}",
    )(in_hbm(block), rate, coef, *more)


def small(kernel, name, outs, *operands):
    return pl.pallas_call(
        kernel,
        in_specs=[SMEM] * 2 + [VMEM] * (len(operands) - 2),
        out_specs=[VMEM] * len(outs),
        out_shape=[jax.ShapeDtypeStruct(shape, F32) for shape in outs],
        compiler_params=params(8),
        name=name,
    )(*operands)


def act_and_edges(core, local, incoming, vert_rate, vert_coef, horiz_rate):
    edge = pl.BlockSpec((ACT_ROWS // 8, 8, 8, LANES), lambda i: (i, 0, 0, 0))
    return pl.pallas_call(
        act_kernel,
        grid=(64 // ACT_ROWS,),
        in_specs=[SMEM, pl.BlockSpec((ACT_ROWS, 64, 256), lambda i: (i, 0, 0)), VMEM, VMEM, VMEM, VMEM],
        out_specs=[pl.BlockSpec((64, ACT_ROWS, 256), lambda i: (0, i, 0)), edge, edge],
        out_shape=[pltpu.HBM((64, 64, 256), BF16)] + [jax.ShapeDtypeStruct((8, 8, 8, LANES), F32)] * 2,
        scratch_shapes=[
            pltpu.VMEM((2, 8, 8, 8, LANES), F32),
            pltpu.VMEM((2, ACT_ROWS * PITCH, LANES), F32),
        ],
        compiler_params=params(24),
        name="act_and_edges",
    )(core, in_hbm(local), incoming, vert_rate, vert_coef, horiz_rate)


def mix(core, local, keep, got, horiz_rate, horiz_coef, w_in, w_out):
    return pl.pallas_call(
        mix_kernel,
        grid=(64 // MIX_ROWS,),
        in_specs=[SMEM, pl.BlockSpec((64, MIX_ROWS, 256), lambda i: (0, i, 0))] + [VMEM] * 6,
        out_specs=pl.BlockSpec((MIX_ROWS, 64, 256), lambda i: (i, 0, 0)),
        out_shape=jax.ShapeDtypeStruct((64, 64, 256), BF16),
        scratch_shapes=[pltpu.VMEM((1024, 256), F32), pltpu.VMEM((2, 16 * PITCH, LANES), F32)],
        compiler_params=params(40),
        name="mix",
    )(core, in_hbm(local), keep, got, horiz_rate, horiz_coef, w_in, w_out)


def swap(block, bits):
    n = lax.axis_size("col")
    return lax.ppermute(block, "col", [(i, i ^ bits) for i in range(n)])


def together(arrived, local):
    return lax.optimization_barrier((arrived, local))


def on_device(image, vert_rate, vert_coef, horiz_rate, horiz_coef, w_in, w_out):
    rows, cols = lax.axis_size("row"), lax.axis_size("col")
    piece = lax.axis_index("row")
    col = lax.axis_index("col").reshape(1)
    core, chip = col % 2, col // 2
    side = [core, chip % 2, chip // 2 % 2]
    upper = chip // 4
    here = [side[1] ^ upper, side[2] ^ upper, upper]
    rate_along = lax.dynamic_slice_in_dim(horiz_rate, core[0] * LANES, LANES, 1)

    edges = row_edges(image, vert_rate).reshape(rows, 8, 8, LANES)
    edges = lax.all_to_all(edges, "row", 0, 0, tiled=True)
    rate = lax.dynamic_slice_in_dim(vert_rate, (piece // 8) * LANES, LANES, 1)
    local = local_scan(image, vert_rate, vert_coef, "vert_local", 0.5)
    edges, local, side, here, rate_along = lax.optimization_barrier((edges, local, side, here, rate_along))
    incoming = prefix(edges, rate, 64.0)
    incoming = lax.all_to_all(incoming, "row", 0, 0, tiled=True).reshape(2, 8, 8, 8, LANES)

    act, mine, other = act_and_edges(side[0], local, incoming, vert_rate, vert_coef, horiz_rate)

    eight, four, two = (8, 8, 8, LANES), (4, 8, 8, LANES), (2, 8, 8, LANES)

    def horiz(part, into):
        return local_piece(act, horiz_rate, horiz_coef, part, into)

    def join(level, outs, keep, came):
        kernel = functools.partial(join_kernel, 64.0 * 2**level)
        return small(kernel, f"join_{level}", outs, side[level], here[level], keep, came, rate_along)

    def part(level, shape, chains, first):
        kernel = functools.partial(part_kernel, 64.0 * 2**level)
        return small(kernel, f"part_{level}", [shape] * 2, side[level], here[level], *chains, first, rate_along)

    first_tile, keep, send = join(0, [eight, four, four], mine, swap(other, 1))
    came, local = together(swap(send, 2), horiz(0, None))
    first_chip, keep, send = join(1, [four, two, two], keep, came)
    came, local = together(swap(send, 4), horiz(1, local))
    first_pair, group = join(2, [two, two], keep, came)
    chain = lax.ppermute(group, "col", [(i, i ^ (cols - 2)) for i in range(cols // 2)])
    chain, local = together(chain, horiz(2, local))
    keep, send = part(2, two, [chain], first_pair)
    came, local = together(swap(send, 4), horiz(3, local))
    keep, send = part(1, four, [keep, came], first_chip)
    keep, send = part(0, eight, [keep, swap(send, 2)], first_tile)
    got = swap(send, 1)

    return mix(side[0], local, keep, got, horiz_rate, horiz_coef, w_in, w_out)


def solution(mesh):
    placed = (P("row", "col", None), P(), P(), P(), P(), P(), P())
    return jax.shard_map(
        on_device, mesh=mesh, in_specs=placed, out_specs=P("row", "col", None), check_vma=False
    )
```

```python
import functools
import math

import jax
import jax.numpy as jnp
from jax import lax
from jax.experimental import pallas as pl
from jax.experimental.pallas import tpu as pltpu
from jax.sharding import PartitionSpec as P

F32 = jnp.float32
BF16 = jnp.bfloat16
LANES = 128
MODES = 8
SQRT_2_PI = math.sqrt(2.0 / math.pi)
PITCH = 73
ACT_ROWS = 16
MIX_ROWS = 16


def gelu_of_half(x):
    inner = x * (2.0 * SQRT_2_PI + (8.0 * SQRT_2_PI * 0.044715) * (x * x))
    return x + x * jnp.tanh(inner)


def gelu_packed(x):
    x = x.astype(BF16)
    inner = x * (BF16(SQRT_2_PI) + BF16(SQRT_2_PI * 0.044715) * (x * x))
    half = BF16(0.5) * x
    return half + half * jnp.tanh(inner)


def poles(rate_ref, half, rows):
    lanes = slice(half * LANES, (half + 1) * LANES)
    return [
        jnp.broadcast_to(jnp.exp(-rate_ref[m : m + 1, lanes]), (rows, LANES)) for m in range(MODES)
    ]


def weights(rate_ref, coef_ref, half, rows):
    lanes = slice(half * LANES, (half + 1) * LANES)
    return [
        jnp.broadcast_to(
            coef_ref[m : m + 1, lanes] * jnp.sqrt(1.0 - jnp.exp(-2.0 * rate_ref[m : m + 1, lanes])),
            (rows, LANES),
        )
        for m in range(MODES)
    ]


def tree(terms):
    while len(terms) > 1:
        terms = [a + b for a, b in zip(terms[::2], terms[1::2])]
    return terms[0]


def edge_kernel(image_ref, rate_hbm_ref, edge_ref, image, rate_ref, arrived):
    def fetch(i):
        cols = pl.ds(pl.multiple_of(i * 16, 16), 16)
        return pltpu.make_async_copy(image_ref.at[:, cols, :], image.at[:, cols, :], arrived.at[i])

    rates = pltpu.make_async_copy(rate_hbm_ref, rate_ref, arrived.at[4])
    rates.start()
    for i in range(4):
        fetch(i).start()
    rates.wait()

    def chunk(i, _):
        fetch(i).wait()
        cols = pl.ds(pl.multiple_of(i * 16, 16), 16)
        for half in range(2):
            lanes = slice(half * LANES, (half + 1) * LANES)
            pole = poles(rate_ref, half, 16)

            def steps(j, states, lanes=lanes, pole=pole):
                for k in range(16):
                    u = image[j * 16 + k, cols, lanes].astype(F32)
                    states = [p * h + u for p, h in zip(pole, states)]
                return states

            states = lax.fori_loop(0, 4, steps, [jnp.zeros((16, LANES), F32)] * MODES)
            for m in range(MODES):
                edge_ref[half, pl.ds(i * 2, 2), m] = states[m].reshape(2, 8, LANES)
        return 0

    lax.fori_loop(0, 4, chunk, 0)


def prefix_kernel(span, half_ref, edge_ref, rate_ref, out_ref):
    decay = decays(rate_ref, half_ref, span)
    states = [jnp.zeros((8, LANES), F32)] * MODES
    for r in range(edge_ref.shape[0]):
        for m in range(MODES):
            out_ref[r, m] = states[m]
            states[m] = decay[m] * states[m] + edge_ref[r, m]


def local_kernel(scale, block_ref, rate_hbm_ref, coef_hbm_ref, out_ref, block, result, rate_ref, coef_ref, arrived, left):
    def part(i):
        return pl.ds(pl.multiple_of(i * 16, 16), 16)

    def fetch(i):
        return pltpu.make_async_copy(block_ref.at[:, part(i), :], block.at[:, part(i), :], arrived.at[i])

    def put(i):
        return pltpu.make_async_copy(result.at[:, part(i), :], out_ref.at[:, part(i), :], left.at[i])

    tables = [
        pltpu.make_async_copy(rate_hbm_ref, rate_ref, arrived.at[4]),
        pltpu.make_async_copy(coef_hbm_ref, coef_ref, arrived.at[5]),
    ]
    for table in tables:
        table.start()
    for i in range(4):
        fetch(i).start()
    for table in tables:
        table.wait()

    def chunk(i, _):
        fetch(i).wait()
        for half in range(2):
            lanes = slice(half * LANES, (half + 1) * LANES)
            pole = poles(rate_ref, half, 16)
            weight = [scale * q for q in weights(rate_ref, coef_ref, half, 16)]

            def steps(j, states, lanes=lanes, pole=pole, weight=weight):
                for k in range(16):
                    s = j * 16 + k
                    u = block[s, part(i), lanes].astype(F32)
                    states = [p * h + u for p, h in zip(pole, states)]
                    result[s, part(i), lanes] = tree([q * h for q, h in zip(weight, states)])
                return states

            lax.fori_loop(0, 4, steps, [jnp.zeros((16, LANES), F32)] * MODES)
        put(i).start()
        return 0

    lax.fori_loop(0, 4, chunk, 0)
    for i in range(4):
        put(i).wait()


def decays(rate_ref, half_ref, span):
    lanes = pl.ds(pl.multiple_of(half_ref[0] * LANES, LANES), LANES)
    return [jnp.broadcast_to(jnp.exp(-span * rate_ref[m : m + 1, lanes]), (8, LANES)) for m in range(MODES)]


def join_kernel(span, half_ref, left_ref, here_ref, keep_ref, came_ref, rate_ref, first_ref, *out_refs):
    left_here, here = left_ref[0] == 0, here_ref[0]
    decay = decays(rate_ref, half_ref, span)
    part = keep_ref.shape[0] // len(out_refs)
    for b in range(part):
        for k, out_ref in enumerate(out_refs):
            at = b if len(out_refs) == 1 else (here * part if k == 0 else part - here * part) + b
            for m in range(MODES):
                keep, came = keep_ref[at, m], came_ref[at, m]
                first = jnp.where(left_here, keep, came)
                first_ref[at, m] = first
                out_ref[b, m] = decay[m] * first + jnp.where(left_here, came, keep)


def part_kernel(span, half_ref, left_ref, here_ref, *refs):
    *in_refs, first_ref, rate_ref, keep_ref, send_ref = refs
    left_here, here = left_ref[0] == 0, here_ref[0]
    decay = decays(rate_ref, half_ref, span)
    part = first_ref.shape[0] // len(in_refs)
    for b in range(part):
        for k, in_ref in enumerate(in_refs):
            at = b if len(in_refs) == 1 else (here * part if k == 0 else part - here * part) + b
            for m in range(MODES):
                chain = in_ref[b, m]
                if len(in_refs) == 1:
                    chain = jnp.where(here == 1, chain, 0.0)
                after = decay[m] * chain + first_ref[at, m]
                keep_ref[at, m] = jnp.where(left_here, chain, after)
                send_ref[at, m] = jnp.where(left_here, after, chain)


def piece_kernel(part, block_ref, rate_ref, coef_ref, *refs):
    out_ref, block, result, arrived, left = refs[-5:]
    rows = pl.ds(part * 16, 16)

    def fetch(half):
        lanes = pl.ds(half * LANES, LANES)
        return pltpu.make_async_copy(block_ref.at[:, rows, lanes], block.at[:, :, lanes], arrived.at[half])

    def put(half):
        lanes = pl.ds(half * LANES, LANES)
        return pltpu.make_async_copy(result.at[:, :, lanes], out_ref.at[:, rows, lanes], left.at[half])

    for half in range(2):
        fetch(half).start()
    for half in range(2):
        lanes = slice(half * LANES, (half + 1) * LANES)
        pole = poles(rate_ref, half, 16)
        weight = weights(rate_ref, coef_ref, half, 16)
        fetch(half).wait()

        def steps(j, states, lanes=lanes, pole=pole, weight=weight):
            for k in range(16):
                s = j * 16 + k
                u = block[s, :, lanes].astype(F32)
                states = [p * h + u for p, h in zip(pole, states)]
                result[s, :, lanes] = tree([q * h for q, h in zip(weight, states)])
            return states

        lax.fori_loop(0, 4, steps, [jnp.zeros((16, LANES), F32)] * MODES)
        put(half).start()
    for half in range(2):
        put(half).wait()


def act_kernel(core_ref, local_ref, in_ref, vr_ref, vc_ref, hr_ref, act_ref, mine_ref, other_ref, tails, field):
    for half in range(2):
        lanes = slice(half * LANES, (half + 1) * LANES)
        pole = poles(vr_ref, half, 16)

        @pl.when(pl.program_id(0) == 0)
        def _(half=half, pole=pole):
            weight = weights(vr_ref, vc_ref, half, 16)
            for m in range(MODES):
                factor = (0.5 * pole[m] * weight[m])[None, :8]
                tails[half, :, m] = in_ref[half, :, m] * factor

        def block(b, _, half=half, lanes=lanes, pole=pole):
            pair = pl.ds(b * 2, 2)
            cols = pl.ds(pl.multiple_of(b * 16, 16), 16)
            tail = [tails[half, pair, m].reshape(16, LANES) for m in range(MODES)]
            for s in range(local_ref.shape[0]):
                y = local_ref[s, cols, lanes] + tree(tail)
                tail = [p * g for p, g in zip(pole, tail)]
                a = gelu_of_half(y).astype(BF16).astype(F32)
                field[half, pl.ds(s * PITCH + b * 16, 16), :] = a
            for m in range(MODES):
                tails[half, pair, m] = tail[m].reshape(2, 8, LANES)
            return 0

        lax.fori_loop(0, 4, block, 0)

    for half in range(2):
        lanes = slice(half * LANES, (half + 1) * LANES)
        pole = poles(hr_ref, half, 16)
        mine = core_ref[0] == half
        for r in range(0, local_ref.shape[0], 16):

            def steps(i, states, half=half, lanes=lanes, pole=pole, r=r):
                for k in range(16):
                    w = i * 16 + k
                    u = field[half, pl.ds(w + r * PITCH, 16, stride=PITCH), :]
                    act_ref[w, r : r + 16, lanes] = u.astype(BF16)
                    states = [p * h + u for p, h in zip(pole, states)]
                return states

            states = lax.fori_loop(0, 4, steps, [jnp.zeros((16, LANES), F32)] * MODES)

            @pl.when(mine)
            def _(states=states, r=r):
                for m in range(MODES):
                    mine_ref[r // 8 : r // 8 + 2, m] = states[m].reshape(2, 8, LANES)

            @pl.when(jnp.logical_not(mine))
            def _(states=states, r=r):
                for m in range(MODES):
                    other_ref[r // 8 : r // 8 + 2, m] = states[m].reshape(2, 8, LANES)


def mix_kernel(core_ref, local_ref, keep_ref, got_ref, hr_ref, hc_ref, w_in_ref, w_out_ref, out_ref, horiz, mixed):
    core = core_ref[0]
    rows = local_ref.shape[1]
    for r in range(0, rows, 16):
        pair = pl.ds(pl.program_id(0) * (rows // 8) + r // 8, 2)
        for half in range(2):
            lanes = slice(half * LANES, (half + 1) * LANES)
            pole = poles(hr_ref, half, 16)
            weight = weights(hr_ref, hc_ref, half, 16)
            mine = core == half
            tail = [
                jnp.where(mine, keep_ref[pair, m], got_ref[pair, m]).reshape(16, LANES)
                * (pole[m] * weight[m])
                for m in range(MODES)
            ]

            def steps(i, tail, lanes=lanes, pole=pole, r=r):
                for k in range(8):
                    w = i * 8 + k
                    y = local_ref[w, r : r + 16, lanes] + tree(tail)
                    tail = [p * g for p, g in zip(pole, tail)]
                    horiz[pl.ds(pl.multiple_of(w * 16, 16), 16), lanes] = y
                return tail

            lax.fori_loop(0, 8, steps, tail)

        y = horiz[...]
        scale = lax.rsqrt(jnp.mean(y * y, axis=-1, keepdims=True) + 1e-06)
        normed = (y * scale).astype(BF16)
        hidden = gelu_packed(jnp.dot(normed, w_in_ref[...], preferred_element_type=F32))
        out = y + jnp.dot(hidden, w_out_ref[...], preferred_element_type=F32)
        for w in range(64):
            for half in range(2):
                lanes = slice(half * LANES, (half + 1) * LANES)
                mixed[half, pl.ds(w, 16, stride=PITCH), :] = out[w * 16 : (w + 1) * 16, lanes]
        for half in range(2):
            lanes = slice(half * LANES, (half + 1) * LANES)
            for h in range(16):
                out_ref[r + h, :, lanes] = mixed[half, h * PITCH : h * PITCH + 64].astype(BF16)


def in_hbm(block):
    return pltpu.with_memory_space_constraint(block, pltpu.HBM)


def whole(shape):
    return pl.BlockSpec(shape, lambda i: (0,) * len(shape))


def params(mib):
    return pltpu.CompilerParams(vmem_limit_bytes=mib * 1024 * 1024)


VMEM = pl.BlockSpec(memory_space=pltpu.VMEM)
HBM = pl.BlockSpec(memory_space=pltpu.HBM)
SMEM = pl.BlockSpec(memory_space=pltpu.SMEM)


def row_edges(image, rate):
    return pl.pallas_call(
        edge_kernel,
        in_specs=[HBM, HBM],
        out_specs=VMEM,
        out_shape=jax.ShapeDtypeStruct((2, 8, 8, 8, LANES), F32),
        scratch_shapes=[
            pltpu.VMEM((64, 64, 256), BF16),
            pltpu.VMEM((8, 256), F32),
            pltpu.SemaphoreType.DMA((5,)),
        ],
        compiler_params=params(24),
        name="row_edges",
    )(in_hbm(image), in_hbm(rate))


def prefix(half, edges, rate, span):
    return pl.pallas_call(
        functools.partial(prefix_kernel, span),
        in_specs=[SMEM, VMEM, VMEM],
        out_specs=VMEM,
        out_shape=jax.ShapeDtypeStruct(edges.shape, F32),
        compiler_params=params(8),
        name="prefix",
    )(half, edges, rate)


def local_scan(block, rate, coef, name, scale):
    return pl.pallas_call(
        functools.partial(local_kernel, scale),
        in_specs=[HBM, HBM, HBM],
        out_specs=HBM,
        out_shape=pltpu.HBM((64, 64, 256), F32),
        scratch_shapes=[
            pltpu.VMEM((64, 64, 256), BF16),
            pltpu.VMEM((64, 64, 256), F32),
            pltpu.VMEM((8, 256), F32),
            pltpu.VMEM((8, 256), F32),
            pltpu.SemaphoreType.DMA((6,)),
            pltpu.SemaphoreType.DMA((4,)),
        ],
        compiler_params=params(24),
        cost_estimate=pl.CostEstimate(flops=5_000_000_000, bytes_accessed=8_000_000, transcendentals=0),
        name=name,
    )(in_hbm(block), in_hbm(rate), in_hbm(coef))


def local_piece(block, rate, coef, part, into):
    more = [] if into is None else [in_hbm(into)]
    return pl.pallas_call(
        functools.partial(piece_kernel, part),
        in_specs=[HBM, VMEM, VMEM] + [HBM] * len(more),
        out_specs=HBM,
        out_shape=pltpu.HBM((64, 64, 256), F32),
        input_output_aliases={3: 0} if more else {},
        scratch_shapes=[
            pltpu.VMEM((64, 16, 256), BF16),
            pltpu.VMEM((64, 16, 256), F32),
            pltpu.SemaphoreType.DMA((2,)),
            pltpu.SemaphoreType.DMA((2,)),
        ],
        compiler_params=params(8),
        cost_estimate=pl.CostEstimate(flops=1_250_000_000, bytes_accessed=2_000_000, transcendentals=0),
        name=f"horiz_local_{part}",
    )(in_hbm(block), rate, coef, *more)


def small(kernel, name, outs, *operands):
    return pl.pallas_call(
        kernel,
        in_specs=[SMEM] * 3 + [VMEM] * (len(operands) - 3),
        out_specs=[VMEM] * len(outs),
        out_shape=[jax.ShapeDtypeStruct(shape, F32) for shape in outs],
        compiler_params=params(8),
        name=name,
    )(*operands)


def act_and_edges(core, local, incoming, vert_rate, vert_coef, horiz_rate):
    edge = pl.BlockSpec((ACT_ROWS // 8, 8, 8, LANES), lambda i: (i, 0, 0, 0))
    return pl.pallas_call(
        act_kernel,
        grid=(64 // ACT_ROWS,),
        in_specs=[SMEM, pl.BlockSpec((ACT_ROWS, 64, 256), lambda i: (i, 0, 0)), VMEM, VMEM, VMEM, VMEM],
        out_specs=[pl.BlockSpec((64, ACT_ROWS, 256), lambda i: (0, i, 0)), edge, edge],
        out_shape=[pltpu.HBM((64, 64, 256), BF16)] + [jax.ShapeDtypeStruct((8, 8, 8, LANES), F32)] * 2,
        scratch_shapes=[
            pltpu.VMEM((2, 8, 8, 8, LANES), F32),
            pltpu.VMEM((2, ACT_ROWS * PITCH, LANES), F32),
        ],
        compiler_params=params(24),
        name="act_and_edges",
    )(core, in_hbm(local), incoming, vert_rate, vert_coef, horiz_rate)


def mix(core, local, keep, got, horiz_rate, horiz_coef, w_in, w_out):
    return pl.pallas_call(
        mix_kernel,
        grid=(64 // MIX_ROWS,),
        in_specs=[SMEM, pl.BlockSpec((64, MIX_ROWS, 256), lambda i: (0, i, 0))] + [VMEM] * 6,
        out_specs=pl.BlockSpec((MIX_ROWS, 64, 256), lambda i: (i, 0, 0)),
        out_shape=jax.ShapeDtypeStruct((64, 64, 256), BF16),
        scratch_shapes=[pltpu.VMEM((1024, 256), F32), pltpu.VMEM((2, 16 * PITCH, LANES), F32)],
        compiler_params=params(40),
        name="mix",
    )(core, in_hbm(local), keep, got, horiz_rate, horiz_coef, w_in, w_out)


def swap(block, bits):
    n = lax.axis_size("col")
    return lax.ppermute(block, "col", [(i, i ^ bits) for i in range(n)])


def together(arrived, local):
    return lax.optimization_barrier((arrived, local))


def on_device(image, vert_rate, vert_coef, horiz_rate, horiz_coef, w_in, w_out):
    rows, cols = lax.axis_size("row"), lax.axis_size("col")
    piece_half = (lax.axis_index("row") // (rows // 2)).reshape(1)
    col = lax.axis_index("col").reshape(1)
    core, chip = col % 2, col // 2
    side = [core, chip % 2, chip // 2 % 2]
    upper = chip // 4
    here = [side[1] ^ upper, side[2] ^ upper, upper]

    edges = row_edges(image, vert_rate).reshape(rows, 8, 8, LANES)
    edges = lax.all_to_all(edges, "row", 0, 0, tiled=True)
    local = local_scan(image, vert_rate, vert_coef, "vert_local", 0.5)
    edges, local, side, here = lax.optimization_barrier((edges, local, side, here))
    core = side[0]
    incoming = prefix(piece_half, edges, vert_rate, 64.0)
    incoming = lax.all_to_all(incoming, "row", 0, 0, tiled=True).reshape(2, 8, 8, 8, LANES)

    act, mine, other = act_and_edges(core, local, incoming, vert_rate, vert_coef, horiz_rate)

    eight, four, two = (8, 8, 8, LANES), (4, 8, 8, LANES), (2, 8, 8, LANES)

    def horiz(part, into):
        return local_piece(act, horiz_rate, horiz_coef, part, into)

    def join(level, outs, keep, came):
        kernel = functools.partial(join_kernel, 64.0 * 2**level)
        return small(kernel, f"join_{level}", outs, core, side[level], here[level], keep, came, horiz_rate)

    def part(level, shape, chains, first):
        kernel = functools.partial(part_kernel, 64.0 * 2**level)
        return small(kernel, f"part_{level}", [shape] * 2, core, side[level], here[level], *chains, first, horiz_rate)

    first_tile, keep, send = join(0, [eight, four, four], mine, swap(other, 1))
    came, local = together(swap(send, 2), horiz(0, None))
    first_chip, keep, send = join(1, [four, two, two], keep, came)
    came, local = together(swap(send, 4), horiz(1, local))
    first_pair, group = join(2, [two, two], keep, came)
    chain, local = together(swap(group, cols - 2), horiz(2, local))
    keep, send = part(2, two, [chain], first_pair)
    came, local = together(swap(send, 4), horiz(3, local))
    keep, send = part(1, four, [keep, came], first_chip)
    keep, send = part(0, eight, [keep, swap(send, 2)], first_tile)
    got = swap(send, 1)

    return mix(core, local, keep, got, horiz_rate, horiz_coef, w_in, w_out)


def solution(mesh):
    placed = (P("row", "col", None), P(), P(), P(), P(), P(), P())
    return jax.shard_map(
        on_device, mesh=mesh, in_specs=placed, out_specs=P("row", "col", None), check_vma=False
    )
```

```python
import functools
import math

import jax
import jax.numpy as jnp
from jax import lax
from jax.experimental import pallas as pl
from jax.experimental.pallas import tpu as pltpu
from jax.sharding import PartitionSpec as P

F32 = jnp.float32
BF16 = jnp.bfloat16
LANES = 128
MODES = 8
SQRT_2_PI = math.sqrt(2.0 / math.pi)
PITCH = 73
ACT_ROWS = 16
MIX_ROWS = 16


def gelu_of_half(x):
    inner = x * (2.0 * SQRT_2_PI + (8.0 * SQRT_2_PI * 0.044715) * (x * x))
    return x + x * jnp.tanh(inner)


def gelu_packed(x):
    x = x.astype(BF16)
    inner = x * (BF16(SQRT_2_PI) + BF16(SQRT_2_PI * 0.044715) * (x * x))
    half = BF16(0.5) * x
    return half + half * jnp.tanh(inner)


def poles(rate_ref, half, rows):
    lanes = slice(half * LANES, (half + 1) * LANES)
    return [
        jnp.broadcast_to(jnp.exp(-rate_ref[m : m + 1, lanes]), (rows, LANES)) for m in range(MODES)
    ]


def weights(rate_ref, coef_ref, half, rows):
    lanes = slice(half * LANES, (half + 1) * LANES)
    return [
        jnp.broadcast_to(
            coef_ref[m : m + 1, lanes] * jnp.sqrt(1.0 - jnp.exp(-2.0 * rate_ref[m : m + 1, lanes])),
            (rows, LANES),
        )
        for m in range(MODES)
    ]


def tree(terms):
    while len(terms) > 1:
        terms = [a + b for a, b in zip(terms[::2], terms[1::2])]
    return terms[0]


def edge_kernel(image_ref, rate_hbm_ref, edge_ref, image, rate_ref, arrived):
    def fetch(i):
        cols = pl.ds(pl.multiple_of(i * 16, 16), 16)
        return pltpu.make_async_copy(image_ref.at[:, cols, :], image.at[:, cols, :], arrived.at[i])

    rates = pltpu.make_async_copy(rate_hbm_ref, rate_ref, arrived.at[4])
    rates.start()
    for i in range(4):
        fetch(i).start()
    rates.wait()

    def chunk(i, _):
        fetch(i).wait()
        cols = pl.ds(pl.multiple_of(i * 16, 16), 16)
        for half in range(2):
            lanes = slice(half * LANES, (half + 1) * LANES)
            pole = poles(rate_ref, half, 16)

            def steps(j, states, lanes=lanes, pole=pole):
                for k in range(16):
                    u = image[j * 16 + k, cols, lanes].astype(F32)
                    states = [p * h + u for p, h in zip(pole, states)]
                return states

            states = lax.fori_loop(0, 4, steps, [jnp.zeros((16, LANES), F32)] * MODES)
            for m in range(MODES):
                edge_ref[half, pl.ds(i * 2, 2), m] = states[m].reshape(2, 8, LANES)
        return 0

    lax.fori_loop(0, 4, chunk, 0)


def prefix_kernel(span, half_ref, edge_ref, rate_ref, out_ref):
    decay = decays(rate_ref, half_ref, span)
    states = [jnp.zeros((8, LANES), F32)] * MODES
    for r in range(edge_ref.shape[0]):
        for m in range(MODES):
            out_ref[r, m] = states[m]
            states[m] = decay[m] * states[m] + edge_ref[r, m]


def local_kernel(scale, block_ref, rate_hbm_ref, coef_hbm_ref, out_ref, block, result, rate_ref, coef_ref, arrived, left):
    def part(i):
        return pl.ds(pl.multiple_of(i * 16, 16), 16)

    def fetch(i):
        return pltpu.make_async_copy(block_ref.at[:, part(i), :], block.at[:, part(i), :], arrived.at[i])

    def put(i):
        return pltpu.make_async_copy(result.at[:, part(i), :], out_ref.at[:, part(i), :], left.at[i])

    tables = [
        pltpu.make_async_copy(rate_hbm_ref, rate_ref, arrived.at[4]),
        pltpu.make_async_copy(coef_hbm_ref, coef_ref, arrived.at[5]),
    ]
    for table in tables:
        table.start()
    for i in range(4):
        fetch(i).start()
    for table in tables:
        table.wait()

    def chunk(i, _):
        fetch(i).wait()
        for half in range(2):
            lanes = slice(half * LANES, (half + 1) * LANES)
            pole = poles(rate_ref, half, 16)
            weight = [scale * q for q in weights(rate_ref, coef_ref, half, 16)]

            def steps(j, states, lanes=lanes, pole=pole, weight=weight):
                for k in range(16):
                    s = j * 16 + k
                    u = block[s, part(i), lanes].astype(F32)
                    states = [p * h + u for p, h in zip(pole, states)]
                    result[s, part(i), lanes] = tree([q * h for q, h in zip(weight, states)])
                return states

            lax.fori_loop(0, 4, steps, [jnp.zeros((16, LANES), F32)] * MODES)
        put(i).start()
        return 0

    lax.fori_loop(0, 4, chunk, 0)
    for i in range(4):
        put(i).wait()


def decays(rate_ref, half_ref, span):
    lanes = pl.ds(pl.multiple_of(half_ref[0] * LANES, LANES), LANES)
    return [jnp.broadcast_to(jnp.exp(-span * rate_ref[m : m + 1, lanes]), (8, LANES)) for m in range(MODES)]


def join_kernel(span, half_ref, left_ref, here_ref, keep_ref, came_ref, rate_ref, first_ref, *out_refs):
    left_here, here = left_ref[0] == 0, here_ref[0]
    decay = decays(rate_ref, half_ref, span)
    part = keep_ref.shape[0] // len(out_refs)
    for b in range(part):
        for k, out_ref in enumerate(out_refs):
            at = b if len(out_refs) == 1 else (here * part if k == 0 else part - here * part) + b
            for m in range(MODES):
                keep, came = keep_ref[at, m], came_ref[at, m]
                first = jnp.where(left_here, keep, came)
                first_ref[at, m] = first
                out_ref[b, m] = decay[m] * first + jnp.where(left_here, came, keep)


def part_kernel(span, half_ref, left_ref, here_ref, *refs):
    *in_refs, first_ref, rate_ref, keep_ref, send_ref = refs
    left_here, here = left_ref[0] == 0, here_ref[0]
    decay = decays(rate_ref, half_ref, span)
    part = first_ref.shape[0] // len(in_refs)
    for b in range(part):
        for k, in_ref in enumerate(in_refs):
            at = b if len(in_refs) == 1 else (here * part if k == 0 else part - here * part) + b
            for m in range(MODES):
                chain = in_ref[b, m]
                if len(in_refs) == 1:
                    chain = jnp.where(here == 1, chain, 0.0)
                after = decay[m] * chain + first_ref[at, m]
                keep_ref[at, m] = jnp.where(left_here, chain, after)
                send_ref[at, m] = jnp.where(left_here, after, chain)


def piece_kernel(part, block_ref, rate_ref, coef_ref, *refs):
    out_ref, block, result, arrived, left = refs[-5:]
    rows = pl.ds(part * 16, 16)

    def fetch(q):
        cols = pl.ds(q * 16, 16)
        return pltpu.make_async_copy(block_ref.at[cols, rows, :], block.at[cols], arrived.at[q])

    def put(half, q):
        cols, lanes = pl.ds(q * 16, 16), pl.ds(half * LANES, LANES)
        return pltpu.make_async_copy(
            result.at[cols, :, lanes], out_ref.at[cols, rows, lanes], left.at[half * 4 + q]
        )

    for q in range(4):
        fetch(q).start()
    for half in range(2):
        lanes = slice(half * LANES, (half + 1) * LANES)
        pole = poles(rate_ref, half, 16)
        weight = weights(rate_ref, coef_ref, half, 16)
        states = [jnp.zeros((16, LANES), F32)] * MODES
        for q in range(4):
            if half == 0:
                fetch(q).wait()
            for s in range(q * 16, q * 16 + 16):
                u = block[s, :, lanes].astype(F32)
                states = [p * h + u for p, h in zip(pole, states)]
                result[s, :, lanes] = tree([q * h for q, h in zip(weight, states)])
            put(half, q).start()
    for half in range(2):
        for q in range(4):
            put(half, q).wait()


def act_kernel(core_ref, local_ref, in_ref, vr_ref, vc_ref, hr_ref, act_ref, mine_ref, other_ref, tails, field):
    for half in range(2):
        lanes = slice(half * LANES, (half + 1) * LANES)
        pole = poles(vr_ref, half, 16)

        @pl.when(pl.program_id(0) == 0)
        def _(half=half, pole=pole):
            weight = weights(vr_ref, vc_ref, half, 16)
            for m in range(MODES):
                factor = (0.5 * pole[m] * weight[m])[None, :8]
                tails[half, :, m] = in_ref[half, :, m] * factor

        def block(b, _, half=half, lanes=lanes, pole=pole):
            pair = pl.ds(b * 2, 2)
            cols = pl.ds(pl.multiple_of(b * 16, 16), 16)
            tail = [tails[half, pair, m].reshape(16, LANES) for m in range(MODES)]
            for s in range(local_ref.shape[0]):
                y = local_ref[s, cols, lanes] + tree(tail)
                tail = [p * g for p, g in zip(pole, tail)]
                a = gelu_of_half(y).astype(BF16).astype(F32)
                field[half, pl.ds(s * PITCH + b * 16, 16), :] = a
            for m in range(MODES):
                tails[half, pair, m] = tail[m].reshape(2, 8, LANES)
            return 0

        lax.fori_loop(0, 4, block, 0)

    for half in range(2):
        lanes = slice(half * LANES, (half + 1) * LANES)
        pole = poles(hr_ref, half, 16)
        mine = core_ref[0] == half
        for r in range(0, local_ref.shape[0], 16):

            def steps(i, states, half=half, lanes=lanes, pole=pole, r=r):
                for k in range(16):
                    w = i * 16 + k
                    u = field[half, pl.ds(w + r * PITCH, 16, stride=PITCH), :]
                    act_ref[w, r : r + 16, lanes] = u.astype(BF16)
                    states = [p * h + u for p, h in zip(pole, states)]
                return states

            states = lax.fori_loop(0, 4, steps, [jnp.zeros((16, LANES), F32)] * MODES)

            @pl.when(mine)
            def _(states=states, r=r):
                for m in range(MODES):
                    mine_ref[r // 8 : r // 8 + 2, m] = states[m].reshape(2, 8, LANES)

            @pl.when(jnp.logical_not(mine))
            def _(states=states, r=r):
                for m in range(MODES):
                    other_ref[r // 8 : r // 8 + 2, m] = states[m].reshape(2, 8, LANES)


def mix_kernel(core_ref, local_ref, keep_ref, got_ref, hr_ref, hc_ref, w_in_ref, w_out_ref, out_ref, horiz, mixed):
    core = core_ref[0]
    rows = local_ref.shape[1]
    for r in range(0, rows, 16):
        pair = pl.ds(pl.program_id(0) * (rows // 8) + r // 8, 2)
        for half in range(2):
            lanes = slice(half * LANES, (half + 1) * LANES)
            pole = poles(hr_ref, half, 16)
            weight = weights(hr_ref, hc_ref, half, 16)
            mine = core == half
            tail = [
                jnp.where(mine, keep_ref[pair, m], got_ref[pair, m]).reshape(16, LANES)
                * (pole[m] * weight[m])
                for m in range(MODES)
            ]

            def steps(i, tail, lanes=lanes, pole=pole, r=r):
                for k in range(8):
                    w = i * 8 + k
                    y = local_ref[w, r : r + 16, lanes] + tree(tail)
                    tail = [p * g for p, g in zip(pole, tail)]
                    horiz[pl.ds(pl.multiple_of(w * 16, 16), 16), lanes] = y
                return tail

            lax.fori_loop(0, 8, steps, tail)

        y = horiz[...]
        scale = lax.rsqrt(jnp.mean(y * y, axis=-1, keepdims=True) + 1e-06)
        normed = (y * scale).astype(BF16)
        hidden = gelu_packed(jnp.dot(normed, w_in_ref[...], preferred_element_type=F32))
        out = y + jnp.dot(hidden, w_out_ref[...], preferred_element_type=F32)
        for w in range(64):
            for half in range(2):
                lanes = slice(half * LANES, (half + 1) * LANES)
                mixed[half, pl.ds(w, 16, stride=PITCH), :] = out[w * 16 : (w + 1) * 16, lanes]
        for half in range(2):
            lanes = slice(half * LANES, (half + 1) * LANES)
            for h in range(16):
                out_ref[r + h, :, lanes] = mixed[half, h * PITCH : h * PITCH + 64].astype(BF16)


def in_hbm(block):
    return pltpu.with_memory_space_constraint(block, pltpu.HBM)


def whole(shape):
    return pl.BlockSpec(shape, lambda i: (0,) * len(shape))


def params(mib):
    return pltpu.CompilerParams(vmem_limit_bytes=mib * 1024 * 1024)


VMEM = pl.BlockSpec(memory_space=pltpu.VMEM)
HBM = pl.BlockSpec(memory_space=pltpu.HBM)
SMEM = pl.BlockSpec(memory_space=pltpu.SMEM)


def row_edges(image, rate):
    return pl.pallas_call(
        edge_kernel,
        in_specs=[HBM, HBM],
        out_specs=VMEM,
        out_shape=jax.ShapeDtypeStruct((2, 8, 8, 8, LANES), F32),
        scratch_shapes=[
            pltpu.VMEM((64, 64, 256), BF16),
            pltpu.VMEM((8, 256), F32),
            pltpu.SemaphoreType.DMA((5,)),
        ],
        compiler_params=params(24),
        name="row_edges",
    )(in_hbm(image), in_hbm(rate))


def prefix(half, edges, rate, span):
    return pl.pallas_call(
        functools.partial(prefix_kernel, span),
        in_specs=[SMEM, VMEM, VMEM],
        out_specs=VMEM,
        out_shape=jax.ShapeDtypeStruct(edges.shape, F32),
        compiler_params=params(8),
        name="prefix",
    )(half, edges, rate)


def local_scan(block, rate, coef, name, scale):
    return pl.pallas_call(
        functools.partial(local_kernel, scale),
        in_specs=[HBM, HBM, HBM],
        out_specs=HBM,
        out_shape=pltpu.HBM((64, 64, 256), F32),
        scratch_shapes=[
            pltpu.VMEM((64, 64, 256), BF16),
            pltpu.VMEM((64, 64, 256), F32),
            pltpu.VMEM((8, 256), F32),
            pltpu.VMEM((8, 256), F32),
            pltpu.SemaphoreType.DMA((6,)),
            pltpu.SemaphoreType.DMA((4,)),
        ],
        compiler_params=params(24),
        cost_estimate=pl.CostEstimate(flops=5_000_000_000, bytes_accessed=8_000_000, transcendentals=0),
        name=name,
    )(in_hbm(block), in_hbm(rate), in_hbm(coef))


def local_piece(block, rate, coef, part, into):
    more = [] if into is None else [in_hbm(into)]
    return pl.pallas_call(
        functools.partial(piece_kernel, part),
        in_specs=[HBM, VMEM, VMEM] + [HBM] * len(more),
        out_specs=HBM,
        out_shape=pltpu.HBM((64, 64, 256), F32),
        input_output_aliases={3: 0} if more else {},
        scratch_shapes=[
            pltpu.VMEM((64, 16, 256), BF16),
            pltpu.VMEM((64, 16, 256), F32),
            pltpu.SemaphoreType.DMA((4,)),
            pltpu.SemaphoreType.DMA((8,)),
        ],
        compiler_params=params(8),
        cost_estimate=pl.CostEstimate(flops=1_250_000_000, bytes_accessed=2_000_000, transcendentals=0),
        name=f"horiz_local_{part}",
    )(in_hbm(block), rate, coef, *more)


def small(kernel, name, outs, *operands):
    return pl.pallas_call(
        kernel,
        in_specs=[SMEM] * 3 + [VMEM] * (len(operands) - 3),
        out_specs=[VMEM] * len(outs),
        out_shape=[jax.ShapeDtypeStruct(shape, F32) for shape in outs],
        compiler_params=params(8),
        name=name,
    )(*operands)


def act_and_edges(core, local, incoming, vert_rate, vert_coef, horiz_rate):
    edge = pl.BlockSpec((ACT_ROWS // 8, 8, 8, LANES), lambda i: (i, 0, 0, 0))
    return pl.pallas_call(
        act_kernel,
        grid=(64 // ACT_ROWS,),
        in_specs=[SMEM, pl.BlockSpec((ACT_ROWS, 64, 256), lambda i: (i, 0, 0)), VMEM, VMEM, VMEM, VMEM],
        out_specs=[pl.BlockSpec((64, ACT_ROWS, 256), lambda i: (0, i, 0)), edge, edge],
        out_shape=[pltpu.HBM((64, 64, 256), BF16)] + [jax.ShapeDtypeStruct((8, 8, 8, LANES), F32)] * 2,
        scratch_shapes=[
            pltpu.VMEM((2, 8, 8, 8, LANES), F32),
            pltpu.VMEM((2, ACT_ROWS * PITCH, LANES), F32),
        ],
        compiler_params=params(24),
        name="act_and_edges",
    )(core, in_hbm(local), incoming, vert_rate, vert_coef, horiz_rate)


def mix(core, local, keep, got, horiz_rate, horiz_coef, w_in, w_out):
    return pl.pallas_call(
        mix_kernel,
        grid=(64 // MIX_ROWS,),
        in_specs=[SMEM, pl.BlockSpec((64, MIX_ROWS, 256), lambda i: (0, i, 0))] + [VMEM] * 6,
        out_specs=pl.BlockSpec((MIX_ROWS, 64, 256), lambda i: (i, 0, 0)),
        out_shape=jax.ShapeDtypeStruct((64, 64, 256), BF16),
        scratch_shapes=[pltpu.VMEM((1024, 256), F32), pltpu.VMEM((2, 16 * PITCH, LANES), F32)],
        compiler_params=params(40),
        name="mix",
    )(core, in_hbm(local), keep, got, horiz_rate, horiz_coef, w_in, w_out)


def swap(block, bits):
    n = lax.axis_size("col")
    return lax.ppermute(block, "col", [(i, i ^ bits) for i in range(n)])


def together(arrived, local):
    return lax.optimization_barrier((arrived, local))


def on_device(image, vert_rate, vert_coef, horiz_rate, horiz_coef, w_in, w_out):
    rows, cols = lax.axis_size("row"), lax.axis_size("col")
    piece_half = (lax.axis_index("row") // (rows // 2)).reshape(1)
    col = lax.axis_index("col").reshape(1)
    core, chip = col % 2, col // 2
    side = [core, chip % 2, chip // 2 % 2]
    upper = chip // 4
    here = [side[1] ^ upper, side[2] ^ upper, upper]

    edges = row_edges(image, vert_rate).reshape(rows, 8, 8, LANES)
    edges = lax.all_to_all(edges, "row", 0, 0, tiled=True)
    local = local_scan(image, vert_rate, vert_coef, "vert_local", 0.5)
    edges, local, side, here = lax.optimization_barrier((edges, local, side, here))
    core = side[0]
    incoming = prefix(piece_half, edges, vert_rate, 64.0)
    incoming = lax.all_to_all(incoming, "row", 0, 0, tiled=True).reshape(2, 8, 8, 8, LANES)

    act, mine, other = act_and_edges(core, local, incoming, vert_rate, vert_coef, horiz_rate)

    eight, four, two = (8, 8, 8, LANES), (4, 8, 8, LANES), (2, 8, 8, LANES)

    def horiz(part, into):
        return local_piece(act, horiz_rate, horiz_coef, part, into)

    def join(level, outs, keep, came):
        kernel = functools.partial(join_kernel, 64.0 * 2**level)
        return small(kernel, f"join_{level}", outs, core, side[level], here[level], keep, came, horiz_rate)

    def part(level, shape, chains, first):
        kernel = functools.partial(part_kernel, 64.0 * 2**level)
        return small(kernel, f"part_{level}", [shape] * 2, core, side[level], here[level], *chains, first, horiz_rate)

    first_tile, keep, send = join(0, [eight, four, four], mine, swap(other, 1))
    came, local = together(swap(send, 2), horiz(0, None))
    first_chip, keep, send = join(1, [four, two, two], keep, came)
    came, local = together(swap(send, 4), horiz(1, local))
    first_pair, group = join(2, [two, two], keep, came)
    chain, local = together(swap(group, cols - 2), horiz(2, local))
    keep, send = part(2, two, [chain], first_pair)
    came, local = together(swap(send, 4), horiz(3, local))
    keep, send = part(1, four, [keep, came], first_chip)
    keep, send = part(0, eight, [keep, swap(send, 2)], first_tile)
    got = swap(send, 1)

    return mix(core, local, keep, got, horiz_rate, horiz_coef, w_in, w_out)


def solution(mesh):
    placed = (P("row", "col", None), P(), P(), P(), P(), P(), P())
    return jax.shard_map(
        on_device, mesh=mesh, in_specs=placed, out_specs=P("row", "col", None), check_vma=False
    )
```

```python
import functools
import math

import jax
import jax.numpy as jnp
from jax import lax
from jax.experimental import pallas as pl
from jax.experimental.pallas import tpu as pltpu
from jax.sharding import PartitionSpec as P

F32 = jnp.float32
BF16 = jnp.bfloat16
LANES = 128
MODES = 8
SQRT_2_PI = math.sqrt(2.0 / math.pi)
PITCH = 73
ACT_ROWS = 16
MIX_ROWS = 16


def gelu_of_half(x):
    inner = x * (2.0 * SQRT_2_PI + (8.0 * SQRT_2_PI * 0.044715) * (x * x))
    return x + x * jnp.tanh(inner)


def gelu_packed(x):
    x = x.astype(BF16)
    inner = x * (BF16(SQRT_2_PI) + BF16(SQRT_2_PI * 0.044715) * (x * x))
    half = BF16(0.5) * x
    return half + half * jnp.tanh(inner)


def poles(rate_ref, half, rows):
    lanes = slice(half * LANES, (half + 1) * LANES)
    return [
        jnp.broadcast_to(jnp.exp(-rate_ref[m : m + 1, lanes]), (rows, LANES)) for m in range(MODES)
    ]


def weights(rate_ref, coef_ref, half, rows):
    lanes = slice(half * LANES, (half + 1) * LANES)
    return [
        jnp.broadcast_to(
            coef_ref[m : m + 1, lanes] * jnp.sqrt(1.0 - jnp.exp(-2.0 * rate_ref[m : m + 1, lanes])),
            (rows, LANES),
        )
        for m in range(MODES)
    ]


def tree(terms):
    while len(terms) > 1:
        terms = [a + b for a, b in zip(terms[::2], terms[1::2])]
    return terms[0]


def edge_kernel(image_ref, rate_hbm_ref, edge_ref, image, rate_ref, arrived):
    def fetch(i):
        cols = pl.ds(pl.multiple_of(i * 16, 16), 16)
        return pltpu.make_async_copy(image_ref.at[:, cols, :], image.at[:, cols, :], arrived.at[i])

    rates = pltpu.make_async_copy(rate_hbm_ref, rate_ref, arrived.at[4])
    rates.start()
    for i in range(4):
        fetch(i).start()
    rates.wait()

    def chunk(i, _):
        fetch(i).wait()
        cols = pl.ds(pl.multiple_of(i * 16, 16), 16)
        for half in range(2):
            lanes = slice(half * LANES, (half + 1) * LANES)
            pole = poles(rate_ref, half, 16)

            def steps(j, states, lanes=lanes, pole=pole):
                for k in range(16):
                    u = image[j * 16 + k, cols, lanes].astype(F32)
                    states = [p * h + u for p, h in zip(pole, states)]
                return states

            states = lax.fori_loop(0, 4, steps, [jnp.zeros((16, LANES), F32)] * MODES)
            for m in range(MODES):
                edge_ref[half, pl.ds(i * 2, 2), m] = states[m].reshape(2, 8, LANES)
        return 0

    lax.fori_loop(0, 4, chunk, 0)


def prefix_kernel(span, half_ref, edge_ref, rate_ref, out_ref):
    decay = decays(rate_ref, half_ref, span)
    states = [jnp.zeros((8, LANES), F32)] * MODES
    for r in range(edge_ref.shape[0]):
        for m in range(MODES):
            out_ref[r, m] = states[m]
            states[m] = decay[m] * states[m] + edge_ref[r, m]


def local_kernel(scale, block_ref, rate_hbm_ref, coef_hbm_ref, out_ref, block, result, rate_ref, coef_ref, arrived, left):
    def part(i):
        return pl.ds(pl.multiple_of(i * 16, 16), 16)

    def fetch(i):
        return pltpu.make_async_copy(block_ref.at[:, part(i), :], block.at[:, part(i), :], arrived.at[i])

    def put(i):
        return pltpu.make_async_copy(result.at[:, part(i), :], out_ref.at[:, part(i), :], left.at[i])

    tables = [
        pltpu.make_async_copy(rate_hbm_ref, rate_ref, arrived.at[4]),
        pltpu.make_async_copy(coef_hbm_ref, coef_ref, arrived.at[5]),
    ]
    for table in tables:
        table.start()
    for i in range(4):
        fetch(i).start()
    for table in tables:
        table.wait()

    def chunk(i, _):
        fetch(i).wait()
        for half in range(2):
            lanes = slice(half * LANES, (half + 1) * LANES)
            pole = poles(rate_ref, half, 16)
            weight = [scale * q for q in weights(rate_ref, coef_ref, half, 16)]

            def steps(j, states, lanes=lanes, pole=pole, weight=weight):
                for k in range(16):
                    s = j * 16 + k
                    u = block[s, part(i), lanes].astype(F32)
                    states = [p * h + u for p, h in zip(pole, states)]
                    result[s, part(i), lanes] = tree([q * h for q, h in zip(weight, states)])
                return states

            lax.fori_loop(0, 4, steps, [jnp.zeros((16, LANES), F32)] * MODES)
        put(i).start()
        return 0

    lax.fori_loop(0, 4, chunk, 0)
    for i in range(4):
        put(i).wait()


def decays(rate_ref, half_ref, span):
    lanes = pl.ds(pl.multiple_of(half_ref[0] * LANES, LANES), LANES)
    return [jnp.broadcast_to(jnp.exp(-span * rate_ref[m : m + 1, lanes]), (8, LANES)) for m in range(MODES)]


def join_kernel(span, half_ref, left_ref, here_ref, keep_ref, came_ref, rate_ref, first_ref, *out_refs):
    left_here, here = left_ref[0] == 0, here_ref[0]
    decay = decays(rate_ref, half_ref, span)
    part = keep_ref.shape[0] // len(out_refs)
    for b in range(part):
        for k, out_ref in enumerate(out_refs):
            at = b if len(out_refs) == 1 else (here * part if k == 0 else part - here * part) + b
            for m in range(MODES):
                keep, came = keep_ref[at, m], came_ref[at, m]
                first = jnp.where(left_here, keep, came)
                first_ref[at, m] = first
                out_ref[b, m] = decay[m] * first + jnp.where(left_here, came, keep)


def part_kernel(span, half_ref, left_ref, here_ref, *refs):
    *in_refs, first_ref, rate_ref, keep_ref, send_ref = refs
    left_here, here = left_ref[0] == 0, here_ref[0]
    decay = decays(rate_ref, half_ref, span)
    part = first_ref.shape[0] // len(in_refs)
    for b in range(part):
        for k, in_ref in enumerate(in_refs):
            at = b if len(in_refs) == 1 else (here * part if k == 0 else part - here * part) + b
            for m in range(MODES):
                chain = in_ref[b, m]
                if len(in_refs) == 1:
                    chain = jnp.where(here == 1, chain, 0.0)
                after = decay[m] * chain + first_ref[at, m]
                keep_ref[at, m] = jnp.where(left_here, chain, after)
                send_ref[at, m] = jnp.where(left_here, after, chain)


def piece_kernel(part, block_ref, rate_ref, coef_ref, *refs):
    out_ref, block, result, arrived, left = refs[-5:]
    rows = pl.ds(part * 16, 16)

    def fetch(q):
        cols = pl.ds(q * 16, 16)
        return pltpu.make_async_copy(block_ref.at[cols, rows, :], block.at[cols], arrived.at[q])

    def put(half, q):
        cols, lanes = pl.ds(q * 16, 16), pl.ds(half * LANES, LANES)
        return pltpu.make_async_copy(
            result.at[cols, :, lanes], out_ref.at[cols, rows, lanes], left.at[half * 4 + q]
        )

    for q in range(4):
        fetch(q).start()
    for half in range(2):
        lanes = slice(half * LANES, (half + 1) * LANES)
        pole = poles(rate_ref, half, 16)
        weight = weights(rate_ref, coef_ref, half, 16)
        states = [jnp.zeros((16, LANES), F32)] * MODES
        for q in range(4):
            if half == 0:
                fetch(q).wait()
            for s in range(q * 16, q * 16 + 16):
                u = block[s, :, lanes].astype(F32)
                states = [p * h + u for p, h in zip(pole, states)]
                result[s, :, lanes] = tree([q * h for q, h in zip(weight, states)])
            put(half, q).start()
    for half in range(2):
        for q in range(4):
            put(half, q).wait()


def act_kernel(core_ref, local_ref, in_ref, vr_ref, vc_ref, hr_ref, act_ref, mine_ref, other_ref, tails, field):
    for half in range(2):
        lanes = slice(half * LANES, (half + 1) * LANES)
        pole = poles(vr_ref, half, 16)

        @pl.when(pl.program_id(0) == 0)
        def _(half=half, pole=pole):
            weight = weights(vr_ref, vc_ref, half, 16)
            for m in range(MODES):
                factor = (0.5 * pole[m] * weight[m])[None, :8]
                tails[half, :, m] = in_ref[half, :, m] * factor

        def block(b, _, half=half, lanes=lanes, pole=pole):
            pair = pl.ds(b * 2, 2)
            cols = pl.ds(pl.multiple_of(b * 16, 16), 16)
            tail = [tails[half, pair, m].reshape(16, LANES) for m in range(MODES)]
            for s in range(local_ref.shape[0]):
                y = local_ref[s, cols, lanes] + tree(tail)
                tail = [p * g for p, g in zip(pole, tail)]
                a = gelu_of_half(y).astype(BF16).astype(F32)
                field[half, pl.ds(s * PITCH + b * 16, 16), :] = a
            for m in range(MODES):
                tails[half, pair, m] = tail[m].reshape(2, 8, LANES)
            return 0

        lax.fori_loop(0, 4, block, 0)

    for half in range(2):
        lanes = slice(half * LANES, (half + 1) * LANES)
        pole = poles(hr_ref, half, 16)
        mine = core_ref[0] == half
        for r in range(0, local_ref.shape[0], 16):

            def steps(i, states, half=half, lanes=lanes, pole=pole, r=r):
                for k in range(16):
                    w = i * 16 + k
                    u = field[half, pl.ds(w + r * PITCH, 16, stride=PITCH), :]
                    act_ref[w, r : r + 16, lanes] = u.astype(BF16)
                    states = [p * h + u for p, h in zip(pole, states)]
                return states

            states = lax.fori_loop(0, 4, steps, [jnp.zeros((16, LANES), F32)] * MODES)

            @pl.when(mine)
            def _(states=states, r=r):
                for m in range(MODES):
                    mine_ref[r // 8 : r // 8 + 2, m] = states[m].reshape(2, 8, LANES)

            @pl.when(jnp.logical_not(mine))
            def _(states=states, r=r):
                for m in range(MODES):
                    other_ref[r // 8 : r // 8 + 2, m] = states[m].reshape(2, 8, LANES)


def mix_kernel(core_ref, local_ref, keep_ref, got_ref, hr_ref, hc_ref, w_in_ref, w_out_ref, out_ref, horiz, mixed):
    core = core_ref[0]
    rows = local_ref.shape[1]
    for r in range(0, rows, 16):
        pair = pl.ds(pl.program_id(0) * (rows // 8) + r // 8, 2)
        for half in range(2):
            lanes = slice(half * LANES, (half + 1) * LANES)
            pole = poles(hr_ref, half, 16)
            weight = weights(hr_ref, hc_ref, half, 16)
            mine = core == half
            tail = [
                jnp.where(mine, keep_ref[pair, m], got_ref[pair, m]).reshape(16, LANES)
                * (pole[m] * weight[m])
                for m in range(MODES)
            ]

            def steps(i, tail, lanes=lanes, pole=pole, r=r):
                for k in range(8):
                    w = i * 8 + k
                    y = local_ref[w, r : r + 16, lanes] + tree(tail)
                    tail = [p * g for p, g in zip(pole, tail)]
                    horiz[pl.ds(pl.multiple_of(w * 16, 16), 16), lanes] = y
                return tail

            lax.fori_loop(0, 8, steps, tail)

        y = horiz[...]
        scale = lax.rsqrt(jnp.mean(y * y, axis=-1, keepdims=True) + 1e-06)
        normed = (y * scale).astype(BF16)
        hidden = gelu_packed(jnp.dot(normed, w_in_ref[...], preferred_element_type=F32))
        out = y + jnp.dot(hidden, w_out_ref[...], preferred_element_type=F32)
        for w in range(64):
            for half in range(2):
                lanes = slice(half * LANES, (half + 1) * LANES)
                mixed[half, pl.ds(w, 16, stride=PITCH), :] = out[w * 16 : (w + 1) * 16, lanes]
        for half in range(2):
            lanes = slice(half * LANES, (half + 1) * LANES)
            for h in range(16):
                out_ref[r + h, :, lanes] = mixed[half, h * PITCH : h * PITCH + 64].astype(BF16)


def in_hbm(block):
    return pltpu.with_memory_space_constraint(block, pltpu.HBM)


def whole(shape):
    return pl.BlockSpec(shape, lambda i: (0,) * len(shape))


def params(mib):
    return pltpu.CompilerParams(vmem_limit_bytes=mib * 1024 * 1024)


VMEM = pl.BlockSpec(memory_space=pltpu.VMEM)
HBM = pl.BlockSpec(memory_space=pltpu.HBM)
SMEM = pl.BlockSpec(memory_space=pltpu.SMEM)


def row_edges(image, rate):
    return pl.pallas_call(
        edge_kernel,
        in_specs=[HBM, HBM],
        out_specs=VMEM,
        out_shape=jax.ShapeDtypeStruct((2, 8, 8, 8, LANES), F32),
        scratch_shapes=[
            pltpu.VMEM((64, 64, 256), BF16),
            pltpu.VMEM((8, 256), F32),
            pltpu.SemaphoreType.DMA((5,)),
        ],
        compiler_params=params(24),
        name="row_edges",
    )(in_hbm(image), in_hbm(rate))


def prefix(half, edges, rate, span):
    return pl.pallas_call(
        functools.partial(prefix_kernel, span),
        in_specs=[SMEM, VMEM, VMEM],
        out_specs=VMEM,
        out_shape=jax.ShapeDtypeStruct(edges.shape, F32),
        compiler_params=params(8),
        name="prefix",
    )(half, edges, rate)


def local_scan(block, rate, coef, name, scale):
    return pl.pallas_call(
        functools.partial(local_kernel, scale),
        in_specs=[HBM, HBM, HBM],
        out_specs=HBM,
        out_shape=pltpu.HBM((64, 64, 256), F32),
        scratch_shapes=[
            pltpu.VMEM((64, 64, 256), BF16),
            pltpu.VMEM((64, 64, 256), F32),
            pltpu.VMEM((8, 256), F32),
            pltpu.VMEM((8, 256), F32),
            pltpu.SemaphoreType.DMA((6,)),
            pltpu.SemaphoreType.DMA((4,)),
        ],
        compiler_params=params(24),
        cost_estimate=pl.CostEstimate(flops=5_000_000_000, bytes_accessed=8_000_000, transcendentals=0),
        name=name,
    )(in_hbm(block), in_hbm(rate), in_hbm(coef))


def local_piece(block, rate, coef, part, into):
    more = [] if into is None else [in_hbm(into)]
    return pl.pallas_call(
        functools.partial(piece_kernel, part),
        in_specs=[HBM, VMEM, VMEM] + [HBM] * len(more),
        out_specs=HBM,
        out_shape=pltpu.HBM((64, 64, 256), F32),
        input_output_aliases={3: 0} if more else {},
        scratch_shapes=[
            pltpu.VMEM((64, 16, 256), BF16),
            pltpu.VMEM((64, 16, 256), F32),
            pltpu.SemaphoreType.DMA((4,)),
            pltpu.SemaphoreType.DMA((8,)),
        ],
        compiler_params=params(8),
        cost_estimate=pl.CostEstimate(flops=1_250_000_000, bytes_accessed=2_000_000, transcendentals=0),
        name=f"horiz_local_{part}",
    )(in_hbm(block), rate, coef, *more)


def small(kernel, name, outs, *operands):
    return pl.pallas_call(
        kernel,
        in_specs=[SMEM] * 3 + [VMEM] * (len(operands) - 3),
        out_specs=[VMEM] * len(outs),
        out_shape=[jax.ShapeDtypeStruct(shape, F32) for shape in outs],
        compiler_params=params(8),
        name=name,
    )(*operands)


def act_and_edges(core, local, incoming, vert_rate, vert_coef, horiz_rate):
    edge = pl.BlockSpec((ACT_ROWS // 8, 8, 8, LANES), lambda i: (i, 0, 0, 0))
    return pl.pallas_call(
        act_kernel,
        grid=(64 // ACT_ROWS,),
        in_specs=[SMEM, pl.BlockSpec((ACT_ROWS, 64, 256), lambda i: (i, 0, 0)), VMEM, VMEM, VMEM, VMEM],
        out_specs=[pl.BlockSpec((64, ACT_ROWS, 256), lambda i: (0, i, 0)), edge, edge],
        out_shape=[pltpu.HBM((64, 64, 256), BF16)] + [jax.ShapeDtypeStruct((8, 8, 8, LANES), F32)] * 2,
        scratch_shapes=[
            pltpu.VMEM((2, 8, 8, 8, LANES), F32),
            pltpu.VMEM((2, (ACT_ROWS + 1) * PITCH, LANES), F32),
        ],
        compiler_params=params(24),
        name="act_and_edges",
    )(core, in_hbm(local), incoming, vert_rate, vert_coef, horiz_rate)


def mix(core, local, keep, got, horiz_rate, horiz_coef, w_in, w_out):
    return pl.pallas_call(
        mix_kernel,
        grid=(64 // MIX_ROWS,),
        in_specs=[SMEM, pl.BlockSpec((64, MIX_ROWS, 256), lambda i: (0, i, 0))] + [VMEM] * 6,
        out_specs=pl.BlockSpec((MIX_ROWS, 64, 256), lambda i: (i, 0, 0)),
        out_shape=jax.ShapeDtypeStruct((64, 64, 256), BF16),
        scratch_shapes=[pltpu.VMEM((1024, 256), F32), pltpu.VMEM((2, 17 * PITCH, LANES), F32)],
        compiler_params=params(40),
        name="mix",
    )(core, in_hbm(local), keep, got, horiz_rate, horiz_coef, w_in, w_out)


def swap(block, bits):
    n = lax.axis_size("col")
    return lax.ppermute(block, "col", [(i, i ^ bits) for i in range(n)])


def together(arrived, local):
    return lax.optimization_barrier((arrived, local))


def on_device(image, vert_rate, vert_coef, horiz_rate, horiz_coef, w_in, w_out):
    rows, cols = lax.axis_size("row"), lax.axis_size("col")
    piece_half = (lax.axis_index("row") // (rows // 2)).reshape(1)
    col = lax.axis_index("col").reshape(1)
    core, chip = col % 2, col // 2
    side = [core, chip % 2, chip // 2 % 2]
    upper = chip // 4
    here = [side[1] ^ upper, side[2] ^ upper, upper]

    edges = row_edges(image, vert_rate).reshape(rows, 8, 8, LANES)
    edges = lax.all_to_all(edges, "row", 0, 0, tiled=True)
    local = local_scan(image, vert_rate, vert_coef, "vert_local", 0.5)
    edges, local, side, here = lax.optimization_barrier((edges, local, side, here))
    core = side[0]
    incoming = prefix(piece_half, edges, vert_rate, 64.0)
    incoming = lax.all_to_all(incoming, "row", 0, 0, tiled=True).reshape(2, 8, 8, 8, LANES)

    act, mine, other = act_and_edges(core, local, incoming, vert_rate, vert_coef, horiz_rate)

    eight, four, two = (8, 8, 8, LANES), (4, 8, 8, LANES), (2, 8, 8, LANES)

    def horiz(part, into):
        return local_piece(act, horiz_rate, horiz_coef, part, into)

    def join(level, outs, keep, came):
        kernel = functools.partial(join_kernel, 64.0 * 2**level)
        return small(kernel, f"join_{level}", outs, core, side[level], here[level], keep, came, horiz_rate)

    def part(level, shape, chains, first):
        kernel = functools.partial(part_kernel, 64.0 * 2**level)
        return small(kernel, f"part_{level}", [shape] * 2, core, side[level], here[level], *chains, first, horiz_rate)

    first_tile, keep, send = join(0, [eight, four, four], mine, swap(other, 1))
    came, local = together(swap(send, 2), horiz(0, None))
    first_chip, keep, send = join(1, [four, two, two], keep, came)
    came, local = together(swap(send, 4), horiz(1, local))
    first_pair, group = join(2, [two, two], keep, came)
    chain, local = together(swap(group, cols - 2), horiz(2, local))
    keep, send = part(2, two, [chain], first_pair)
    came, local = together(swap(send, 4), horiz(3, local))
    keep, send = part(1, four, [keep, came], first_chip)
    keep, send = part(0, eight, [keep, swap(send, 2)], first_tile)
    got = swap(send, 1)

    return mix(core, local, keep, got, horiz_rate, horiz_coef, w_in, w_out)


def solution(mesh):
    placed = (P("row", "col", None), P(), P(), P(), P(), P(), P())
    return jax.shard_map(
        on_device, mesh=mesh, in_specs=placed, out_specs=P("row", "col", None), check_vma=False
    )
```
